32 devices in a mesh: seq: 8 (over z, y), ctx: 4 (over x, core).
Axes of the slice: x: 2, y: 2, z: 4, core: 2. Of those that a mesh axis runs over, the one named last changes fastest.
Arguments:
- tokens: bfloat16 [16, 1024, 1536], P('seq', 'ctx'), may hold values from -6 to 6
- norm_gain: bfloat16 [1536], P(('seq', 'ctx')), may hold values from 0.5 to 1.5
- input_weight: bfloat16 [1536, 6448], P(('seq', 'ctx')), may hold values from -0.15625 to 0.15625
- conv_w: bfloat16 [4, 3328], P(None, ('seq', 'ctx')), may hold values from -3 to 3
- conv_b: bfloat16 [3328], P(('seq', 'ctx')), may hold values from -3 to 3
- dt_bias: float32 [48], replicated, may hold values from -5.5 to -2.5
- a_log: float32 [48], replicated, may hold values from -5.5 to 0
- d_skip: float32 [48], replicated, may hold values from 0.5 to 1.5
- gate_gain: bfloat16 [3072], P(('seq', 'ctx')), may hold values from 0.5 to 1.5
- output_weight: bfloat16 [3072, 1536], P(('seq', 'ctx')), may hold values from -0.109375 to 0.109375
- segments: int32 [16, 1024], P('seq', 'ctx'), may hold values from 0 to 17, as said below
- cotangent: bfloat16 [16, 1024, 1536], P('seq', 'ctx'), may hold values from -6 to 6
Outputs:
- output: bfloat16 [16, 1024, 1536], P('seq', 'ctx')
- input_grad: bfloat16 [16, 1024, 1536], P('seq', 'ctx')
- grad_norm_gain: float32 [1536], P(('seq', 'ctx'))
- grad_w_in: float32 [1536, 6448], P(('seq', 'ctx'))
- grad_conv_w: float32 [4, 3328], P(None, ('seq', 'ctx'))
- grad_conv_b: float32 [3328], P(('seq', 'ctx'))
- grad_dt_bias: float32 [48], replicated
- grad_a_log: float32 [48], replicated
- grad_d_skip: float32 [48], replicated
- grad_gate_gain: float32 [3072], P(('seq', 'ctx'))
- out_weight_gradient: float32 [3072, 1536], P(('seq', 'ctx'))
The draws below stay inside these ranges and needn't reach their ends.
Inputs may be any that keep to these rules, and one draw needn't show every extreme that they name: `segments`: document numbers start at 0 in every sequence, never fall along it, and rise by one at each document's first token; documents hold 60 tokens or more except a sequence's last one. In each aligned group of 2 sequences one sequence, drawn from the seed, has a first document that starts at its first token and ends within its last 256 tokens. The largest document number is reached in every draw.
All inputs are finite; a program needn't handle non-finite values.
Results may differ from the reference program's by a relative error of at most 0.0087.
Values may be sent and summed in bfloat16 or wider, within the bound.
A program may use at most 320 MiB of HBM per device.

```python
import math
import jax
import jax.numpy as jnp
from jax import lax

D = 1536
HEADS = 48
STATE = 128
HEADDIM = 64
CONV = 4
BLOCK = 256
SEQ_DEV = 2
D_INNER = 3072
CHANNELS = 3328
PROJ = 6448
SEQS = 16
LENGTH = 1024


def draw_segments(key, part):
    key = jax.random.fold_in(key, 7)
    doc_slots = LENGTH // 60 + 2
    lengths = jax.random.randint(jax.random.fold_in(key, 1), (SEQS, doc_slots), 60, 801)
    starts = jnp.cumsum(lengths, axis=1)
    positions = jnp.arange(LENGTH)
    drawn = jnp.sum((starts[:, None, :] <= positions[None, :, None]).astype(jnp.int32), axis=2)
    tail_len = jax.random.randint(jax.random.fold_in(key, 2), (SEQS,), min(60, BLOCK // 2), min(201, BLOCK))
    single = (positions[None, :] >= LENGTH - tail_len[:, None]).astype(jnp.int32)
    chosen = jax.random.randint(jax.random.fold_in(key, 3), (SEQS // SEQ_DEV,), 0, SEQ_DEV)
    row_index = jnp.arange(SEQS)
    chosen_row = row_index % SEQ_DEV == jnp.repeat(chosen, SEQ_DEV)
    shortest = jnp.broadcast_to((positions // 60)[None, :], (SEQS, LENGTH)).astype(jnp.int32)
    short_row = row_index == (chosen[0] + 1) % SEQ_DEV
    result = jnp.where(short_row[:, None], shortest, drawn)
    return jnp.where(chosen_row[:, None], single, result).astype(jnp.int32)


def spiked(entries, own_key, source, target, shards_of, factor):
    owner, partner = [(jnp.arange(entries.shape[dim]) // (entries.shape[dim] // shards_of)).reshape([-1 if axis == dim else 1 for axis in range(entries.ndim)]) for dim in (source, target)]
    chosen = jax.random.permutation(own_key, shards_of)[partner]
    strong = (owner == chosen) | (owner == (partner + shards_of // 2) % shards_of)
    return jnp.where(strong, factor * entries, entries)


def block_levels(own_key, shape, cuts, smallest, high):
    gain = 1.0
    for axis_at, shards_of in cuts:
        draws = jax.random.uniform(jax.random.fold_in(jax.random.fold_in(own_key, 6), axis_at), (shards_of,), jnp.float32, smallest / len(cuts), high / len(cuts))
        gain = gain * jnp.repeat(jnp.exp(draws), shape[axis_at] // shards_of).reshape((-1,) + (1,) * (len(shape) - 1 - axis_at))
    return gain


def noise(own_key, extent, width, bound, shards=(), dtype=jnp.bfloat16):
    gain = block_levels(own_key, extent, shards, -0.22, 0.18) if shards else 1.0
    entries = jax.random.normal(own_key, extent, jnp.float32) * width * gain
    return jnp.minimum(jnp.maximum(entries, -bound), bound).astype(dtype)


def gaussian_with(key, dims, scale, bound, split, heavy, dtype=jnp.bfloat16):
    values = scale * jax.random.normal(key, dims, jnp.float32)
    if split:
        values = values * block_levels(key, dims, split, -0.22, 0.18)
    return jnp.clip(spiked(values, jax.random.fold_in(key, 3), *heavy), -bound, bound).astype(dtype)


def setup_inputs(seed: int = 0) -> dict:
    keys = jax.random.split(jax.random.key(seed), 13)
    return {
        "tokens": gaussian_with(keys[0], (SEQS, LENGTH, D), 1.0, 6.0, ((0, 8), (1, 4)), (0, 2, 8, 2.0)),
        "norm_gain": jnp.clip(1.0 + 0.1 * jax.random.normal(keys[1], (D,), jnp.float32), 0.5, 1.5).astype(jnp.bfloat16),
        "input_weight": noise(keys[2], (D, PROJ), D ** -0.5, 0.15625, ((0, 32),)),
        "conv_w": noise(keys[3], (CONV, CHANNELS), CONV ** -0.5, 3.0, ((1, 32),)),
        "conv_b": noise(keys[4], (CHANNELS,), 0.5, 3.0, ((0, 32),)),
        "dt_bias": jnp.clip(jax.random.uniform(keys[5], (HEADS,), jnp.float32, -5.5, -2.5), -5.5, -2.5),
        "a_log": jnp.clip(jax.random.uniform(keys[6], (HEADS,), jnp.float32, -5.5, 0.0), -5.5, 0.0),
        "d_skip": jnp.clip(jax.random.uniform(keys[7], (HEADS,), jnp.float32, 0.5, 1.5), 0.5, 1.5),
        "gate_gain": jnp.clip(1.0 + 0.1 * jax.random.normal(keys[8], (D_INNER,), jnp.float32), 0.5, 1.5).astype(jnp.bfloat16),
        "output_weight": noise(keys[9], (D_INNER, D), D_INNER ** -0.5, 0.109375, ((0, 32),)),
        "segments": draw_segments(jax.random.fold_in(keys[12], 71), 0),
        "cotangent": noise(keys[11], (SEQS, LENGTH, D), 1.0, 6.0, ((0, 8), (1, 4))),
    }


EPSILON = 1e-05
PRECISION_MAX = lax.Precision.HIGHEST

@jax.custom_vjp
def reduced_value(v):
    return lax.optimization_barrier(v.astype(jnp.bfloat16)).astype(jnp.float32)

@jax.custom_vjp
def reduced_backward(v):
    return v

def low_keep(v):
    return (reduced_value(v), None)

def low_pass(kept, grad):
    return (grad,)

def back_keep(v):
    return (v, None)

def back_low(kept, grad):
    return (reduced_value(grad),)
reduced_value.defvjp(low_keep, low_pass)
reduced_backward.defvjp(back_keep, back_low)

def rms_scale(source, gain_vec):
    return source * lax.rsqrt(lax.optimization_barrier(jnp.mean(source * source, axis=-1, keepdims=True)) + EPSILON) * gain_vec

def ssd_block(carry, pieces):
    state_now, prev_ids = carry
    values, keys_b, queries_c, step_sizes, rates, ids_blk = pieces
    length = ids_blk.shape[1]
    log_decay = jnp.cumsum(rates, axis=1)
    across = jnp.transpose(log_decay, (0, 2, 1))
    causal = jnp.arange(length)[:, None] >= jnp.arange(length)[None, :]
    inside = ((ids_blk[:, :, None] == ids_blk[:, None, :]) & causal[None])[:, None]
    spread = across[:, :, :, None] - across[:, :, None, :]
    weights = jnp.where(inside, jnp.exp(jnp.where(inside, spread, 0.0)), 0.0)
    intersection = jnp.einsum('sqn,skn->sqk', queries_c, keys_b, precision=PRECISION_MAX)
    scores = intersection[:, None] * weights * jnp.transpose(step_sizes, (0, 2, 1))[:, :, None, :]
    output = jnp.einsum('shqk,skhp->sqhp', scores, values, precision=PRECISION_MAX)
    carried = (ids_blk == prev_ids[:, None]).astype(jnp.float32)
    from_state = jnp.einsum('sqn,shpn->sqhp', queries_c, state_now, precision=PRECISION_MAX)
    output = output + (jnp.exp(log_decay) * carried[:, :, None])[..., None] * from_state
    ending = (ids_blk == ids_blk[:, -1:]).astype(jnp.float32)
    toward = jnp.exp(log_decay[:, -1:, :] - log_decay) * step_sizes * ending[:, :, None]
    fresh_state = jnp.einsum('sqhp,sqn->shpn', toward[..., None] * values, keys_b, precision=PRECISION_MAX)
    decay_total = jnp.exp(log_decay[:, -1, :]) * carried[:, -1:]
    new_state = fresh_state + decay_total[:, :, None, None] * state_now
    return ((new_state, ids_blk[:, -1]), output)

def mixer_layer(inputs, norm_gain, input_weight, conv_w, conv_b, dt_bias, a_log, d_skip, gate_gain, output_weight, segments):
    seq_count, length, model_width = inputs.shape
    inner_width = HEADS * HEADDIM
    channels = inner_width + 2 * STATE
    normalized_input = reduced_value(rms_scale(inputs, norm_gain))
    projected_input = reduced_backward(reduced_value(jnp.einsum('ive,eu->ivu', normalized_input, input_weight, precision=PRECISION_MAX)))
    gate_z = projected_input[..., :inner_width]
    mixed_in = projected_input[..., inner_width:inner_width + channels]
    step_raw = projected_input[..., inner_width + channels:]
    conv_out = conv_b + conv_w[0] * mixed_in
    for shift_by in range(1, CONV):
        earlier = jnp.pad(mixed_in, ((0, 0), (shift_by, 0), (0, 0)))[:, :length]
        same_doc = jnp.concatenate([jnp.zeros((seq_count, shift_by), bool), segments[:, shift_by:] == segments[:, :-shift_by]], axis=1)
        conv_out = conv_out + conv_w[shift_by] * earlier * same_doc[..., None].astype(jnp.float32)
    activated = jax.nn.silu(conv_out)
    values = activated[..., :inner_width].reshape(seq_count, length, HEADS, HEADDIM)
    keys_b = activated[..., inner_width:inner_width + STATE]
    queries_c = activated[..., inner_width + STATE:]
    step_sizes = jax.nn.softplus(step_raw + dt_bias)
    rates = -step_sizes * jnp.exp(a_log)
    block_count = length // BLOCK

    def to_blocks(source):
        shaped = source.reshape((seq_count, block_count, BLOCK) + source.shape[2:])
        return jnp.moveaxis(shaped, 1, 0)
    start = (jnp.zeros((seq_count, HEADS, HEADDIM, STATE), jnp.float32), jnp.full((seq_count,), -1, jnp.int32))
    blocked = tuple(map(to_blocks, (values, keys_b, queries_c, step_sizes, rates, segments)))
    final_carry, outputs = lax.scan(jax.checkpoint(ssd_block), start, blocked)
    outputs = jnp.moveaxis(outputs, 0, 1).reshape(seq_count, length, HEADS, HEADDIM)
    outputs = outputs + d_skip[:, None] * values
    gated_out = outputs.reshape(seq_count, length, inner_width) * jax.nn.silu(gate_z)
    gated_normalized = reduced_value(rms_scale(gated_out, gate_gain))
    branch_value = jnp.einsum('rph,hw->rpw', gated_normalized, output_weight, precision=PRECISION_MAX)
    return inputs + branch_value

def reference(tokens, norm_gain, input_weight, conv_w, conv_b, dt_bias, a_log, d_skip, gate_gain, output_weight, segments, cotangent):
    weights = tuple((source.astype(jnp.float32) for source in (norm_gain, input_weight, conv_w, conv_b, dt_bias, a_log, d_skip, gate_gain, output_weight)))
    per_group = math.gcd(SEQS, max(1, 4096 // LENGTH))
    group_count = SEQS // per_group

    def regroup(source):
        return source.reshape((group_count, per_group) + source.shape[1:])

    def one_group(totals, pieces):
        inputs, segment_ids, cot_block = pieces

        def forward(inputs_f, norm_f, in_f, conv_wf, conv_bf, bias_f, alog_f, skip_f, gate_f, out_f):
            return mixer_layer(inputs_f, norm_f, in_f, conv_wf, conv_bf, bias_f, alog_f, skip_f, gate_f, out_f, segment_ids)
        result, pullback = jax.vjp(forward, inputs.astype(jnp.float32), weights[0], weights[1], weights[2], weights[3], weights[4], weights[5], weights[6], weights[7], weights[8])
        gradients = pullback(cot_block.astype(jnp.float32))
        totals = tuple((total + extra for total, extra in zip(totals, gradients[1:])))
        return (totals, (result.astype(jnp.bfloat16), gradients[0].astype(jnp.bfloat16)))
    zero_grads = tuple((jnp.zeros_like(source) for source in weights))
    totals, (outputs, input_grads) = lax.scan(one_group, zero_grads, (regroup(tokens), regroup(segments), regroup(cotangent)))
    return (outputs.reshape(tokens.shape), input_grads.reshape(tokens.shape), totals[0], totals[1], totals[2], totals[3], totals[4], totals[5], totals[6], totals[7], totals[8])
```

```python
from functools import partial

import jax
import jax.numpy as jnp
from jax import lax
from jax.experimental import pallas as pl
from jax.experimental.pallas import tpu as pltpu
from jax.sharding import PartitionSpec as P

HEADS = 48
STATE = 128
HEADDIM = 64
CONV = 4
INNER = HEADS * HEADDIM
CHANNELS = INNER + 2 * STATE
GROUP = 8
GROUPS = HEADS // GROUP
WIDTH = GROUP * HEADDIM
LANES = 128
EPSILON = 1e-05
VMEM = 60 * 1024 * 1024
BOTH = ("seq", "ctx")
FAR = -1e30
f32 = jnp.float32
bf16 = jnp.bfloat16
MM = partial(jnp.dot, preferred_element_type=f32)


def mm_nt(a, b):
    return lax.dot_general(a, b, (((1,), (1,)), ((), ())), preferred_element_type=f32)


def mm_tn(a, b):
    return lax.dot_general(a, b, (((0,), (0,)), ((), ())), preferred_element_type=f32)


def at(j, width):
    return pl.ds(pl.multiple_of(j * width, width), width)


def low_half(rows):
    return lax.broadcasted_iota(jnp.int32, (rows, LANES), 1) < HEADDIM


def to_front(columns, g):
    return pltpu.roll(columns, lax.rem(LANES - GROUP * g, LANES), 1)


def spread(front, pair, low):
    return jnp.where(low, front[:, 2 * pair : 2 * pair + 1], front[:, 2 * pair + 1 : 2 * pair + 2])


def head_sums(product, g):
    lane = lax.broadcasted_iota(jnp.int32, (WIDTH, LANES), 1)
    row = lax.broadcasted_iota(jnp.int32, (WIDTH, LANES), 0)
    pick = jnp.where(lane == GROUP * g + row // HEADDIM, 1.0, 0.0).astype(bf16)
    high = product.astype(bf16)
    rest = (product - high.astype(f32)).astype(bf16)
    return MM(high, pick) + MM(rest, pick)


def taps(px_ref, tail, j, w_ref, b_ref, masks, ext):
    here = at(j, LANES)
    length = px_ref.shape[0]
    own = px_ref[:, here].astype(f32)
    ext[0:8, :] = tail
    ext[8 : 8 + length, :] = own
    inputs = [own] + [
        masks[k - 1] * ext[8 - k : 8 - k + length, :] for k in range(1, CONV)
    ]
    out = b_ref[0:1, here]
    for k in range(CONV):
        out = out + w_ref[k : k + 1, here] * inputs[k]
    return out, inputs


def tail_of(tail_ref, s, here):
    both = tail_ref[:, here].astype(f32)
    return jnp.where(s == 0, both[0:8], both[8:16])


def lane_masks(cols_ref, length):
    return [
        jnp.broadcast_to(cols_ref[0, :, k : k + 1], (length, LANES)) for k in range(CONV - 1)
    ]


def before_kernel(px_ref, tail_ref, w_ref, b_ref, cols_ref, heads_ref,
                  act_ref, tok_ref, cst_ref, fresh_ref, ext):
    s = pl.program_id(0)
    length = px_ref.shape[0]
    masks = lane_masks(cols_ref, length)

    @pl.loop(0, CHANNELS // LANES)
    def _(j):
        here = at(j, LANES)
        conv, _unused = taps(px_ref, tail_of(tail_ref, s, here), j, w_ref, b_ref, masks, ext)
        act_ref[0, :, here] = conv * jax.nn.sigmoid(conv)

    raw = px_ref[:, CHANNELS : CHANNELS + HEADS].astype(f32) + heads_ref[0:1, :HEADS]
    step = jnp.maximum(raw, 0.0) + jnp.log1p(jnp.exp(-jnp.abs(raw)))
    step = jnp.concatenate([step, jnp.zeros((length, LANES - HEADS), f32)], axis=1)
    rate = -step * jnp.exp(heads_ref[1:2, :])
    before = (
        lax.broadcasted_iota(jnp.int32, (length, length), 0)
        >= lax.broadcasted_iota(jnp.int32, (length, length), 1)
    ).astype(f32)
    decay = jnp.dot(before, rate, precision=lax.Precision.HIGHEST, preferred_element_type=f32)
    tok_ref[0, :, 0:LANES] = step
    tok_ref[0, :, LANES : 2 * LANES] = decay
    cst_ref[0] = decay.T[:HEADS]
    toward = jnp.exp(decay[length - 1 : length] - decay) * step * cols_ref[0, :, 4:5]
    keys = act_ref[0, :, INNER : INNER + STATE].astype(bf16)
    low = low_half(length)

    @pl.loop(0, GROUPS)
    def _(g):
        front = to_front(toward, g)
        for pair in range(GROUP // 2):
            here = pl.ds(pl.multiple_of(g * WIDTH + pair * LANES, LANES), LANES)
            scaled = (act_ref[0, :, here] * spread(front, pair, low)).astype(bf16)
            fresh_ref[0, here, :] = mm_tn(scaled, keys)


def bias_of(ids_col, ids_row, transposed):
    shape = (ids_col.shape[0], ids_row.shape[1])
    down = lax.broadcasted_iota(jnp.int32, shape, 0)
    across = lax.broadcasted_iota(jnp.int32, shape, 1)
    order = (down <= across) if transposed else (down >= across)
    return jnp.where(order & (ids_col == ids_row), 0.0, FAR)


def within_kernel(act_ref, tok_ref, cst_ref, cols_ref, rows_ref, y_ref, cross, bias):
    length = act_ref.shape[1]
    half = length // 2
    cross[...] = mm_nt(
        act_ref[0, :, INNER + STATE :].astype(bf16),
        act_ref[0, :, INNER : INNER + STATE].astype(bf16),
    )
    bias[...] = bias_of(cols_ref[0, :, 5:6], rows_ref[0, 0:1, :], False)
    low = low_half(length)

    @pl.loop(0, GROUPS)
    def _(g):
        step = to_front(tok_ref[0, :, 0:LANES], g)
        decay = to_front(tok_ref[0, :, LANES : 2 * LANES], g)
        rows = cst_ref[0, at(g, GROUP), :]
        for pair in range(GROUP // 2):
            here = pl.ds(pl.multiple_of(g * WIDTH + pair * LANES, LANES), LANES)
            scaled = act_ref[0, :, here] * spread(step, pair, low)
            top, bottom = 0.0, 0.0
            for which in range(2):
                h = 2 * pair + which
                mine = jnp.where(low == (which == 0), scaled, 0.0).astype(bf16)
                col, row = decay[:, h : h + 1], rows[h : h + 1, :]
                w = jnp.exp(col[:half] - row[:, :half] + bias[:half, :half])
                top = top + MM((cross[:half, :half] * w).astype(bf16), mine[:half])
                w = jnp.exp(col[half:] - row + bias[half:, :])
                bottom = bottom + MM((cross[half:, :] * w).astype(bf16), mine)
            y_ref[0, :half, here] = top
            y_ref[0, half:, here] = bottom


def gate_kernel(z_ref, act_ref, tok_ref, cols_ref, y_ref, state_ref, dgn_ref, lanes_ref,
                gn_ref, dz_ref, dy_ref, dstate_ref, q_ref, dq_ref, sums_ref, total, queries_acc):
    length = act_ref.shape[1]
    low = low_half(length)
    enter = jnp.exp(tok_ref[0, :, LANES : 2 * LANES]) * cols_ref[0, :, 3:4]
    queries = act_ref[0, :, INNER + STATE :].astype(bf16)

    def first(g, carry):
        square, inner = carry
        front = to_front(enter, g)
        for pair in range(GROUP // 2):
            here = pl.ds(pl.multiple_of(g * WIDTH + pair * LANES, LANES), LANES)
            far = mm_nt(queries, state_ref[0, here, :])
            y = y_ref[0, :, here] + spread(front, pair, low) * far
            total[:, here] = y
            y = y + lanes_ref[1:2, here] * act_ref[0, :, here]
            z = z_ref[:, here].astype(f32)
            gated = y * (z * jax.nn.sigmoid(z))
            square = square + gated * gated
            inner = inner + lanes_ref[0:1, here] * dgn_ref[:, here] * gated
        return square, inner

    zero = jnp.zeros((length, LANES), f32)
    square, inner = lax.fori_loop(0, GROUPS, first, (zero, zero))
    scale = lax.rsqrt(jnp.sum(square, axis=1, keepdims=True) * (1.0 / INNER) + EPSILON)
    back = scale * scale * scale * (jnp.sum(inner, axis=1, keepdims=True) * (1.0 / INNER))
    scale = jnp.broadcast_to(scale, (length, LANES))
    back = jnp.broadcast_to(back, (length, LANES))
    queries_acc[...] = jnp.zeros_like(queries_acc)
    dq_ref[0] = jnp.zeros_like(dq_ref[0])

    @pl.loop(0, GROUPS)
    def _(g):
        front = to_front(enter, g)
        products = []
        for pair in range(GROUP // 2):
            here = pl.ds(pl.multiple_of(g * WIDTH + pair * LANES, LANES), LANES)
            xs = act_ref[0, :, here]
            inside = total[:, here]
            y = inside + lanes_ref[1:2, here] * xs
            z = z_ref[:, here].astype(f32)
            sg = jax.nn.sigmoid(z)
            gate = z * sg
            gated = y * gate
            gain = lanes_ref[0:1, here]
            dgn = dgn_ref[:, here]
            gn = gated * scale
            gn_ref[:, here] = (gn * gain).astype(bf16)
            dgated = scale * (gain * dgn) - gated * back
            dy = dgated * gate
            dz_ref[:, here] = (dgated * y * (sg * (1.0 + z * (1.0 - sg)))).astype(bf16)
            rounded = dy.astype(bf16)
            dy_ref[0, :, here] = rounded
            sums_ref[0, 0:1, here] = jnp.sum(dgn * gn, axis=0, keepdims=True)
            sums_ref[0, 1:2, here] = jnp.sum(dy * xs, axis=0, keepdims=True)
            entered = (rounded.astype(f32) * spread(front, pair, low)).astype(bf16)
            dstate_ref[0, here, :] = mm_tn(entered, queries)
            queries_acc[...] += MM(entered, state_ref[0, here, :])
            products.append(rounded.astype(f32) * inside)
        dq_ref[0] += head_sums(jnp.concatenate(products, axis=1), g)

    q_ref[0] = queries_acc[...]


def scan_back_kernel(act_ref, tok_ref, cst_ref, cols_ref, rows_ref, dy_ref,
                     dx_ref, dbc_ref, cross, bias, dcross):
    length = act_ref.shape[1]
    half = length // 2
    keys = act_ref[0, :, INNER : INNER + STATE].astype(bf16)
    queries = act_ref[0, :, INNER + STATE :].astype(bf16)
    cross[...] = mm_nt(keys, queries)
    bias[...] = bias_of(cols_ref[0, :, 5:6], rows_ref[0, 0:1, :], True)
    dcross[...] = jnp.zeros_like(dcross)
    low = low_half(length)

    @pl.loop(0, GROUPS)
    def _(g):
        step = to_front(tok_ref[0, :, 0:LANES], g)
        decay = to_front(tok_ref[0, :, LANES : 2 * LANES], g)
        rows = cst_ref[0, at(g, GROUP), :]
        for pair in range(GROUP // 2):
            here = pl.ds(pl.multiple_of(g * WIDTH + pair * LANES, LANES), LANES)
            scaled = (act_ref[0, :, here] * spread(step, pair, low)).astype(bf16)
            dy = dy_ref[0, :, here].astype(f32)
            top, bottom = 0.0, 0.0
            for which in range(2):
                h = 2 * pair + which
                mine = jnp.where(low == (which == 0), dy, 0.0).astype(bf16)
                col, row = decay[:, h : h + 1], rows[h : h + 1, :]
                w = jnp.exp(row - col[:half] + bias[:half, :])
                dcross[:half, :] += mm_nt(scaled[:half], mine) * w
                top = top + MM((cross[:half, :] * w).astype(bf16), mine)
                w = jnp.exp(row[:, half:] - col[half:] + bias[half:, half:])
                dcross[half:, half:] += mm_nt(scaled[half:], mine[half:]) * w
                bottom = bottom + MM((cross[half:, half:] * w).astype(bf16), mine[half:])
            dx_ref[0, :half, here] = top
            dx_ref[0, half:, here] = bottom

    d = dcross[...].astype(bf16)
    dbc_ref[0, :, :STATE] = MM(d, queries)
    dbc_ref[0, :, STATE:] = mm_tn(d, keys)


def after_kernel(px_ref, tail_ref, w_ref, b_ref, cols_ref, heads_ref, act_ref, tok_ref, lanes_ref,
                 dy_ref, dx_ref, dbc_ref, q_ref, dq_ref, later_ref, kept_ref,
                 dpx_ref, edge_ref, dconv_ref, dheads_ref, ext, moved, grad, dstep_acc, dcol_acc, keys_acc, ends, sent):
    s = pl.program_id(0)
    length = act_ref.shape[1]
    low = low_half(length)
    step = tok_ref[0, :, 0:LANES]
    decay = tok_ref[0, :, LANES : 2 * LANES]
    leave = jnp.exp(decay[length - 1 : length] - decay) * cols_ref[0, :, 4:5]
    keys = act_ref[0, :, INNER : INNER + STATE].astype(bf16)
    dstep_acc[...] = jnp.zeros_like(dstep_acc)
    dcol_acc[...] = jnp.zeros_like(dcol_acc)
    sent[...] = jnp.zeros_like(sent)
    keys_acc[...] = dbc_ref[0, :, :STATE]
    ends[...] = jnp.zeros_like(ends)

    @pl.loop(0, GROUPS)
    def _(g):
        step_front, leave_front = to_front(step, g), to_front(leave, g)
        products, columns = [], []
        for pair in range(GROUP // 2):
            here = pl.ds(pl.multiple_of(g * WIDTH + pair * LANES, LANES), LANES)
            later = later_ref[0, here, :]
            xs = act_ref[0, :, here]
            steps = spread(step_front, pair, low)
            leaving = spread(leave_front, pair, low)
            through = leaving * mm_nt(keys, later)
            dscaled = dx_ref[0, :, here] + through
            scaled = steps * xs
            rounded = scaled.astype(bf16).astype(f32)
            keys_acc[...] += MM((leaving * scaled).astype(bf16), later)
            products.append(xs * dscaled)
            columns.append(rounded * dscaled)
            sent[0:1, here] = jnp.sum(rounded * through, axis=0, keepdims=True)
            grad[:, here] = steps * dscaled + lanes_ref[1:2, here] * dy_ref[0, :, here].astype(f32)
            both = later.astype(f32) * kept_ref[0, here, :]
            at_row = GROUP * g + 2 * pair
            ends[pl.ds(at_row, 1), :] = jnp.sum(both[:HEADDIM], axis=0, keepdims=True)
            ends[pl.ds(at_row + 1, 1), :] = jnp.sum(both[HEADDIM:], axis=0, keepdims=True)
        dstep_acc[...] += head_sums(jnp.concatenate(products, axis=1), g)
        dcol_acc[...] += head_sums(jnp.concatenate(columns, axis=1), g)

    grad[:, INNER : INNER + STATE] = keys_acc[...]
    grad[:, INNER + STATE :] = dbc_ref[0, :, STATE:] + q_ref[0]
    dstep = dstep_acc[...]
    at_end = jnp.sum(ends[...].T, axis=0, keepdims=True)
    for g in range(GROUPS):
        at_end = at_end + head_sums(sent[:, g * WIDTH : (g + 1) * WIDTH], g)[0:1]
    row = lax.broadcasted_iota(jnp.int32, (length, LANES), 0)
    ddecay = dq_ref[0] - dcol_acc[...] + jnp.where(row == length - 1, at_end, 0.0)
    onward = (
        lax.broadcasted_iota(jnp.int32, (length, length), 0)
        <= lax.broadcasted_iota(jnp.int32, (length, length), 1)
    ).astype(f32)
    drate = jnp.dot(onward, ddecay, precision=lax.Precision.HIGHEST, preferred_element_type=f32)
    speed = jnp.exp(heads_ref[1:2, :])
    raw = px_ref[:, CHANNELS : CHANNELS + HEADS].astype(f32) + heads_ref[0:1, :HEADS]
    draw = (dstep - drate * speed)[:, :HEADS] * jax.nn.sigmoid(raw)
    dpx_ref[:, CHANNELS:] = jnp.concatenate(
        [draw, jnp.zeros((length, LANES - HEADS), f32)], axis=1
    ).astype(bf16)
    edge_ref[0, :, CHANNELS:] = jnp.zeros((8, LANES), f32)
    dheads_ref[0] = jnp.zeros((8, LANES), f32)
    dheads_ref[0, 0:1, :HEADS] = jnp.sum(draw, axis=0, keepdims=True)
    dheads_ref[0, 1:2, :] = jnp.sum(drate * (-step * speed), axis=0, keepdims=True)

    masks = lane_masks(cols_ref, length)
    moved[...] = jnp.zeros_like(moved)
    dconv_ref[0] = jnp.zeros((8, CHANNELS), f32)

    @pl.loop(0, CHANNELS // LANES)
    def _(j):
        here = at(j, LANES)
        conv, inputs = taps(px_ref, tail_of(tail_ref, s, here), j, w_ref, b_ref, masks, ext)
        sg = jax.nn.sigmoid(conv)
        dconv = grad[:, here] * (sg * (1.0 + conv * (1.0 - sg)))
        for k in range(CONV):
            dconv_ref[0, k : k + 1, here] = jnp.sum(dconv * inputs[k], axis=0, keepdims=True)
        dconv_ref[0, CONV : CONV + 1, here] = jnp.sum(dconv, axis=0, keepdims=True)
        dx = w_ref[0:1, here] * dconv
        edge = jnp.zeros((8, LANES), f32)
        for k in range(1, CONV):
            moved[k - 1, 8 : 8 + length, :] = dconv * masks[k - 1]
            dx = dx + w_ref[k : k + 1, here] * moved[k - 1, 8 + k : 8 + k + length, :]
            edge = edge + w_ref[k : k + 1, here] * moved[k - 1, k : 8 + k, :]
        dpx_ref[:, here] = dx.astype(bf16)
        edge_ref[0, :, here] = edge


def whole(shape):
    return pl.BlockSpec(shape, lambda s: (0,) * len(shape))


def per_seq(*tail):
    return pl.BlockSpec((1,) + tail, lambda s: (s,) + (0,) * len(tail))


def per_rows(rows, width):
    return pl.BlockSpec((rows, width), lambda s: (s, 0))


def call(kernel, count, in_specs, outs, scratch, *args):
    return pl.pallas_call(
        kernel,
        grid=(count,),
        in_specs=in_specs,
        out_specs=[spec for spec, _unused in outs],
        out_shape=[jax.ShapeDtypeStruct(*made) for _unused, made in outs],
        scratch_shapes=scratch,
        compiler_params=pltpu.CompilerParams(vmem_limit_bytes=VMEM),
    )(*args)


def chain(own, factor, steps):
    entered = jnp.zeros(own.shape, bf16)
    for source, target in steps:
        sent = (own + factor * entered.astype(f32)).astype(bf16)
        entered = entered + lax.ppermute(sent, "ctx", [(source, target)])
    return entered


def pad_lanes(v):
    return jnp.pad(v, (0, LANES - v.shape[0]))


NZ = 4


def place():
    seq, ctx = lax.axis_index("seq"), lax.axis_index("ctx")
    return seq // 2, lax.rem(seq, 2), ctx // 2, lax.rem(ctx, 2)


def device(z, y, x, c):
    return {"seq": z * 2 + y, "ctx": x * 2 + c}


def greet(z, y, x, c):
    barrier = pltpu.get_barrier_semaphore()
    others = [device(z, y, x, 1 - c), device(z, y, 1 - x, c), device(z, 1 - y, x, c)]
    others += [device(lax.rem(z + d, NZ), y, x, c) for d in range(1, NZ)]
    for other in others:
        pl.semaphore_signal(barrier, inc=1, device_id=other, device_id_type=pl.DeviceIdType.MESH)
    pl.semaphore_wait(barrier, len(others))


def remote(src, dst, send, recv, target):
    return pltpu.make_async_remote_copy(
        src_ref=src, dst_ref=dst, send_sem=send, recv_sem=recv, device_id=target,
        device_id_type=pl.DeviceIdType.MESH,
    )


def gather_kernel(units, n, *refs):
    ins, outs, (send, recv, local) = refs[:n], refs[n : 2 * n], refs[2 * n :]
    x_first = [first for _array, _row, _rows, first in units]
    z, y, x, c = place()
    greet(z, y, x, c)
    started = []

    def shard(u):
        a, row, rows, _first = units[u]
        return ins[a].at[pl.ds(row, rows)]

    def slot_of(u, *at):
        a, row, rows, _first = units[u]
        return outs[a].at[at + (pl.ds(row, rows),)]

    def push(u, zz, yy, xx, stage, own=False):
        slot = slot_of(u, zz, yy, xx, c)
        kind, index = stage
        target = {
            "x": device(z, y, 1 - x, c), "y": device(z, 1 - y, x, c), "c": device(z, y, x, 1 - c),
        }.get(kind)
        if kind == "z":
            target = device(lax.rem(z + index, NZ), y, x, c)
        copy = remote(shard(u) if own else slot, slot, send.at[u, number(u, stage)], recv.at[u, number(u, stage)], target)
        copy.start()
        started.append(copy)
        return copy

    def number(u, stage):
        kind, index = stage
        first = "x" if x_first[u] else "y"
        base = 0 if kind == "z" else 3 if kind == first else 15 if kind == "c" else 7
        return base + (index - 1 if kind == "z" else index)

    def came(u, zz, yy, xx, cc, stage):
        slot = slot_of(u, zz, yy, xx, cc)
        k = number(u, stage)
        remote(slot, slot, send.at[u, k], recv.at[u, k], device(z, y, x, 1 - c)).wait_recv()

    back = [lax.rem(z + NZ - d, NZ) for d in range(NZ)]
    own_copies = []
    for u in range(len(units)):
        a, b = ("x", "y") if x_first[u] else ("y", "x")
        for d in range(1, NZ):
            push(u, z, y, x, ("z", d), own=True)
        push(u, z, y, x, (b, 0), own=True)
        push(u, z, y, x, (a, 0), own=True)
        push(u, z, y, x, ("c", 0), own=True)
        own_copies.append(pltpu.make_async_copy(shard(u), slot_of(u, z, y, x, c), local.at[u]))
        own_copies[-1].start()
    for d in range(1, NZ + 1):
        for u in range(len(units)):
            a, b = ("x", "y") if x_first[u] else ("y", "x")
            if d < NZ:
                came(u, back[d], y, x, c, ("z", d))
                push(u, back[d], y, x, (b, d))
                push(u, back[d], y, x, (a, d))
                push(u, back[d], y, x, ("c", d))
            yy, xx = (y, 1 - x) if a == "x" else (1 - y, x)
            came(u, back[d - 1], yy, xx, c, (a, d - 1))
            push(u, back[d - 1], yy, xx, (b, NZ + d - 1))
            push(u, back[d - 1], yy, xx, ("c", NZ + d - 1))
    for half in range(2):
        for d in range(NZ):
            for u in range(len(units)):
                a, b = ("x", "y") if x_first[u] else ("y", "x")
                yy, xx = (1 - y, x) if b == "y" else (y, 1 - x)
                if half:
                    yy, xx = 1 - y, 1 - x
                came(u, back[d], yy, xx, c, (b, NZ * half + d))
                push(u, back[d], yy, xx, ("c", 2 * NZ + NZ * half + d))
    for u in range(len(units)):
        for k in range(16):
            a = "x" if x_first[u] else "y"
            away_a, away_b = (k // NZ) % 2, k // (2 * NZ)
            ax, ay = (away_a, away_b) if a == "x" else (away_b, away_a)
            xx = 1 - x if ax else x
            yy = 1 - y if ay else y
            came(u, back[k % NZ], yy, xx, 1 - c, ("c", k))
    for copy in started:
        copy.wait_send()
    for copy in own_copies:
        copy.wait()


def gather_all(shards, units):
    n, m = len(shards), len(units)
    return pl.pallas_call(
        partial(gather_kernel, tuple(units), n),
        out_shape=[jax.ShapeDtypeStruct((NZ, 2, 2, 2) + v.shape, v.dtype) for v in shards],
        in_specs=[pl.BlockSpec(memory_space=pl.ANY)] * n,
        out_specs=[pl.BlockSpec(memory_space=pl.ANY)] * n,
        scratch_shapes=[
            pltpu.SemaphoreType.DMA((m, 31)), pltpu.SemaphoreType.DMA((m, 31)), pltpu.SemaphoreType.DMA((m,)),
        ],
        compiler_params=pltpu.CompilerParams(collective_id=0, has_side_effects=True, vmem_limit_bytes=8 * 1024 * 1024),
    )(*shards)


CUT_ROWS, CUT = 48, 512


def cuts_of(shape):
    rows, columns = shape[-2:]
    return [(r, k, min(CUT, columns - k)) for k in range(0, columns, CUT) for r in range(0, rows, CUT_ROWS)]


def reduce_kernel(n, lead, *refs):
    ins, outs, scratch = refs[: n + 1], refs[n + 1 : 2 * n + 2], refs[2 * n + 2 :]
    (own, core, first, second, last, own_s, core_s, first_s, second_s, last_s, sem, semz) = scratch
    z, y, x, c = place()
    greet(z, y, x, c)
    pieces = [(a, cut) for a in range(n) for cut in cuts_of(ins[a].shape)]
    total = len(pieces) + 1
    sent = []

    def begin(i):
        own_i, core_i = view(i, 0), view(i, 1)
        if i == total - 1:
            src_out, src_own = ins[n].at[:, :, :, 1 - c], ins[n].at[:, :, :, c]
        else:
            a, (r, k, w) = pieces[i]
            rows, cols = pl.ds(r, CUT_ROWS), pl.ds(k, w)
            src_out = ins[a].at[:, :, :, 1 - c, rows, cols]
            src_own = ins[a].at[:, :, :, c, rows, cols]
        go = remote(src_out, core_i, sem.at[0, i], sem.at[1, i], device(z, y, x, 1 - c))
        go.start()
        sent.append(go)
        pltpu.make_async_copy(src_own, own_i, sem.at[2, i]).start()

    def view(i, k):
        if i == total - 1:
            return (own_s, core_s, first_s, second_s, last_s)[k]
        v = (own, core, first, second, last)[k]
        w = pieces[i][1][2]
        if w == CUT:
            return v.at[i]
        free = len(v.shape) - 2
        return v.at[(i,) + (slice(None),) * free + (pl.ds(0, w),)]

    def x_goes_first(i):
        return i % 2 == 0

    def after_core(i):
        own_i, core_i = view(i, 0), view(i, 1)
        remote(core_i, core_i, sem.at[0, i], sem.at[1, i], device(z, y, x, 1 - c)).wait_recv()
        pltpu.make_async_copy(own_i, own_i, sem.at[2, i]).wait()

        @pl.loop(0, NZ)
        def _(zz):
            for yy in range(2):
                for xx in range(2):
                    core_i[zz, yy, xx] = core_i[zz, yy, xx] + own_i[zz, yy, xx]

        if x_goes_first(i):
            src, to = core_i.at[:, :, 1 - x], device(z, y, 1 - x, c)
        else:
            src, to = core_i.at[:, 1 - y], device(z, 1 - y, x, c)
        go = remote(src, view(i, 2), sem.at[3, i], sem.at[4, i], to)
        go.start()
        sent.append(go)

    def after_first(i):
        core_i, first_i = view(i, 1), view(i, 2)
        remote(first_i, first_i, sem.at[3, i], sem.at[4, i], device(z, y, x, 1 - c)).wait_recv()

        @pl.loop(0, NZ)
        def _(zz):
            for o in range(2):
                mine = core_i[zz, o, x] if x_goes_first(i) else core_i[zz, y, o]
                first_i[zz, o] = first_i[zz, o] + mine

        if x_goes_first(i):
            src, to = first_i.at[:, 1 - y], device(z, 1 - y, x, c)
        else:
            src, to = first_i.at[:, 1 - x], device(z, y, 1 - x, c)
        go = remote(src, view(i, 3), sem.at[5, i], sem.at[6, i], to)
        go.start()
        sent.append(go)

    def after_second(i):
        first_i, second_i, last_i = view(i, 2), view(i, 3), view(i, 4)
        remote(second_i, second_i, sem.at[5, i], sem.at[6, i], device(z, y, x, 1 - c)).wait_recv()

        @pl.loop(0, NZ)
        def _(zz):
            second_i[zz] = second_i[zz] + (first_i[zz, y] if x_goes_first(i) else first_i[zz, x])

        for d in range(1, NZ):
            zz = lax.rem(z + d, NZ)
            go = remote(second_i.at[zz], last_i.at[z], semz.at[0, d, i], semz.at[1, d, i], device(zz, y, x, c))
            go.start()
            sent.append(go)
        last_i[z] = second_i[z]

    def after_last(i):
        last_i = view(i, 4)
        for d in range(1, NZ):
            zz = lax.rem(z + NZ - d, NZ)
            remote(last_i.at[zz], last_i.at[zz], semz.at[0, d, i], semz.at[1, d, i], device(z, y, x, 1 - c)).wait_recv()
        value = last_i[0].astype(f32)
        for zz in range(1, NZ):
            value = value + last_i[zz].astype(f32)
        if i == total - 1:
            outs[n][...] = value
        else:
            a, (r, k, w) = pieces[i]
            outs[a][r : r + CUT_ROWS, k : k + w] = value

    order = [total - 1] + list(range(total - 1))
    for i in order:
        begin(i)
    stages = (after_core, after_first, after_second, after_last)
    for t in range(total + lead[-1]):
        for stage, skew in reversed(list(zip(stages, lead))):
            if 0 <= t - skew < total:
                stage(order[t - skew])
    for go in sent:
        go.wait_send()


def reduce_all(arrays, small, lead=(0, 4, 6, 8)):
    n = len(arrays)
    arrays = [v.reshape((NZ, 2, 2, 2, -1, v.shape[-1])) for v in arrays]
    small = small.reshape((NZ, 2, 2, 2, -1, small.shape[-1]))
    p = sum(len(cuts_of(v.shape)) for v in arrays)
    ss = small.shape[-2:]
    made = [jax.ShapeDtypeStruct(v.shape[-2:], f32) for v in arrays + [small]]
    dims = [(NZ, 2, 2), (NZ, 2, 2), (NZ, 2), (NZ,), (NZ,)]
    return pl.pallas_call(
        partial(reduce_kernel, n, tuple(lead)),
        out_shape=made,
        in_specs=[pl.BlockSpec(memory_space=pl.ANY)] * (n + 1),
        out_specs=[pl.BlockSpec(memory_space=pltpu.VMEM)] * (n + 1),
        scratch_shapes=[pltpu.VMEM((p,) + d + (CUT_ROWS, CUT), bf16) for d in dims]
        + [pltpu.VMEM(d + ss, f32) for d in dims]
        + [pltpu.SemaphoreType.DMA((7, p + 1)), pltpu.SemaphoreType.DMA((2, NZ, p + 1))],
        compiler_params=pltpu.CompilerParams(collective_id=1, has_side_effects=True, vmem_limit_bytes=VMEM),
    )(*arrays, small)


def local(tokens, norm_gain, input_weight, conv_w, conv_b, dt_bias, a_log, d_skip, gate_gain,
          output_weight, segments, cotangent):
    seqs, length, width = tokens.shape
    n_ctx = lax.axis_size("ctx")
    n_all = n_ctx * lax.axis_size("seq")
    count = seqs * length
    shares = [norm_gain.shape[0], gate_gain.shape[0], CONV * conv_b.shape[0], conv_b.shape[0]]
    cuts = [sum(shares[: i + 1]) for i in range(3)]
    packed = jnp.concatenate([norm_gain, gate_gain, conv_w.reshape(-1), conv_b])
    torus = lax.axis_size("seq") == 2 * NZ and n_ctx == 4 and norm_gain.shape[0] == CUT_ROWS
    w_z, w_x = input_weight[:, :INNER], input_weight[:, INNER:]
    if torus:
        size = packed.shape[0]
        small = jnp.pad(packed, (0, 16 * LANES - size)).reshape(16, LANES)
        half = output_weight.shape[0] // 2
        w_x, w_z, w_out, packed = gather_all(
            [w_x, w_z, output_weight, small],
            [(0, 0, CUT_ROWS, True), (1, 0, CUT_ROWS, False), (2, 0, half, True),
             (2, half, half, False), (3, 0, 16, True)],
        )
        w_x, w_z, w_out = (w.reshape(-1, w.shape[-1]) for w in (w_x, w_z, w_out))
        packed = packed.reshape(n_all, -1)[:, :size]
    else:
        packed = lax.all_gather(packed, BOTH, axis=0)
        w_in, w_out = (
            lax.all_gather(w, BOTH, axis=0, tiled=True) for w in (input_weight, output_weight)
        )
        w_z, w_x = w_in[:, :INNER], w_in[:, INNER:]
    norm_full, gate_full, conv_w_full, conv_b_full = jnp.split(packed.astype(f32), cuts, axis=1)
    norm_full = norm_full.reshape(1, -1)
    gate_full = gate_full.reshape(1, -1)
    conv_b_full = conv_b_full.reshape(1, -1)
    conv_w_full = conv_w_full.reshape(n_all, CONV, -1).transpose(1, 0, 2).reshape(CONV, -1)

    onward = [(i, i + 1) for i in range(n_ctx - 1)]
    tail_tokens = lax.ppermute(tokens[:, length - (CONV - 1) :], "ctx", onward)
    tail_ids = lax.ppermute(segments[:, length - (CONV - 1) :], "ctx", onward)
    tail_ids = jnp.where(lax.axis_index("ctx") == 0, -1, tail_ids)
    tail_tokens = jnp.pad(tail_tokens, ((0, 0), (8 - (CONV - 1), 0), (0, 0)))
    x_all = jnp.concatenate([tokens.reshape(count, width), tail_tokens.reshape(seqs * 8, width)])
    x_all = x_all.astype(f32)
    r_all = lax.rsqrt(jnp.mean(x_all * x_all, axis=-1, keepdims=True) + EPSILON)
    normed = (x_all * r_all * norm_full).astype(bf16)

    ids_ext = jnp.concatenate([tail_ids, segments], axis=1)
    flags = [
        segments == ids_ext[:, CONV - 1 - k : CONV - 1 - k + length] for k in range(1, CONV)
    ] + [segments == ids_ext[:, CONV - 2 : CONV - 1], segments == segments[:, -1:]]
    cols = jnp.stack([f.astype(f32) for f in flags] + [segments.astype(f32)], axis=-1)
    cols = jnp.pad(cols, ((0, 0), (0, 0), (0, LANES - cols.shape[-1])))
    rows = jnp.pad(segments.astype(f32)[:, None], ((0, 0), (0, 7), (0, 0)))
    heads = jnp.pad(jnp.stack([pad_lanes(dt_bias), pad_lanes(a_log)]), ((0, 6), (0, 0)))
    lanes = jnp.concatenate([gate_full, jnp.repeat(d_skip, HEADDIM)[None]])
    lanes = jnp.pad(lanes, ((0, 6), (0, 0)))
    conv_w8 = jnp.pad(conv_w_full, ((0, 8 - CONV), (0, 0)))
    conv_b8 = jnp.pad(conv_b_full, ((0, 7), (0, 0)))

    px = MM(normed, w_x).astype(bf16)
    px_width, dpx_width = CHANNELS + HEADS, CHANNELS + LANES
    tail_spec = pl.BlockSpec((16, px_width), lambda s: (count // 16, 0))
    act, tok, cst, fresh = call(
        before_kernel, seqs,
        [per_rows(length, px_width), tail_spec, whole((8, CHANNELS)), whole((8, CHANNELS)),
         per_seq(length, LANES), whole((8, LANES))],
        [(per_seq(length, CHANNELS), ((seqs, length, CHANNELS), f32)),
         (per_seq(length, 2 * LANES), ((seqs, length, 2 * LANES), f32)),
         (per_seq(HEADS, length), ((seqs, HEADS, length), f32)),
         (per_seq(INNER, STATE), ((seqs, INNER, STATE), f32))],
        [pltpu.VMEM((length + 8, LANES), f32)],
        px, px, conv_w8, conv_b8, cols, heads,
    )
    carried = cols[:, length - 1, 3]
    kept = jnp.exp(cst[:, :, length - 1]) * carried[:, None]
    kept = jnp.repeat(kept, HEADDIM, axis=1)[..., None]
    entering = chain(fresh, kept, onward)
    stayed = kept * entering.astype(f32)
    pz = MM(normed[:count], w_z).astype(bf16)
    g2 = cotangent.reshape(count, width)
    dgn = lax.dot_general(g2, w_out, (((1,), (1,)), ((), ())), preferred_element_type=f32)
    [y] = call(
        within_kernel, seqs,
        [per_seq(length, CHANNELS), per_seq(length, 2 * LANES), per_seq(HEADS, length),
         per_seq(length, LANES), per_seq(8, length)],
        [(per_seq(length, INNER), ((seqs, length, INNER), f32))],
        [pltpu.VMEM((length, length), f32), pltpu.VMEM((length, length), f32)],
        act, tok, cst, cols, rows,
    )
    gn, dz, dy, dstate, dqueries, ddecay, sums = call(
        gate_kernel, seqs,
        [per_rows(length, INNER), per_seq(length, CHANNELS), per_seq(length, 2 * LANES),
         per_seq(length, LANES), per_seq(length, INNER), per_seq(INNER, STATE),
         per_rows(length, INNER), whole((8, INNER))],
        [(per_rows(length, INNER), ((count, INNER), bf16)),
         (per_rows(length, INNER), ((count, INNER), bf16)),
         (per_seq(length, INNER), ((seqs, length, INNER), bf16)),
         (per_seq(INNER, STATE), ((seqs, INNER, STATE), f32)),
         (per_seq(length, STATE), ((seqs, length, STATE), f32)),
         (per_seq(length, LANES), ((seqs, length, LANES), f32)),
         (per_seq(8, INNER), ((seqs, 8, INNER), f32))],
        [pltpu.VMEM((length, INNER), f32), pltpu.VMEM((length, STATE), f32)],
        pz, act, tok, cols, y, entering, dgn, lanes,
    )
    later = chain(dstate, kept, [(b, a) for a, b in reversed(onward)])
    output = (x_all[:count] + MM(gn, w_out)).astype(bf16)
    dw_out = lax.dot_general(gn, g2, (((0,), (0,)), ((), ())), preferred_element_type=f32)
    dw_z = lax.dot_general(normed[:count], dz, (((0,), (0,)), ((), ())), preferred_element_type=f32)
    dx, dbc = call(
        scan_back_kernel, seqs,
        [per_seq(length, CHANNELS), per_seq(length, 2 * LANES), per_seq(HEADS, length),
         per_seq(length, LANES), per_seq(8, length), per_seq(length, INNER)],
        [(per_seq(length, INNER), ((seqs, length, INNER), f32)),
         (per_seq(length, 2 * STATE), ((seqs, length, 2 * STATE), f32))],
        [pltpu.VMEM((length, length), f32)] * 3,
        act, tok, cst, cols, rows, dy,
    )
    dpx, edge, dconv, dheads = call(
        after_kernel, seqs,
        [per_rows(length, px_width), tail_spec, whole((8, CHANNELS)), whole((8, CHANNELS)),
         per_seq(length, LANES), whole((8, LANES)), per_seq(length, CHANNELS),
         per_seq(length, 2 * LANES), whole((8, INNER)), per_seq(length, INNER),
         per_seq(length, INNER), per_seq(length, 2 * STATE), per_seq(length, STATE),
         per_seq(length, LANES), per_seq(INNER, STATE), per_seq(INNER, STATE)],
        [(per_rows(length, dpx_width), ((count, dpx_width), bf16)),
         (per_seq(8, dpx_width), ((seqs, 8, dpx_width), f32)),
         (per_seq(8, CHANNELS), ((seqs, 8, CHANNELS), f32)),
         (per_seq(8, LANES), ((seqs, 8, LANES), f32))],
        [pltpu.VMEM((length + 8, LANES), f32), pltpu.VMEM((CONV - 1, length + 16, LANES), f32),
         pltpu.VMEM((length, CHANNELS), f32), pltpu.VMEM((length, LANES), f32),
         pltpu.VMEM((length, LANES), f32), pltpu.VMEM((length, STATE), f32), pltpu.VMEM((LANES, LANES), f32),
         pltpu.VMEM((8, INNER), f32)],
        px, px, conv_w8, conv_b8, cols, heads, act, tok, lanes, dy, dx, dbc, dqueries, ddecay,
        later, stayed,
    )
    dpx_all = jnp.concatenate([dpx, edge.reshape(seqs * 8, dpx_width).astype(bf16)])
    dw_x = lax.dot_general(normed, dpx_all, (((0,), (0,)), ((), ())), preferred_element_type=f32)
    nt = (((1,), (1,)), ((), ()))
    dnormed_x = lax.dot_general(dpx_all[:, :px_width], w_x, nt, preferred_element_type=f32)
    dnormed = dnormed_x[:count] + lax.dot_general(dz, w_z, nt, preferred_element_type=f32)
    back = dnormed_x[count:].reshape(seqs, 8, width)[:, 8 - (CONV - 1) :].astype(bf16)
    back = lax.ppermute(back, "ctx", [(b, a) for a, b in onward])
    back = jnp.pad(back.astype(f32), ((0, 0), (length - (CONV - 1), 0), (0, 0)))
    dnormed = dnormed + back.reshape(count, width)
    x, r = x_all[:count], r_all[:count]
    d_gain = jnp.sum(x * r * dnormed, axis=0)
    scaled = norm_full * dnormed
    dx_in = r * (scaled - x * (r * r) * jnp.mean(x * scaled, axis=-1, keepdims=True))
    input_grad = (g2.astype(f32) + dx_in).astype(bf16)

    sums = jnp.sum(sums, axis=0)
    dconv = jnp.sum(dconv, axis=0)
    dheads = jnp.sum(dheads, axis=0)
    d_skip_sum = jnp.sum(sums[1].reshape(HEADS, HEADDIM), axis=1)
    split = [d_gain.reshape(n_all, -1), sums[0].reshape(n_all, -1),
             dconv[:CONV].reshape(CONV, n_all, -1).transpose(1, 0, 2).reshape(n_all, -1),
             dconv[CONV].reshape(n_all, -1)]
    shared = jnp.concatenate([dheads[0, :HEADS], dheads[1, :HEADS], d_skip_sum])
    split = jnp.concatenate(split, axis=1)
    share = sum(shares)
    if torus:
        fill = 8 * LANES - share - shared.shape[0]
        split = [split, jnp.broadcast_to(shared, (n_all,) + shared.shape), jnp.zeros((n_all, fill), f32)]
        dw_out, dw_z, dw_x, mine = reduce_all(
            [v.astype(bf16) for v in (dw_out, dw_z, dw_x)],
            jnp.concatenate(split, axis=1).reshape(n_all, 8, LANES),
        )
        dw_in = jnp.concatenate([dw_z, dw_x[:, :px_width]], axis=1)
        mine = mine.reshape(-1)
        mine, shared = mine[:share], mine[share : share + shared.shape[0]]
    else:
        dw_in = jnp.concatenate([dw_z, dw_x[:, :px_width]], axis=1)
        dw_out, dw_in = (
            lax.psum_scatter(v, BOTH, scatter_dimension=0, tiled=True) for v in (dw_out, dw_in)
        )
        every = lax.psum(jnp.concatenate([split.reshape(-1), shared]), BOTH)
        me = lax.axis_index("seq") * n_ctx + lax.axis_index("ctx")
        mine, shared = lax.dynamic_slice(every, (me * share,), (share,)), every[n_all * share :]
    d_norm, d_gate, d_conv_w, d_conv_b = jnp.split(mine, cuts)
    d_bias, d_alog, d_skips = jnp.split(shared, 3)
    return (
        output.reshape(tokens.shape), input_grad.reshape(tokens.shape), d_norm, dw_in,
        d_conv_w.reshape(CONV, -1), d_conv_b, d_bias, d_alog, d_skips, d_gate, dw_out,
    )


def solution(mesh):
    split = P(BOTH)
    rows = P(BOTH, None)
    seq = P("seq", "ctx", None)
    in_specs = (seq, split, rows, P(None, BOTH), split, P(), P(), P(), split, rows,
                P("seq", "ctx"), seq)
    out_specs = (seq, seq, split, rows, P(None, BOTH), split, P(), P(), P(), split, rows)
    return jax.shard_map(local, mesh=mesh, in_specs=in_specs, out_specs=out_specs, check_vma=False)
```

```python
from functools import partial

import jax
import jax.numpy as jnp
from jax import lax
from jax.experimental import pallas as pl
from jax.experimental.pallas import tpu as pltpu
from jax.sharding import PartitionSpec as P

HEADS = 48
STATE = 128
HEADDIM = 64
CONV = 4
INNER = HEADS * HEADDIM
CHANNELS = INNER + 2 * STATE
GROUP = 8
GROUPS = HEADS // GROUP
WIDTH = GROUP * HEADDIM
LANES = 128
EPSILON = 1e-05
VMEM = 60 * 1024 * 1024
BOTH = ("seq", "ctx")
FAR = -1e30
f32 = jnp.float32
bf16 = jnp.bfloat16
MM = partial(jnp.dot, preferred_element_type=f32)


def mm_nt(a, b):
    return lax.dot_general(a, b, (((1,), (1,)), ((), ())), preferred_element_type=f32)


def mm_tn(a, b):
    return lax.dot_general(a, b, (((0,), (0,)), ((), ())), preferred_element_type=f32)


def at(j, width):
    return pl.ds(pl.multiple_of(j * width, width), width)


def low_half(rows):
    return lax.broadcasted_iota(jnp.int32, (rows, LANES), 1) < HEADDIM


def to_front(columns, g):
    return pltpu.roll(columns, lax.rem(LANES - GROUP * g, LANES), 1)


def spread(front, pair, low):
    return jnp.where(low, front[:, 2 * pair : 2 * pair + 1], front[:, 2 * pair + 1 : 2 * pair + 2])


def head_sums(product, g):
    lane = lax.broadcasted_iota(jnp.int32, (WIDTH, LANES), 1)
    row = lax.broadcasted_iota(jnp.int32, (WIDTH, LANES), 0)
    pick = jnp.where(lane == GROUP * g + row // HEADDIM, 1.0, 0.0).astype(bf16)
    high = product.astype(bf16)
    rest = (product - high.astype(f32)).astype(bf16)
    return MM(high, pick) + MM(rest, pick)


def taps(px_ref, tail, j, w_ref, b_ref, masks, ext):
    here = at(j, LANES)
    length = px_ref.shape[0]
    own = px_ref[:, here].astype(f32)
    ext[0:8, :] = tail
    ext[8 : 8 + length, :] = own
    inputs = [own] + [
        masks[k - 1] * ext[8 - k : 8 - k + length, :] for k in range(1, CONV)
    ]
    out = b_ref[0:1, here]
    for k in range(CONV):
        out = out + w_ref[k : k + 1, here] * inputs[k]
    return out, inputs


def tail_of(tail_ref, s, here):
    both = tail_ref[:, here].astype(f32)
    return jnp.where(s == 0, both[0:8], both[8:16])


def lane_masks(cols_ref, length):
    return [
        jnp.broadcast_to(cols_ref[0, :, k : k + 1], (length, LANES)) for k in range(CONV - 1)
    ]


def before_kernel(px_ref, tail_ref, w_ref, b_ref, cols_ref, heads_ref,
                  act_ref, tok_ref, cst_ref, fresh_ref, ext):
    s = pl.program_id(0)
    length = px_ref.shape[0]
    masks = lane_masks(cols_ref, length)

    @pl.loop(0, CHANNELS // LANES)
    def _(j):
        here = at(j, LANES)
        conv, _unused = taps(px_ref, tail_of(tail_ref, s, here), j, w_ref, b_ref, masks, ext)
        act_ref[0, :, here] = conv * jax.nn.sigmoid(conv)

    raw = px_ref[:, CHANNELS : CHANNELS + HEADS].astype(f32) + heads_ref[0:1, :HEADS]
    step = jnp.maximum(raw, 0.0) + jnp.log1p(jnp.exp(-jnp.abs(raw)))
    step = jnp.concatenate([step, jnp.zeros((length, LANES - HEADS), f32)], axis=1)
    rate = -step * jnp.exp(heads_ref[1:2, :])
    before = (
        lax.broadcasted_iota(jnp.int32, (length, length), 0)
        >= lax.broadcasted_iota(jnp.int32, (length, length), 1)
    ).astype(f32)
    decay = jnp.dot(before, rate, precision=lax.Precision.HIGHEST, preferred_element_type=f32)
    tok_ref[0, :, 0:LANES] = step
    tok_ref[0, :, LANES : 2 * LANES] = decay
    cst_ref[0] = decay.T[:HEADS]
    toward = jnp.exp(decay[length - 1 : length] - decay) * step * cols_ref[0, :, 4:5]
    keys = act_ref[0, :, INNER : INNER + STATE].astype(bf16)
    low = low_half(length)

    @pl.loop(0, GROUPS)
    def _(g):
        front = to_front(toward, g)
        for pair in range(GROUP // 2):
            here = pl.ds(pl.multiple_of(g * WIDTH + pair * LANES, LANES), LANES)
            scaled = (act_ref[0, :, here] * spread(front, pair, low)).astype(bf16)
            fresh_ref[0, here, :] = mm_tn(scaled, keys)


def bias_of(ids_col, ids_row, transposed):
    shape = (ids_col.shape[0], ids_row.shape[1])
    down = lax.broadcasted_iota(jnp.int32, shape, 0)
    across = lax.broadcasted_iota(jnp.int32, shape, 1)
    order = (down <= across) if transposed else (down >= across)
    return jnp.where(order & (ids_col == ids_row), 0.0, FAR)


def within_kernel(act_ref, tok_ref, cst_ref, cols_ref, rows_ref, y_ref, cross, bias):
    length = act_ref.shape[1]
    half = length // 2
    cross[...] = mm_nt(
        act_ref[0, :, INNER + STATE :].astype(bf16),
        act_ref[0, :, INNER : INNER + STATE].astype(bf16),
    )
    bias[...] = bias_of(cols_ref[0, :, 5:6], rows_ref[0, 0:1, :], False)
    low = low_half(length)

    @pl.loop(0, GROUPS)
    def _(g):
        step = to_front(tok_ref[0, :, 0:LANES], g)
        decay = to_front(tok_ref[0, :, LANES : 2 * LANES], g)
        rows = cst_ref[0, at(g, GROUP), :]
        for pair in range(GROUP // 2):
            here = pl.ds(pl.multiple_of(g * WIDTH + pair * LANES, LANES), LANES)
            scaled = act_ref[0, :, here] * spread(step, pair, low)
            top, bottom = 0.0, 0.0
            for which in range(2):
                h = 2 * pair + which
                mine = jnp.where(low == (which == 0), scaled, 0.0).astype(bf16)
                col, row = decay[:, h : h + 1], rows[h : h + 1, :]
                w = jnp.exp(col[:half] - row[:, :half] + bias[:half, :half])
                top = top + MM((cross[:half, :half] * w).astype(bf16), mine[:half])
                w = jnp.exp(col[half:] - row + bias[half:, :])
                bottom = bottom + MM((cross[half:, :] * w).astype(bf16), mine)
            y_ref[0, :half, here] = top
            y_ref[0, half:, here] = bottom


def gate_kernel(z_ref, act_ref, tok_ref, cols_ref, y_ref, state_ref, dgn_ref, lanes_ref,
                gn_ref, dz_ref, dy_ref, dstate_ref, q_ref, dq_ref, sums_ref, total, queries_acc):
    length = act_ref.shape[1]
    low = low_half(length)
    enter = jnp.exp(tok_ref[0, :, LANES : 2 * LANES]) * cols_ref[0, :, 3:4]
    queries = act_ref[0, :, INNER + STATE :].astype(bf16)

    def first(g, carry):
        square, inner = carry
        front = to_front(enter, g)
        for pair in range(GROUP // 2):
            here = pl.ds(pl.multiple_of(g * WIDTH + pair * LANES, LANES), LANES)
            far = mm_nt(queries, state_ref[0, here, :])
            y = y_ref[0, :, here] + spread(front, pair, low) * far
            total[:, here] = y
            y = y + lanes_ref[1:2, here] * act_ref[0, :, here]
            z = z_ref[:, here].astype(f32)
            gated = y * (z * jax.nn.sigmoid(z))
            square = square + gated * gated
            inner = inner + lanes_ref[0:1, here] * dgn_ref[:, here] * gated
        return square, inner

    zero = jnp.zeros((length, LANES), f32)
    square, inner = lax.fori_loop(0, GROUPS, first, (zero, zero))
    scale = lax.rsqrt(jnp.sum(square, axis=1, keepdims=True) * (1.0 / INNER) + EPSILON)
    back = scale * scale * scale * (jnp.sum(inner, axis=1, keepdims=True) * (1.0 / INNER))
    scale = jnp.broadcast_to(scale, (length, LANES))
    back = jnp.broadcast_to(back, (length, LANES))
    queries_acc[...] = jnp.zeros_like(queries_acc)
    dq_ref[0] = jnp.zeros_like(dq_ref[0])

    @pl.loop(0, GROUPS)
    def _(g):
        front = to_front(enter, g)
        products = []
        for pair in range(GROUP // 2):
            here = pl.ds(pl.multiple_of(g * WIDTH + pair * LANES, LANES), LANES)
            xs = act_ref[0, :, here]
            inside = total[:, here]
            y = inside + lanes_ref[1:2, here] * xs
            z = z_ref[:, here].astype(f32)
            sg = jax.nn.sigmoid(z)
            gate = z * sg
            gated = y * gate
            gain = lanes_ref[0:1, here]
            dgn = dgn_ref[:, here]
            gn = gated * scale
            gn_ref[:, here] = (gn * gain).astype(bf16)
            dgated = scale * (gain * dgn) - gated * back
            dy = dgated * gate
            dz_ref[:, here] = (dgated * y * (sg * (1.0 + z * (1.0 - sg)))).astype(bf16)
            rounded = dy.astype(bf16)
            dy_ref[0, :, here] = rounded
            sums_ref[0, 0:1, here] = jnp.sum(dgn * gn, axis=0, keepdims=True)
            sums_ref[0, 1:2, here] = jnp.sum(dy * xs, axis=0, keepdims=True)
            entered = (rounded.astype(f32) * spread(front, pair, low)).astype(bf16)
            dstate_ref[0, here, :] = mm_tn(entered, queries)
            queries_acc[...] += MM(entered, state_ref[0, here, :])
            products.append(rounded.astype(f32) * inside)
        dq_ref[0] += head_sums(jnp.concatenate(products, axis=1), g)

    q_ref[0] = queries_acc[...]


def scan_back_kernel(act_ref, tok_ref, cst_ref, cols_ref, rows_ref, dy_ref,
                     dx_ref, dbc_ref, cross, bias, dcross):
    length = act_ref.shape[1]
    half = length // 2
    keys = act_ref[0, :, INNER : INNER + STATE].astype(bf16)
    queries = act_ref[0, :, INNER + STATE :].astype(bf16)
    cross[...] = mm_nt(keys, queries)
    bias[...] = bias_of(cols_ref[0, :, 5:6], rows_ref[0, 0:1, :], True)
    dcross[...] = jnp.zeros_like(dcross)
    low = low_half(length)

    @pl.loop(0, GROUPS)
    def _(g):
        step = to_front(tok_ref[0, :, 0:LANES], g)
        decay = to_front(tok_ref[0, :, LANES : 2 * LANES], g)
        rows = cst_ref[0, at(g, GROUP), :]
        for pair in range(GROUP // 2):
            here = pl.ds(pl.multiple_of(g * WIDTH + pair * LANES, LANES), LANES)
            scaled = (act_ref[0, :, here] * spread(step, pair, low)).astype(bf16)
            dy = dy_ref[0, :, here].astype(f32)
            top, bottom = 0.0, 0.0
            for which in range(2):
                h = 2 * pair + which
                mine = jnp.where(low == (which == 0), dy, 0.0).astype(bf16)
                col, row = decay[:, h : h + 1], rows[h : h + 1, :]
                w = jnp.exp(row - col[:half] + bias[:half, :])
                dcross[:half, :] += mm_nt(scaled[:half], mine) * w
                top = top + MM((cross[:half, :] * w).astype(bf16), mine)
                w = jnp.exp(row[:, half:] - col[half:] + bias[half:, half:])
                dcross[half:, half:] += mm_nt(scaled[half:], mine[half:]) * w
                bottom = bottom + MM((cross[half:, half:] * w).astype(bf16), mine[half:])
            dx_ref[0, :half, here] = top
            dx_ref[0, half:, here] = bottom

    d = dcross[...].astype(bf16)
    dbc_ref[0, :, :STATE] = MM(d, queries)
    dbc_ref[0, :, STATE:] = mm_tn(d, keys)


def after_kernel(px_ref, tail_ref, w_ref, b_ref, cols_ref, heads_ref, act_ref, tok_ref, lanes_ref,
                 dy_ref, dx_ref, dbc_ref, q_ref, dq_ref, later_ref, kept_ref,
                 dpx_ref, edge_ref, dconv_ref, dheads_ref, ext, moved, grad, dstep_acc, dcol_acc, keys_acc, ends, sent):
    s = pl.program_id(0)
    length = act_ref.shape[1]
    low = low_half(length)
    step = tok_ref[0, :, 0:LANES]
    decay = tok_ref[0, :, LANES : 2 * LANES]
    leave = jnp.exp(decay[length - 1 : length] - decay) * cols_ref[0, :, 4:5]
    keys = act_ref[0, :, INNER : INNER + STATE].astype(bf16)
    dstep_acc[...] = jnp.zeros_like(dstep_acc)
    dcol_acc[...] = jnp.zeros_like(dcol_acc)
    sent[...] = jnp.zeros_like(sent)
    keys_acc[...] = dbc_ref[0, :, :STATE]
    ends[...] = jnp.zeros_like(ends)

    @pl.loop(0, GROUPS)
    def _(g):
        step_front, leave_front = to_front(step, g), to_front(leave, g)
        products, columns = [], []
        for pair in range(GROUP // 2):
            here = pl.ds(pl.multiple_of(g * WIDTH + pair * LANES, LANES), LANES)
            later = later_ref[0, here, :]
            xs = act_ref[0, :, here]
            steps = spread(step_front, pair, low)
            leaving = spread(leave_front, pair, low)
            through = leaving * mm_nt(keys, later)
            dscaled = dx_ref[0, :, here] + through
            scaled = steps * xs
            rounded = scaled.astype(bf16).astype(f32)
            keys_acc[...] += MM((leaving * scaled).astype(bf16), later)
            products.append(xs * dscaled)
            columns.append(rounded * dscaled)
            sent[0:1, here] = jnp.sum(rounded * through, axis=0, keepdims=True)
            grad[:, here] = steps * dscaled + lanes_ref[1:2, here] * dy_ref[0, :, here].astype(f32)
            both = later.astype(f32) * kept_ref[0, here, :]
            at_row = GROUP * g + 2 * pair
            ends[pl.ds(at_row, 1), :] = jnp.sum(both[:HEADDIM], axis=0, keepdims=True)
            ends[pl.ds(at_row + 1, 1), :] = jnp.sum(both[HEADDIM:], axis=0, keepdims=True)
        dstep_acc[...] += head_sums(jnp.concatenate(products, axis=1), g)
        dcol_acc[...] += head_sums(jnp.concatenate(columns, axis=1), g)

    grad[:, INNER : INNER + STATE] = keys_acc[...]
    grad[:, INNER + STATE :] = dbc_ref[0, :, STATE:] + q_ref[0]
    dstep = dstep_acc[...]
    at_end = jnp.sum(ends[...].T, axis=0, keepdims=True)
    for g in range(GROUPS):
        at_end = at_end + head_sums(sent[:, g * WIDTH : (g + 1) * WIDTH], g)[0:1]
    row = lax.broadcasted_iota(jnp.int32, (length, LANES), 0)
    ddecay = dq_ref[0] - dcol_acc[...] + jnp.where(row == length - 1, at_end, 0.0)
    onward = (
        lax.broadcasted_iota(jnp.int32, (length, length), 0)
        <= lax.broadcasted_iota(jnp.int32, (length, length), 1)
    ).astype(f32)
    drate = jnp.dot(onward, ddecay, precision=lax.Precision.HIGHEST, preferred_element_type=f32)
    speed = jnp.exp(heads_ref[1:2, :])
    raw = px_ref[:, CHANNELS : CHANNELS + HEADS].astype(f32) + heads_ref[0:1, :HEADS]
    draw = (dstep - drate * speed)[:, :HEADS] * jax.nn.sigmoid(raw)
    dpx_ref[:, CHANNELS:] = jnp.concatenate(
        [draw, jnp.zeros((length, LANES - HEADS), f32)], axis=1
    ).astype(bf16)
    edge_ref[0, :, CHANNELS:] = jnp.zeros((8, LANES), f32)
    dheads_ref[0] = jnp.zeros((8, LANES), f32)
    dheads_ref[0, 0:1, :HEADS] = jnp.sum(draw, axis=0, keepdims=True)
    dheads_ref[0, 1:2, :] = jnp.sum(drate * (-step * speed), axis=0, keepdims=True)

    masks = lane_masks(cols_ref, length)
    moved[...] = jnp.zeros_like(moved)
    dconv_ref[0] = jnp.zeros((8, CHANNELS), f32)

    @pl.loop(0, CHANNELS // LANES)
    def _(j):
        here = at(j, LANES)
        conv, inputs = taps(px_ref, tail_of(tail_ref, s, here), j, w_ref, b_ref, masks, ext)
        sg = jax.nn.sigmoid(conv)
        dconv = grad[:, here] * (sg * (1.0 + conv * (1.0 - sg)))
        for k in range(CONV):
            dconv_ref[0, k : k + 1, here] = jnp.sum(dconv * inputs[k], axis=0, keepdims=True)
        dconv_ref[0, CONV : CONV + 1, here] = jnp.sum(dconv, axis=0, keepdims=True)
        dx = w_ref[0:1, here] * dconv
        edge = jnp.zeros((8, LANES), f32)
        for k in range(1, CONV):
            moved[k - 1, 8 : 8 + length, :] = dconv * masks[k - 1]
            dx = dx + w_ref[k : k + 1, here] * moved[k - 1, 8 + k : 8 + k + length, :]
            edge = edge + w_ref[k : k + 1, here] * moved[k - 1, k : 8 + k, :]
        dpx_ref[:, here] = dx.astype(bf16)
        edge_ref[0, :, here] = edge


def whole(shape):
    return pl.BlockSpec(shape, lambda s: (0,) * len(shape))


def per_seq(*tail):
    return pl.BlockSpec((1,) + tail, lambda s: (s,) + (0,) * len(tail))


def per_rows(rows, width):
    return pl.BlockSpec((rows, width), lambda s: (s, 0))


def call(kernel, count, in_specs, outs, scratch, *args):
    return pl.pallas_call(
        kernel,
        grid=(count,),
        in_specs=in_specs,
        out_specs=[spec for spec, _unused in outs],
        out_shape=[jax.ShapeDtypeStruct(*made) for _unused, made in outs],
        scratch_shapes=scratch,
        compiler_params=pltpu.CompilerParams(vmem_limit_bytes=VMEM),
    )(*args)


def chain(own, factor, steps, beside):
    entered = jnp.zeros(own.shape, bf16)
    results = []
    for k, (source, target) in enumerate(steps):
        sent = own.astype(bf16) if k == 0 else (own + factor * entered.astype(f32)).astype(bf16)
        came = lax.ppermute(sent, "ctx", [(source, target)])
        for work in beside[k :: len(steps)]:
            results.append(work())
            came, results[-1] = lax.optimization_barrier((came, results[-1]))
        entered = came if k == 0 else entered + came
    return entered, results


def pad_lanes(v):
    return jnp.pad(v, (0, LANES - v.shape[0]))


NZ = 4


def place():
    seq, ctx = lax.axis_index("seq"), lax.axis_index("ctx")
    return seq // 2, lax.rem(seq, 2), ctx // 2, lax.rem(ctx, 2)


def device(z, y, x, c):
    return {"seq": z * 2 + y, "ctx": x * 2 + c}


def greet(z, y, x, c, more=0):
    barrier = pltpu.get_barrier_semaphore()
    others = [device(z, y, x, 1 - c), device(z, y, 1 - x, c), device(z, 1 - y, x, c)]
    others += [device(lax.rem(z + d, NZ), y, x, c) for d in range(1, NZ)]
    for other in others:
        pl.semaphore_signal(barrier, inc=1, device_id=other, device_id_type=pl.DeviceIdType.MESH)
    pl.semaphore_wait(barrier, len(others) + more)


def remote(src, dst, send, recv, target):
    return pltpu.make_async_remote_copy(
        src_ref=src, dst_ref=dst, send_sem=send, recv_sem=recv, device_id=target,
        device_id_type=pl.DeviceIdType.MESH,
    )


def gather_kernel(units, n, *refs):
    ins, outs, land, (tail_land, send, recv, local, store, tail_sem) = (
        refs[: n + 1], refs[n + 1 : 2 * n + 2], refs[2 * n + 2 : 3 * n + 2], refs[3 * n + 2 :]
    )
    x_first = [first for _array, _row, _rows, first in units]
    z, y, x, c = place()
    ctx = x * 2 + c
    after, before = lax.rem(ctx + 1, 4), lax.rem(ctx + 3, 4)
    barrier = pltpu.get_barrier_semaphore()
    for other in (after, before):
        pl.semaphore_signal(
            barrier, inc=1, device_id={"seq": z * 2 + y, "ctx": other},
            device_id_type=pl.DeviceIdType.MESH,
        )
    greet(z, y, x, c, 2)
    started, stored = [], []

    def shard(u):
        a, row, rows, _first = units[u]
        return ins[a].at[pl.ds(row, rows)]

    def slot_of(u, *at, into=None):
        a, row, rows, _first = units[u]
        return (land if into is None else into)[a].at[at + (pl.ds(row, rows),)]

    def number(u, kind, index):
        first = "x" if x_first[u] else "y"
        base = 0 if kind == "z" else 3 if kind == first else 15 if kind == "c" else 7
        return base + (index - 1 if kind == "z" else index)

    def push(u, zz, yy, xx, kind, index):
        slot = slot_of(u, zz, yy, xx, c)
        if kind == "z":
            target = device(lax.rem(z + index, NZ), y, x, c)
        else:
            flip = [1 - v if k == kind else v for k, v in (("y", y), ("x", x), ("c", c))]
            target = device(z, *flip)
        k = number(u, kind, index)
        copy = remote(slot, slot, send.at[u, k], recv.at[u, k], target)
        copy.start()
        started.append(copy)

    def came(u, zz, yy, xx, cc, kind, index):
        slot = slot_of(u, zz, yy, xx, cc)
        k = number(u, kind, index)
        remote(slot, slot, send.at[u, k], recv.at[u, k], device(z, y, x, 1 - c)).wait_recv()
        keep = pltpu.make_async_copy(slot, slot_of(u, zz, yy, xx, cc, into=outs), store.at[u, k])
        keep.start()
        stored.append(keep)

    back = [lax.rem(z + NZ - d, NZ) for d in range(NZ)]
    axes = [("x", "y") if first else ("y", "x") for first in x_first]
    every = range(len(units))
    ring = remote(
        ins[n], tail_land, tail_sem.at[0], tail_sem.at[1], {"seq": z * 2 + y, "ctx": after}
    )
    ring.start()
    for u in every:
        pltpu.make_async_copy(shard(u), slot_of(u, z, y, x, c), local.at[u]).start()

    def open_unit(u):
        a, b = axes[u]
        slot = slot_of(u, z, y, x, c)
        pltpu.make_async_copy(shard(u), slot, local.at[u]).wait()
        for d in (1, 3, 2):
            push(u, z, y, x, "z", d)
        for kind in (b, a, "c"):
            push(u, z, y, x, kind, 0)
        keep = pltpu.make_async_copy(slot, slot_of(u, z, y, x, c, into=outs), local.at[u])
        keep.start()
        stored.append(keep)

    def pass_on(u):
        a, b = axes[u]
        yy, xx = (y, 1 - x) if a == "x" else (1 - y, x)
        for d in range(1, NZ + 1):
            if d < NZ:
                came(u, back[d], y, x, c, "z", d)
                for kind in (b, a, "c"):
                    push(u, back[d], y, x, kind, d)
            came(u, back[d - 1], yy, xx, c, a, d - 1)
            push(u, back[d - 1], yy, xx, b, NZ + d - 1)
            push(u, back[d - 1], yy, xx, "c", NZ + d - 1)

    def cross(u):
        a, b = axes[u]
        for half in range(2):
            yy, xx = (1 - y, x) if b == "y" else (y, 1 - x)
            if half:
                yy, xx = 1 - y, 1 - x
            for d in range(NZ):
                came(u, back[d], yy, xx, c, b, NZ * half + d)
                push(u, back[d], yy, xx, "c", 2 * NZ + NZ * half + d)

    def finish(u):
        a, b = axes[u]
        for k in range(16):
            away = {a: (k // NZ) % 2, b: k // (2 * NZ)}
            came(u, back[k % NZ], 1 - y if away["y"] else y, 1 - x if away["x"] else x, 1 - c, "c", k)

    for t in range(-AHEAD, len(units) + 4):
        if 0 <= t + AHEAD < len(units):
            open_unit(t + AHEAD)
        if 0 <= t < len(units):
            pass_on(t)
        if 0 <= t - 2 < len(units):
            cross(t - 2)
        if 0 <= t - 4 < len(units):
            finish(t - 4)
    ring.wait_recv()
    keep = pltpu.make_async_copy(tail_land, outs[n], tail_sem.at[2])
    keep.start()
    keep.wait()
    ring.wait_send()
    for copy in started:
        copy.wait_send()
    for keep in stored:
        keep.wait()


def gather_all(shards, tail, units):
    n, m = len(shards), len(units)
    full = [(NZ, 2, 2, 2) + v.shape for v in shards]
    return pl.pallas_call(
        partial(gather_kernel, tuple(units), n),
        out_shape=[jax.ShapeDtypeStruct(f, v.dtype) for f, v in zip(full, shards)]
        + [jax.ShapeDtypeStruct(tail.shape, tail.dtype)],
        in_specs=[pl.BlockSpec(memory_space=pl.ANY)] * (n + 1),
        out_specs=[pl.BlockSpec(memory_space=pl.ANY)] * (n + 1),
        scratch_shapes=[pltpu.VMEM(f, v.dtype) for f, v in zip(full, shards)] + [
            pltpu.VMEM(tail.shape, tail.dtype),
            pltpu.SemaphoreType.DMA((m, 31)), pltpu.SemaphoreType.DMA((m, 31)),
            pltpu.SemaphoreType.DMA((m,)), pltpu.SemaphoreType.DMA((m, 31)),
            pltpu.SemaphoreType.DMA((3,)),
        ],
        compiler_params=pltpu.CompilerParams(
            collective_id=0, has_side_effects=True, vmem_limit_bytes=VMEM
        ),
    )(*shards, tail)


CUT_ROWS, CUT = 48, 512
AHEAD = 4


def cuts_of(shape):
    rows, columns = shape[-2:]
    return [(r, k, min(CUT, columns - k)) for k in range(0, columns, CUT) for r in range(0, rows, CUT_ROWS)]


def reduce_kernel(n, lead, *refs):
    ins, outs, scratch = refs[: n + 1], refs[n + 1 : 2 * n + 2], refs[2 * n + 2 :]
    (own, core, first, second, last, own_s, core_s, first_s, second_s, last_s, sem, semz) = scratch
    z, y, x, c = place()
    greet(z, y, x, c)
    pieces = [(a, cut) for a in range(n) for cut in cuts_of(ins[a].shape)]
    total = len(pieces) + 1
    sent = []

    def begin(i):
        own_i, core_i = view(i, 0), view(i, 1)
        if i == total - 1:
            src_out, src_own = ins[n].at[:, :, :, 1 - c], ins[n].at[:, :, :, c]
        else:
            a, (r, k, w) = pieces[i]
            rows, cols = pl.ds(r, CUT_ROWS), pl.ds(k, w)
            src_out = ins[a].at[:, :, :, 1 - c, rows, cols]
            src_own = ins[a].at[:, :, :, c, rows, cols]
        go = remote(src_out, core_i, sem.at[0, i], sem.at[1, i], device(z, y, x, 1 - c))
        go.start()
        sent.append(go)
        pltpu.make_async_copy(src_own, own_i, sem.at[2, i]).start()

    def view(i, k):
        if i == total - 1:
            return (own_s, core_s, first_s, second_s, last_s)[k]
        v = (own, core, first, second, last)[k]
        w = pieces[i][1][2]
        if w == CUT:
            return v.at[i]
        free = len(v.shape) - 2
        return v.at[(i,) + (slice(None),) * free + (pl.ds(0, w),)]

    def x_goes_first(i):
        return i % 2 == 0

    def after_core(i):
        own_i, core_i = view(i, 0), view(i, 1)
        remote(core_i, core_i, sem.at[0, i], sem.at[1, i], device(z, y, x, 1 - c)).wait_recv()
        pltpu.make_async_copy(own_i, own_i, sem.at[2, i]).wait()

        @pl.loop(0, NZ)
        def _(zz):
            for yy in range(2):
                for xx in range(2):
                    core_i[zz, yy, xx] = core_i[zz, yy, xx] + own_i[zz, yy, xx]

        if x_goes_first(i):
            src, to = core_i.at[:, :, 1 - x], device(z, y, 1 - x, c)
        else:
            src, to = core_i.at[:, 1 - y], device(z, 1 - y, x, c)
        go = remote(src, view(i, 2), sem.at[3, i], sem.at[4, i], to)
        go.start()
        sent.append(go)

    def after_first(i):
        core_i, first_i = view(i, 1), view(i, 2)
        remote(first_i, first_i, sem.at[3, i], sem.at[4, i], device(z, y, x, 1 - c)).wait_recv()

        @pl.loop(0, NZ)
        def _(zz):
            for o in range(2):
                mine = core_i[zz, o, x] if x_goes_first(i) else core_i[zz, y, o]
                first_i[zz, o] = first_i[zz, o] + mine

        if x_goes_first(i):
            src, to = first_i.at[:, 1 - y], device(z, 1 - y, x, c)
        else:
            src, to = first_i.at[:, 1 - x], device(z, y, 1 - x, c)
        go = remote(src, view(i, 3), sem.at[5, i], sem.at[6, i], to)
        go.start()
        sent.append(go)

    def after_second(i):
        first_i, second_i, last_i = view(i, 2), view(i, 3), view(i, 4)
        remote(second_i, second_i, sem.at[5, i], sem.at[6, i], device(z, y, x, 1 - c)).wait_recv()

        @pl.loop(0, NZ)
        def _(zz):
            second_i[zz] = second_i[zz] + (first_i[zz, y] if x_goes_first(i) else first_i[zz, x])

        for d in range(1, NZ):
            zz = lax.rem(z + d, NZ)
            go = remote(second_i.at[zz], last_i.at[z], semz.at[0, d, i], semz.at[1, d, i], device(zz, y, x, c))
            go.start()
            sent.append(go)
        last_i[z] = second_i[z]

    def after_last(i):
        last_i = view(i, 4)
        for d in range(1, NZ):
            zz = lax.rem(z + NZ - d, NZ)
            remote(last_i.at[zz], last_i.at[zz], semz.at[0, d, i], semz.at[1, d, i], device(z, y, x, 1 - c)).wait_recv()
        value = last_i[0].astype(f32)
        for zz in range(1, NZ):
            value = value + last_i[zz].astype(f32)
        if i == total - 1:
            outs[n][...] = value
        else:
            a, (r, k, w) = pieces[i]
            outs[a][r : r + CUT_ROWS, k : k + w] = value

    order = [total - 1] + list(range(total - 1))
    for i in order:
        begin(i)
    stages = (after_core, after_first, after_second, after_last)
    for t in range(total + lead[-1]):
        for stage, skew in reversed(list(zip(stages, lead))):
            if 0 <= t - skew < total:
                stage(order[t - skew])
    for go in sent:
        go.wait_send()


def reduce_all(arrays, small, lead=(0, 4, 6, 8)):
    n = len(arrays)
    arrays = [v.reshape((NZ, 2, 2, 2, -1, v.shape[-1])) for v in arrays]
    small = small.reshape((NZ, 2, 2, 2, -1, small.shape[-1]))
    p = sum(len(cuts_of(v.shape)) for v in arrays)
    ss = small.shape[-2:]
    made = [jax.ShapeDtypeStruct(v.shape[-2:], f32) for v in arrays + [small]]
    dims = [(NZ, 2, 2), (NZ, 2, 2), (NZ, 2), (NZ,), (NZ,)]
    return pl.pallas_call(
        partial(reduce_kernel, n, tuple(lead)),
        out_shape=made,
        in_specs=[pl.BlockSpec(memory_space=pl.ANY)] * (n + 1),
        out_specs=[pl.BlockSpec(memory_space=pltpu.VMEM)] * (n + 1),
        scratch_shapes=[pltpu.VMEM((p,) + d + (CUT_ROWS, CUT), bf16) for d in dims]
        + [pltpu.VMEM(d + ss, f32) for d in dims]
        + [pltpu.SemaphoreType.DMA((7, p + 1)), pltpu.SemaphoreType.DMA((2, NZ, p + 1))],
        compiler_params=pltpu.CompilerParams(collective_id=1, has_side_effects=True, vmem_limit_bytes=VMEM),
    )(*arrays, small)


def local(tokens, norm_gain, input_weight, conv_w, conv_b, dt_bias, a_log, d_skip, gate_gain,
          output_weight, segments, cotangent):
    seqs, length, width = tokens.shape
    n_ctx = lax.axis_size("ctx")
    n_all = n_ctx * lax.axis_size("seq")
    count = seqs * length
    shares = [norm_gain.shape[0], gate_gain.shape[0], CONV * conv_b.shape[0], conv_b.shape[0]]
    cuts = [sum(shares[: i + 1]) for i in range(3)]
    packed = jnp.concatenate([norm_gain, gate_gain, conv_w.reshape(-1), conv_b])
    onward = [(i, i + 1) for i in range(n_ctx - 1)]
    tail = jnp.pad(tokens[:, length - (CONV - 1) :], ((0, 0), (8 - (CONV - 1), 0), (0, 0)))
    tail_ids = jnp.pad(
        segments[:, length - (CONV - 1) :].astype(bf16), ((0, 0), (0, width - (CONV - 1)))
    )
    tail = jnp.concatenate([tail_ids[:, None], tail[:, 1:]], axis=1).reshape(seqs * 8, width)
    torus = lax.axis_size("seq") == 2 * NZ and n_ctx == 4 and norm_gain.shape[0] == CUT_ROWS
    w_z, w_x = input_weight[:, :INNER], input_weight[:, INNER:]
    if torus:
        size = packed.shape[0]
        small = jnp.pad(packed, (0, 16 * LANES - size)).reshape(16, LANES)
        w_out = lax.all_gather(output_weight, BOTH, axis=0, tiled=True)
        w_z = lax.all_gather(w_z, BOTH, axis=0, tiled=True)
        w_x, packed, tail = gather_all(
            [w_x, small], tail,
            [(1, 0, 16, True)]
            + [(0, 16 * k, 16, k % 2 == 0) for k in range(3)]
,
        )
        w_x, w_z, w_out = (w.reshape(-1, w.shape[-1]) for w in (w_x, w_z, w_out))
        packed = packed.reshape(n_all, -1)[:, :size]
    else:
        packed = lax.all_gather(packed, BOTH, axis=0)
        tail = lax.ppermute(tail, "ctx", onward)
        w_in, w_out = (
            lax.all_gather(w, BOTH, axis=0, tiled=True) for w in (input_weight, output_weight)
        )
        w_z, w_x = w_in[:, :INNER], w_in[:, INNER:]
    norm_full, gate_full, conv_w_full, conv_b_full = jnp.split(packed.astype(f32), cuts, axis=1)
    norm_full = norm_full.reshape(1, -1)
    gate_full = gate_full.reshape(1, -1)
    conv_b_full = conv_b_full.reshape(1, -1)
    conv_w_full = conv_w_full.reshape(n_all, CONV, -1).transpose(1, 0, 2).reshape(CONV, -1)

    tail = tail.reshape(seqs, 8, width)
    tail_ids = jnp.where(
        lax.axis_index("ctx") == 0, -1, tail[:, 0, : CONV - 1].astype(jnp.int32)
    )
    tail = jnp.pad(tail[:, 8 - (CONV - 1) :], ((0, 0), (8 - (CONV - 1), 0), (0, 0)))
    tail = jnp.where(lax.axis_index("ctx") == 0, 0, tail)
    x_all = jnp.concatenate([tokens.reshape(count, width), tail.reshape(seqs * 8, width)])
    x_all = x_all.astype(f32)
    r_all = lax.rsqrt(jnp.mean(x_all * x_all, axis=-1, keepdims=True) + EPSILON)
    normed = (x_all * r_all * norm_full).astype(bf16)

    ids_ext = jnp.concatenate([tail_ids, segments], axis=1)
    flags = [
        segments == ids_ext[:, CONV - 1 - k : CONV - 1 - k + length] for k in range(1, CONV)
    ] + [segments == ids_ext[:, CONV - 2 : CONV - 1], segments == segments[:, -1:]]
    cols = jnp.stack([f.astype(f32) for f in flags] + [segments.astype(f32)], axis=-1)
    cols = jnp.pad(cols, ((0, 0), (0, 0), (0, LANES - cols.shape[-1])))
    rows = jnp.pad(segments.astype(f32)[:, None], ((0, 0), (0, 7), (0, 0)))
    heads = jnp.pad(jnp.stack([pad_lanes(dt_bias), pad_lanes(a_log)]), ((0, 6), (0, 0)))
    lanes = jnp.concatenate([gate_full, jnp.repeat(d_skip, HEADDIM)[None]])
    lanes = jnp.pad(lanes, ((0, 6), (0, 0)))
    conv_w8 = jnp.pad(conv_w_full, ((0, 8 - CONV), (0, 0)))
    conv_b8 = jnp.pad(conv_b_full, ((0, 7), (0, 0)))

    px = MM(normed, w_x).astype(bf16)
    px_width, dpx_width = CHANNELS + HEADS, CHANNELS + LANES
    tail_spec = pl.BlockSpec((16, px_width), lambda s: (count // 16, 0))
    act, tok, cst, fresh = call(
        before_kernel, seqs,
        [per_rows(length, px_width), tail_spec, whole((8, CHANNELS)), whole((8, CHANNELS)),
         per_seq(length, LANES), whole((8, LANES))],
        [(per_seq(length, CHANNELS), ((seqs, length, CHANNELS), f32)),
         (per_seq(length, 2 * LANES), ((seqs, length, 2 * LANES), f32)),
         (per_seq(HEADS, length), ((seqs, HEADS, length), f32)),
         (per_seq(INNER, STATE), ((seqs, INNER, STATE), f32))],
        [pltpu.VMEM((length + 8, LANES), f32)],
        px, px, conv_w8, conv_b8, cols, heads,
    )
    carried = cols[:, length - 1, 3]
    kept = jnp.exp(cst[:, :, length - 1]) * carried[:, None]
    kept = jnp.repeat(kept, HEADDIM, axis=1)[..., None]
    g2 = cotangent.reshape(count, width)

    def gate_gradient():
        return lax.dot_general(g2, w_out, (((1,), (1,)), ((), ())), preferred_element_type=f32)

    def within():
        [y] = call(
            within_kernel, seqs,
            [per_seq(length, CHANNELS), per_seq(length, 2 * LANES), per_seq(HEADS, length),
             per_seq(length, LANES), per_seq(8, length)],
            [(per_seq(length, INNER), ((seqs, length, INNER), f32))],
            [pltpu.VMEM((length, length), f32), pltpu.VMEM((length, length), f32)],
            act, tok, cst, cols, rows,
        )
        return y

    def gates():
        return MM(normed[:count], w_z).astype(bf16)

    entering, (dgn, y, pz) = chain(fresh, kept, onward, (gate_gradient, within, gates))
    stayed = kept * entering.astype(f32)
    gn, dz, dy, dstate, dqueries, ddecay, sums = call(
        gate_kernel, seqs,
        [per_rows(length, INNER), per_seq(length, CHANNELS), per_seq(length, 2 * LANES),
         per_seq(length, LANES), per_seq(length, INNER), per_seq(INNER, STATE),
         per_rows(length, INNER), whole((8, INNER))],
        [(per_rows(length, INNER), ((count, INNER), bf16)),
         (per_rows(length, INNER), ((count, INNER), bf16)),
         (per_seq(length, INNER), ((seqs, length, INNER), bf16)),
         (per_seq(INNER, STATE), ((seqs, INNER, STATE), f32)),
         (per_seq(length, STATE), ((seqs, length, STATE), f32)),
         (per_seq(length, LANES), ((seqs, length, LANES), f32)),
         (per_seq(8, INNER), ((seqs, 8, INNER), f32))],
        [pltpu.VMEM((length, INNER), f32), pltpu.VMEM((length, STATE), f32)],
        pz, act, tok, cols, y, entering, dgn, lanes,
    )
    tn = (((0,), (0,)), ((), ()))

    def products():
        out = (x_all[:count] + MM(gn, w_out)).astype(bf16)
        return out, lax.dot_general(gn, g2, tn, preferred_element_type=f32).astype(bf16)

    def scan_back():
        return call(
            scan_back_kernel, seqs,
            [per_seq(length, CHANNELS), per_seq(length, 2 * LANES), per_seq(HEADS, length),
             per_seq(length, LANES), per_seq(8, length), per_seq(length, INNER)],
            [(per_seq(length, INNER), ((seqs, length, INNER), f32)),
             (per_seq(length, 2 * STATE), ((seqs, length, 2 * STATE), f32))],
            [pltpu.VMEM((length, length), f32)] * 3,
            act, tok, cst, cols, rows, dy,
        )

    def gate_weights():
        return lax.dot_general(normed[:count], dz, tn, preferred_element_type=f32).astype(bf16)

    later, ((output, dw_out), (dx, dbc), dw_z) = chain(
        dstate, kept, [(b, a) for a, b in reversed(onward)], (products, scan_back, gate_weights)
    )
    dpx, edge, dconv, dheads = call(
        after_kernel, seqs,
        [per_rows(length, px_width), tail_spec, whole((8, CHANNELS)), whole((8, CHANNELS)),
         per_seq(length, LANES), whole((8, LANES)), per_seq(length, CHANNELS),
         per_seq(length, 2 * LANES), whole((8, INNER)), per_seq(length, INNER),
         per_seq(length, INNER), per_seq(length, 2 * STATE), per_seq(length, STATE),
         per_seq(length, LANES), per_seq(INNER, STATE), per_seq(INNER, STATE)],
        [(per_rows(length, dpx_width), ((count, dpx_width), bf16)),
         (per_seq(8, dpx_width), ((seqs, 8, dpx_width), f32)),
         (per_seq(8, CHANNELS), ((seqs, 8, CHANNELS), f32)),
         (per_seq(8, LANES), ((seqs, 8, LANES), f32))],
        [pltpu.VMEM((length + 8, LANES), f32), pltpu.VMEM((CONV - 1, length + 16, LANES), f32),
         pltpu.VMEM((length, CHANNELS), f32), pltpu.VMEM((length, LANES), f32),
         pltpu.VMEM((length, LANES), f32), pltpu.VMEM((length, STATE), f32), pltpu.VMEM((LANES, LANES), f32),
         pltpu.VMEM((8, INNER), f32)],
        px, px, conv_w8, conv_b8, cols, heads, act, tok, lanes, dy, dx, dbc, dqueries, ddecay,
        later, stayed,
    )
    dpx_all = jnp.concatenate([dpx, edge.reshape(seqs * 8, dpx_width).astype(bf16)])
    nt = (((1,), (1,)), ((), ()))
    dnormed_x = lax.dot_general(dpx_all[:, :px_width], w_x, nt, preferred_element_type=f32)
    dnormed = dnormed_x[:count] + lax.dot_general(dz, w_z, nt, preferred_element_type=f32)
    back = dnormed_x[count:].reshape(seqs, 8, width)[:, 8 - (CONV - 1) :].astype(bf16)
    back = lax.ppermute(back, "ctx", [(b, a) for a, b in onward])
    dw_x = lax.dot_general(normed, dpx_all, tn, preferred_element_type=f32).astype(bf16)
    x, r = x_all[:count], r_all[:count]
    d_gain = jnp.sum(x * r * dnormed, axis=0) + jnp.sum(
        x_all[count:] * r_all[count:] * dnormed_x[count:], axis=0
    )
    back, d_gain, dw_x = lax.optimization_barrier((back, d_gain, dw_x))
    back = jnp.pad(back.astype(f32), ((0, 0), (length - (CONV - 1), 0), (0, 0)))
    scaled = norm_full * (dnormed + back.reshape(count, width))
    dx_in = r * (scaled - x * (r * r) * jnp.mean(x * scaled, axis=-1, keepdims=True))
    input_grad = (g2.astype(f32) + dx_in).astype(bf16)

    sums = jnp.sum(sums, axis=0)
    dconv = jnp.sum(dconv, axis=0)
    dheads = jnp.sum(dheads, axis=0)
    d_skip_sum = jnp.sum(sums[1].reshape(HEADS, HEADDIM), axis=1)
    split = [d_gain.reshape(n_all, -1), sums[0].reshape(n_all, -1),
             dconv[:CONV].reshape(CONV, n_all, -1).transpose(1, 0, 2).reshape(n_all, -1),
             dconv[CONV].reshape(n_all, -1)]
    shared = jnp.concatenate([dheads[0, :HEADS], dheads[1, :HEADS], d_skip_sum])
    split = jnp.concatenate(split, axis=1)
    share = sum(shares)
    if torus:
        fill = 8 * LANES - share - shared.shape[0]
        split = [split, jnp.broadcast_to(shared, (n_all,) + shared.shape), jnp.zeros((n_all, fill), f32)]
        dw_out = lax.psum_scatter(dw_out, BOTH, scatter_dimension=0, tiled=True).astype(f32)
        dw_z, dw_x, mine = reduce_all(
            [dw_z, dw_x],
            jnp.concatenate(split, axis=1).reshape(n_all, 8, LANES),
        )
        dw_in = jnp.concatenate([dw_z, dw_x[:, :px_width]], axis=1)
        mine = mine.reshape(-1)
        mine, shared = mine[:share], mine[share : share + shared.shape[0]]
    else:
        dw_in = jnp.concatenate([dw_z, dw_x[:, :px_width]], axis=1)
        dw_out, dw_in = (
            lax.psum_scatter(v.astype(f32), BOTH, scatter_dimension=0, tiled=True)
            for v in (dw_out, dw_in)
        )
        every = lax.psum(jnp.concatenate([split.reshape(-1), shared]), BOTH)
        me = lax.axis_index("seq") * n_ctx + lax.axis_index("ctx")
        mine, shared = lax.dynamic_slice(every, (me * share,), (share,)), every[n_all * share :]
    d_norm, d_gate, d_conv_w, d_conv_b = jnp.split(mine, cuts)
    d_bias, d_alog, d_skips = jnp.split(shared, 3)
    return (
        output.reshape(tokens.shape), input_grad.reshape(tokens.shape), d_norm, dw_in,
        d_conv_w.reshape(CONV, -1), d_conv_b, d_bias, d_alog, d_skips, d_gate, dw_out,
    )


def solution(mesh):
    split = P(BOTH)
    rows = P(BOTH, None)
    seq = P("seq", "ctx", None)
    in_specs = (seq, split, rows, P(None, BOTH), split, P(), P(), P(), split, rows,
                P("seq", "ctx"), seq)
    out_specs = (seq, seq, split, rows, P(None, BOTH), split, P(), P(), P(), split, rows)
    return jax.shard_map(local, mesh=mesh, in_specs=in_specs, out_specs=out_specs, check_vma=False)
```

```python
from functools import partial

import jax
import jax.numpy as jnp
from jax import lax
from jax.experimental import pallas as pl
from jax.experimental.pallas import tpu as pltpu
from jax.sharding import PartitionSpec as P

HEADS = 48
STATE = 128
HEADDIM = 64
CONV = 4
INNER = HEADS * HEADDIM
CHANNELS = INNER + 2 * STATE
GROUP = 8
GROUPS = HEADS // GROUP
WIDTH = GROUP * HEADDIM
LANES = 128
EPSILON = 1e-05
VMEM = 60 * 1024 * 1024
FINISH_VMEM = 62 * 1024 * 1024 - 512 * 1024
BOTH = ("seq", "ctx")
FAR = -1e30
f32 = jnp.float32
bf16 = jnp.bfloat16
MM = partial(jnp.dot, preferred_element_type=f32)


def mm_nt(a, b):
    return lax.dot_general(a, b, (((1,), (1,)), ((), ())), preferred_element_type=f32)


def mm_tn(a, b):
    return lax.dot_general(a, b, (((0,), (0,)), ((), ())), preferred_element_type=f32)


def at(j, width):
    return pl.ds(pl.multiple_of(j * width, width), width)


def low_half(rows):
    return lax.broadcasted_iota(jnp.int32, (rows, LANES), 1) < HEADDIM


def to_front(columns, g):
    return pltpu.roll(columns, lax.rem(LANES - GROUP * g, LANES), 1)


def spread(front, pair, low):
    return jnp.where(low, front[:, 2 * pair : 2 * pair + 1], front[:, 2 * pair + 1 : 2 * pair + 2])


def head_sums(product, g):
    lane = lax.broadcasted_iota(jnp.int32, (WIDTH, LANES), 1)
    row = lax.broadcasted_iota(jnp.int32, (WIDTH, LANES), 0)
    pick = jnp.where(lane == GROUP * g + row // HEADDIM, 1.0, 0.0).astype(bf16)
    high = product.astype(bf16)
    rest = (product - high.astype(f32)).astype(bf16)
    return MM(high, pick) + MM(rest, pick)


def taps(px_ref, tail, j, w_ref, b_ref, masks, ext):
    here = at(j, LANES)
    length = px_ref.shape[0]
    own = px_ref[:, here].astype(f32)
    ext[0:8, :] = tail
    ext[8 : 8 + length, :] = own
    inputs = [own] + [
        masks[k - 1] * ext[8 - k : 8 - k + length, :] for k in range(1, CONV)
    ]
    out = b_ref[0:1, here]
    for k in range(CONV):
        out = out + w_ref[k : k + 1, here] * inputs[k]
    return out, inputs


def tail_of(tail_ref, s, here):
    both = tail_ref[:, here].astype(f32)
    return jnp.where(s == 0, both[0:8], both[8:16])


def lane_masks(cols_ref, length):
    return [
        jnp.broadcast_to(cols_ref[0, :, k : k + 1], (length, LANES)) for k in range(CONV - 1)
    ]


def before_kernel(px_ref, tail_ref, w_ref, b_ref, cols_ref, heads_ref,
                  act_ref, tok_ref, cst_ref, fresh_ref, ext):
    s = pl.program_id(0)
    length = px_ref.shape[0]
    masks = lane_masks(cols_ref, length)

    @pl.loop(0, CHANNELS // LANES)
    def _(j):
        here = at(j, LANES)
        conv, _unused = taps(px_ref, tail_of(tail_ref, s, here), j, w_ref, b_ref, masks, ext)
        act_ref[0, :, here] = conv * jax.nn.sigmoid(conv)

    raw = px_ref[:, CHANNELS : CHANNELS + HEADS].astype(f32) + heads_ref[0:1, :HEADS]
    step = jnp.maximum(raw, 0.0) + jnp.log1p(jnp.exp(-jnp.abs(raw)))
    step = jnp.concatenate([step, jnp.zeros((length, LANES - HEADS), f32)], axis=1)
    rate = -step * jnp.exp(heads_ref[1:2, :])
    before = (
        lax.broadcasted_iota(jnp.int32, (length, length), 0)
        >= lax.broadcasted_iota(jnp.int32, (length, length), 1)
    ).astype(f32)
    decay = jnp.dot(before, rate, precision=lax.Precision.HIGHEST, preferred_element_type=f32)
    tok_ref[0, :, 0:LANES] = step
    tok_ref[0, :, LANES : 2 * LANES] = decay
    cst_ref[0] = decay.T[:HEADS]
    toward = jnp.exp(decay[length - 1 : length] - decay) * step * cols_ref[0, :, 4:5]
    keys = act_ref[0, :, INNER : INNER + STATE].astype(bf16)
    low = low_half(length)

    @pl.loop(0, GROUPS)
    def _(g):
        front = to_front(toward, g)
        for pair in range(GROUP // 2):
            here = pl.ds(pl.multiple_of(g * WIDTH + pair * LANES, LANES), LANES)
            scaled = (act_ref[0, :, here] * spread(front, pair, low)).astype(bf16)
            fresh_ref[0, here, :] = mm_tn(scaled, keys)


def bias_of(ids_col, ids_row, transposed):
    shape = (ids_col.shape[0], ids_row.shape[1])
    down = lax.broadcasted_iota(jnp.int32, shape, 0)
    across = lax.broadcasted_iota(jnp.int32, shape, 1)
    order = (down <= across) if transposed else (down >= across)
    return jnp.where(order & (ids_col == ids_row), 0.0, FAR)


def within_kernel(act_ref, tok_ref, cst_ref, cols_ref, rows_ref, y_ref, cross, bias):
    length = act_ref.shape[1]
    half = length // 2
    cross[...] = mm_nt(
        act_ref[0, :, INNER + STATE :].astype(bf16),
        act_ref[0, :, INNER : INNER + STATE].astype(bf16),
    )
    bias[...] = bias_of(cols_ref[0, :, 5:6], rows_ref[0, 0:1, :], False)
    low = low_half(length)

    @pl.loop(0, GROUPS)
    def _(g):
        step = to_front(tok_ref[0, :, 0:LANES], g)
        decay = to_front(tok_ref[0, :, LANES : 2 * LANES], g)
        rows = cst_ref[0, at(g, GROUP), :]
        for pair in range(GROUP // 2):
            here = pl.ds(pl.multiple_of(g * WIDTH + pair * LANES, LANES), LANES)
            scaled = act_ref[0, :, here] * spread(step, pair, low)
            top, bottom = 0.0, 0.0
            for which in range(2):
                h = 2 * pair + which
                mine = jnp.where(low == (which == 0), scaled, 0.0).astype(bf16)
                col, row = decay[:, h : h + 1], rows[h : h + 1, :]
                w = jnp.exp(col[:half] - row[:, :half] + bias[:half, :half])
                top = top + MM((cross[:half, :half] * w).astype(bf16), mine[:half])
                w = jnp.exp(col[half:] - row + bias[half:, :])
                bottom = bottom + MM((cross[half:, :] * w).astype(bf16), mine)
            y_ref[0, :half, here] = top
            y_ref[0, half:, here] = bottom


def gate_kernel(z_ref, act_ref, tok_ref, cols_ref, y_ref, state_ref, dgn_ref, lanes_ref,
                gn_ref, dz_ref, dy_ref, dstate_ref, q_ref, dq_ref, sums_ref, total, queries_acc):
    length = act_ref.shape[1]
    low = low_half(length)
    enter = jnp.exp(tok_ref[0, :, LANES : 2 * LANES]) * cols_ref[0, :, 3:4]
    queries = act_ref[0, :, INNER + STATE :].astype(bf16)

    def first(g, carry):
        square, inner = carry
        front = to_front(enter, g)
        for pair in range(GROUP // 2):
            here = pl.ds(pl.multiple_of(g * WIDTH + pair * LANES, LANES), LANES)
            far = mm_nt(queries, state_ref[0, here, :])
            y = y_ref[0, :, here] + spread(front, pair, low) * far
            total[:, here] = y
            y = y + lanes_ref[1:2, here] * act_ref[0, :, here]
            z = z_ref[:, here].astype(f32)
            gated = y * (z * jax.nn.sigmoid(z))
            square = square + gated * gated
            inner = inner + lanes_ref[0:1, here] * dgn_ref[:, here] * gated
        return square, inner

    zero = jnp.zeros((length, LANES), f32)
    square, inner = lax.fori_loop(0, GROUPS, first, (zero, zero))
    scale = lax.rsqrt(jnp.sum(square, axis=1, keepdims=True) * (1.0 / INNER) + EPSILON)
    back = scale * scale * scale * (jnp.sum(inner, axis=1, keepdims=True) * (1.0 / INNER))
    scale = jnp.broadcast_to(scale, (length, LANES))
    back = jnp.broadcast_to(back, (length, LANES))
    queries_acc[...] = jnp.zeros_like(queries_acc)
    dq_ref[0] = jnp.zeros_like(dq_ref[0])

    @pl.loop(0, GROUPS)
    def _(g):
        front = to_front(enter, g)
        products = []
        for pair in range(GROUP // 2):
            here = pl.ds(pl.multiple_of(g * WIDTH + pair * LANES, LANES), LANES)
            xs = act_ref[0, :, here]
            inside = total[:, here]
            y = inside + lanes_ref[1:2, here] * xs
            z = z_ref[:, here].astype(f32)
            sg = jax.nn.sigmoid(z)
            gate = z * sg
            gated = y * gate
            gain = lanes_ref[0:1, here]
            dgn = dgn_ref[:, here]
            gn = gated * scale
            gn_ref[:, here] = (gn * gain).astype(bf16)
            dgated = scale * (gain * dgn) - gated * back
            dy = dgated * gate
            dz_ref[:, here] = (dgated * y * (sg * (1.0 + z * (1.0 - sg)))).astype(bf16)
            rounded = dy.astype(bf16)
            dy_ref[0, :, here] = rounded
            sums_ref[0, 0:1, here] = jnp.sum(dgn * gn, axis=0, keepdims=True)
            sums_ref[0, 1:2, here] = jnp.sum(dy * xs, axis=0, keepdims=True)
            entered = (rounded.astype(f32) * spread(front, pair, low)).astype(bf16)
            dstate_ref[0, here, :] = mm_tn(entered, queries)
            queries_acc[...] += MM(entered, state_ref[0, here, :])
            products.append(rounded.astype(f32) * inside)
        dq_ref[0] += head_sums(jnp.concatenate(products, axis=1), g)

    q_ref[0] = queries_acc[...]


def scan_back_kernel(act_ref, tok_ref, cst_ref, cols_ref, rows_ref, dy_ref,
                     dx_ref, dbc_ref, cross, bias, dcross):
    length = act_ref.shape[1]
    half = length // 2
    keys = act_ref[0, :, INNER : INNER + STATE].astype(bf16)
    queries = act_ref[0, :, INNER + STATE :].astype(bf16)
    cross[...] = mm_nt(keys, queries)
    bias[...] = bias_of(cols_ref[0, :, 5:6], rows_ref[0, 0:1, :], True)
    dcross[...] = jnp.zeros_like(dcross)
    low = low_half(length)

    @pl.loop(0, GROUPS)
    def _(g):
        step = to_front(tok_ref[0, :, 0:LANES], g)
        decay = to_front(tok_ref[0, :, LANES : 2 * LANES], g)
        rows = cst_ref[0, at(g, GROUP), :]
        for pair in range(GROUP // 2):
            here = pl.ds(pl.multiple_of(g * WIDTH + pair * LANES, LANES), LANES)
            scaled = (act_ref[0, :, here] * spread(step, pair, low)).astype(bf16)
            dy = dy_ref[0, :, here].astype(f32)
            top, bottom = 0.0, 0.0
            for which in range(2):
                h = 2 * pair + which
                mine = jnp.where(low == (which == 0), dy, 0.0).astype(bf16)
                col, row = decay[:, h : h + 1], rows[h : h + 1, :]
                w = jnp.exp(row - col[:half] + bias[:half, :])
                dcross[:half, :] += mm_nt(scaled[:half], mine) * w
                top = top + MM((cross[:half, :] * w).astype(bf16), mine)
                w = jnp.exp(row[:, half:] - col[half:] + bias[half:, half:])
                dcross[half:, half:] += mm_nt(scaled[half:], mine[half:]) * w
                bottom = bottom + MM((cross[half:, half:] * w).astype(bf16), mine[half:])
            dx_ref[0, :half, here] = top
            dx_ref[0, half:, here] = bottom

    d = dcross[...].astype(bf16)
    dbc_ref[0, :, :STATE] = MM(d, queries)
    dbc_ref[0, :, STATE:] = mm_tn(d, keys)


def after_kernel(px_ref, tail_ref, w_ref, b_ref, cols_ref, heads_ref, act_ref, tok_ref, lanes_ref,
                 dy_ref, dx_ref, dbc_ref, q_ref, dq_ref, later_ref, kept_ref,
                 dpx_ref, edge_ref, dconv_ref, dheads_ref, ext, moved, grad, dstep_acc, dcol_acc, keys_acc, ends, sent):
    s = pl.program_id(0)
    length = act_ref.shape[1]
    low = low_half(length)
    step = tok_ref[0, :, 0:LANES]
    decay = tok_ref[0, :, LANES : 2 * LANES]
    leave = jnp.exp(decay[length - 1 : length] - decay) * cols_ref[0, :, 4:5]
    keys = act_ref[0, :, INNER : INNER + STATE].astype(bf16)
    dstep_acc[...] = jnp.zeros_like(dstep_acc)
    dcol_acc[...] = jnp.zeros_like(dcol_acc)
    sent[...] = jnp.zeros_like(sent)
    keys_acc[...] = dbc_ref[0, :, :STATE]
    ends[...] = jnp.zeros_like(ends)

    @pl.loop(0, GROUPS)
    def _(g):
        step_front, leave_front = to_front(step, g), to_front(leave, g)
        products, columns = [], []
        for pair in range(GROUP // 2):
            here = pl.ds(pl.multiple_of(g * WIDTH + pair * LANES, LANES), LANES)
            later = later_ref[0, here, :]
            xs = act_ref[0, :, here]
            steps = spread(step_front, pair, low)
            leaving = spread(leave_front, pair, low)
            through = leaving * mm_nt(keys, later)
            dscaled = dx_ref[0, :, here] + through
            scaled = steps * xs
            rounded = scaled.astype(bf16).astype(f32)
            keys_acc[...] += MM((leaving * scaled).astype(bf16), later)
            products.append(xs * dscaled)
            columns.append(rounded * dscaled)
            sent[0:1, here] = jnp.sum(rounded * through, axis=0, keepdims=True)
            grad[:, here] = steps * dscaled + lanes_ref[1:2, here] * dy_ref[0, :, here].astype(f32)
            both = later.astype(f32) * kept_ref[0, here, :]
            at_row = GROUP * g + 2 * pair
            ends[pl.ds(at_row, 1), :] = jnp.sum(both[:HEADDIM], axis=0, keepdims=True)
            ends[pl.ds(at_row + 1, 1), :] = jnp.sum(both[HEADDIM:], axis=0, keepdims=True)
        dstep_acc[...] += head_sums(jnp.concatenate(products, axis=1), g)
        dcol_acc[...] += head_sums(jnp.concatenate(columns, axis=1), g)

    grad[:, INNER : INNER + STATE] = keys_acc[...]
    grad[:, INNER + STATE :] = dbc_ref[0, :, STATE:] + q_ref[0]
    dstep = dstep_acc[...]
    at_end = jnp.sum(ends[...].T, axis=0, keepdims=True)
    for g in range(GROUPS):
        at_end = at_end + head_sums(sent[:, g * WIDTH : (g + 1) * WIDTH], g)[0:1]
    row = lax.broadcasted_iota(jnp.int32, (length, LANES), 0)
    ddecay = dq_ref[0] - dcol_acc[...] + jnp.where(row == length - 1, at_end, 0.0)
    onward = (
        lax.broadcasted_iota(jnp.int32, (length, length), 0)
        <= lax.broadcasted_iota(jnp.int32, (length, length), 1)
    ).astype(f32)
    drate = jnp.dot(onward, ddecay, precision=lax.Precision.HIGHEST, preferred_element_type=f32)
    speed = jnp.exp(heads_ref[1:2, :])
    raw = px_ref[:, CHANNELS : CHANNELS + HEADS].astype(f32) + heads_ref[0:1, :HEADS]
    draw = (dstep - drate * speed)[:, :HEADS] * jax.nn.sigmoid(raw)
    dpx_ref[:, CHANNELS:] = jnp.concatenate(
        [draw, jnp.zeros((length, LANES - HEADS), f32)], axis=1
    ).astype(bf16)
    edge_ref[0, :, CHANNELS:] = jnp.zeros((8, LANES), f32)
    dheads_ref[0] = jnp.zeros((8, LANES), f32)
    dheads_ref[0, 0:1, :HEADS] = jnp.sum(draw, axis=0, keepdims=True)
    dheads_ref[0, 1:2, :] = jnp.sum(drate * (-step * speed), axis=0, keepdims=True)

    masks = lane_masks(cols_ref, length)
    moved[...] = jnp.zeros_like(moved)
    dconv_ref[0] = jnp.zeros((8, CHANNELS), f32)

    @pl.loop(0, CHANNELS // LANES)
    def _(j):
        here = at(j, LANES)
        conv, inputs = taps(px_ref, tail_of(tail_ref, s, here), j, w_ref, b_ref, masks, ext)
        sg = jax.nn.sigmoid(conv)
        dconv = grad[:, here] * (sg * (1.0 + conv * (1.0 - sg)))
        for k in range(CONV):
            dconv_ref[0, k : k + 1, here] = jnp.sum(dconv * inputs[k], axis=0, keepdims=True)
        dconv_ref[0, CONV : CONV + 1, here] = jnp.sum(dconv, axis=0, keepdims=True)
        dx = w_ref[0:1, here] * dconv
        edge = jnp.zeros((8, LANES), f32)
        for k in range(1, CONV):
            moved[k - 1, 8 : 8 + length, :] = dconv * masks[k - 1]
            dx = dx + w_ref[k : k + 1, here] * moved[k - 1, 8 + k : 8 + k + length, :]
            edge = edge + w_ref[k : k + 1, here] * moved[k - 1, k : 8 + k, :]
        dpx_ref[:, here] = dx.astype(bf16)
        edge_ref[0, :, here] = edge


def whole(shape):
    return pl.BlockSpec(shape, lambda s: (0,) * len(shape))


def per_seq(*tail):
    return pl.BlockSpec((1,) + tail, lambda s: (s,) + (0,) * len(tail))


def per_rows(rows, width):
    return pl.BlockSpec((rows, width), lambda s: (s, 0))


def call(kernel, count, in_specs, outs, scratch, *args):
    return pl.pallas_call(
        kernel,
        grid=(count,),
        in_specs=in_specs,
        out_specs=[spec for spec, _unused in outs],
        out_shape=[jax.ShapeDtypeStruct(*made) for _unused, made in outs],
        scratch_shapes=scratch,
        compiler_params=pltpu.CompilerParams(vmem_limit_bytes=VMEM),
    )(*args)


def chain(own, factor, steps, beside):
    entered = jnp.zeros(own.shape, bf16)
    results = []
    for k, (source, target) in enumerate(steps):
        sent = own.astype(bf16) if k == 0 else (own + factor * entered.astype(f32)).astype(bf16)
        came = lax.ppermute(sent, "ctx", [(source, target)])
        for work in beside[k :: len(steps)]:
            results.append(work())
            came, results[-1] = lax.optimization_barrier((came, results[-1]))
        entered = came if k == 0 else entered + came
    return entered, results


def pad_lanes(v):
    return jnp.pad(v, (0, LANES - v.shape[0]))


NZ = 4


def place():
    seq, ctx = lax.axis_index("seq"), lax.axis_index("ctx")
    return seq // 2, lax.rem(seq, 2), ctx // 2, lax.rem(ctx, 2)


def device(z, y, x, c):
    return {"seq": z * 2 + y, "ctx": x * 2 + c}


def greet(z, y, x, c, more=0):
    barrier = pltpu.get_barrier_semaphore()
    others = [device(z, y, x, 1 - c), device(z, y, 1 - x, c), device(z, 1 - y, x, c)]
    others += [device(lax.rem(z + d, NZ), y, x, c) for d in range(1, NZ)]
    for other in others:
        pl.semaphore_signal(barrier, inc=1, device_id=other, device_id_type=pl.DeviceIdType.MESH)
    pl.semaphore_wait(barrier, len(others) + more)


def remote(src, dst, send, recv, target):
    return pltpu.make_async_remote_copy(
        src_ref=src, dst_ref=dst, send_sem=send, recv_sem=recv, device_id=target,
        device_id_type=pl.DeviceIdType.MESH,
    )


def gather_kernel(units, n, *refs):
    ins, outs, land, (tail_land, send, recv, local, store, tail_sem) = (
        refs[: n + 1], refs[n + 1 : 2 * n + 2], refs[2 * n + 2 : 3 * n + 2], refs[3 * n + 2 :]
    )
    x_first = [first for _array, _row, _rows, first in units]
    z, y, x, c = place()
    ctx = x * 2 + c
    after, before = lax.rem(ctx + 1, 4), lax.rem(ctx + 3, 4)
    barrier = pltpu.get_barrier_semaphore()
    for other in (after, before):
        pl.semaphore_signal(
            barrier, inc=1, device_id={"seq": z * 2 + y, "ctx": other},
            device_id_type=pl.DeviceIdType.MESH,
        )
    greet(z, y, x, c, 2)
    started, stored = [], []

    def shard(u):
        a, row, rows, _first = units[u]
        return ins[a].at[pl.ds(row, rows)]

    def slot_of(u, *at, into=None):
        a, row, rows, _first = units[u]
        return (land if into is None else into)[a].at[at + (pl.ds(row, rows),)]

    def number(u, kind, index):
        first = "x" if x_first[u] else "y"
        base = 0 if kind == "z" else 3 if kind == first else 15 if kind == "c" else 7
        return base + (index - 1 if kind == "z" else index)

    def push(u, zz, yy, xx, kind, index):
        slot = slot_of(u, zz, yy, xx, c)
        if kind == "z":
            target = device(lax.rem(z + index, NZ), y, x, c)
        else:
            flip = [1 - v if k == kind else v for k, v in (("y", y), ("x", x), ("c", c))]
            target = device(z, *flip)
        k = number(u, kind, index)
        copy = remote(slot, slot, send.at[u, k], recv.at[u, k], target)
        copy.start()
        started.append(copy)

    def came(u, zz, yy, xx, cc, kind, index):
        slot = slot_of(u, zz, yy, xx, cc)
        k = number(u, kind, index)
        remote(slot, slot, send.at[u, k], recv.at[u, k], device(z, y, x, 1 - c)).wait_recv()
        keep = pltpu.make_async_copy(slot, slot_of(u, zz, yy, xx, cc, into=outs), store.at[u, k])
        keep.start()
        stored.append(keep)

    back = [lax.rem(z + NZ - d, NZ) for d in range(NZ)]
    axes = [("x", "y") if first else ("y", "x") for first in x_first]
    every = range(len(units))
    ring = remote(
        ins[n], tail_land, tail_sem.at[0], tail_sem.at[1], {"seq": z * 2 + y, "ctx": after}
    )
    ring.start()
    for u in every:
        pltpu.make_async_copy(shard(u), slot_of(u, z, y, x, c), local.at[u]).start()

    def open_unit(u):
        a, b = axes[u]
        slot = slot_of(u, z, y, x, c)
        pltpu.make_async_copy(shard(u), slot, local.at[u]).wait()
        for d in (1, 3, 2):
            push(u, z, y, x, "z", d)
        for kind in (b, a, "c"):
            push(u, z, y, x, kind, 0)
        keep = pltpu.make_async_copy(slot, slot_of(u, z, y, x, c, into=outs), local.at[u])
        keep.start()
        stored.append(keep)

    def pass_on(u):
        a, b = axes[u]
        yy, xx = (y, 1 - x) if a == "x" else (1 - y, x)
        for d in range(1, NZ + 1):
            if d < NZ:
                came(u, back[d], y, x, c, "z", d)
                for kind in (b, a, "c"):
                    push(u, back[d], y, x, kind, d)
            came(u, back[d - 1], yy, xx, c, a, d - 1)
            push(u, back[d - 1], yy, xx, b, NZ + d - 1)
            push(u, back[d - 1], yy, xx, "c", NZ + d - 1)

    def cross(u):
        a, b = axes[u]
        for half in range(2):
            yy, xx = (1 - y, x) if b == "y" else (y, 1 - x)
            if half:
                yy, xx = 1 - y, 1 - x
            for d in range(NZ):
                came(u, back[d], yy, xx, c, b, NZ * half + d)
                push(u, back[d], yy, xx, "c", 2 * NZ + NZ * half + d)

    def finish(u):
        a, b = axes[u]
        for k in range(16):
            away = {a: (k // NZ) % 2, b: k // (2 * NZ)}
            came(u, back[k % NZ], 1 - y if away["y"] else y, 1 - x if away["x"] else x, 1 - c, "c", k)

    for t in range(-AHEAD, len(units) + 4):
        if 0 <= t + AHEAD < len(units):
            open_unit(t + AHEAD)
        if 0 <= t < len(units):
            pass_on(t)
        if 0 <= t - 2 < len(units):
            cross(t - 2)
        if 0 <= t - 4 < len(units):
            finish(t - 4)
    ring.wait_recv()
    keep = pltpu.make_async_copy(tail_land, outs[n], tail_sem.at[2])
    keep.start()
    keep.wait()
    ring.wait_send()
    for copy in started:
        copy.wait_send()
    for keep in stored:
        keep.wait()


def gather_all(shards, tail, units):
    n, m = len(shards), len(units)
    full = [(NZ, 2, 2, 2) + v.shape for v in shards]
    return pl.pallas_call(
        partial(gather_kernel, tuple(units), n),
        out_shape=[jax.ShapeDtypeStruct(f, v.dtype) for f, v in zip(full, shards)]
        + [jax.ShapeDtypeStruct(tail.shape, tail.dtype)],
        in_specs=[pl.BlockSpec(memory_space=pl.ANY)] * (n + 1),
        out_specs=[pl.BlockSpec(memory_space=pl.ANY)] * (n + 1),
        scratch_shapes=[pltpu.VMEM(f, v.dtype) for f, v in zip(full, shards)] + [
            pltpu.VMEM(tail.shape, tail.dtype),
            pltpu.SemaphoreType.DMA((m, 31)), pltpu.SemaphoreType.DMA((m, 31)),
            pltpu.SemaphoreType.DMA((m,)), pltpu.SemaphoreType.DMA((m, 31)),
            pltpu.SemaphoreType.DMA((3,)),
        ],
        compiler_params=pltpu.CompilerParams(
            collective_id=0, has_side_effects=True, vmem_limit_bytes=VMEM
        ),
    )(*shards, tail)


CUT_ROWS, CUT = 48, 512
AHEAD = 4


def finish_kernel(lead, dwz_ref, small_ref, dpx_ref, normed_ref, dz_ref, wx_ref, wz_ref, x_ref, tail_ref, gain_ref, g_ref,
                  oz_ref, ox_ref, os_ref, grad_ref,
                  own_z, own, core, first, second, last, own_s, core_s, first_s, second_s, last_s,
                  wbuf, total, back, spare, sem, semz, wsem, tail_sem):
    z, y, x, c = place()
    ctx = x * 2 + c
    after, before = lax.rem(ctx + 1, 4), lax.rem(ctx + 3, 4)
    barrier = pltpu.get_barrier_semaphore()
    for other in (after, before):
        pl.semaphore_signal(
            barrier, inc=1, device_id={"seq": z * 2 + y, "ctx": other},
            device_id_type=pl.DeviceIdType.MESH,
        )
    greet(z, y, x, c, 2)
    count = g_ref.shape[0]
    nz = dwz_ref.shape[-1] // CUT
    widths = [CUT] * nz + [
        min(CUT, dpx_ref.shape[1] - k) for k in range(0, dpx_ref.shape[1], CUT)
    ]
    pieces = len(widths)
    sent = []

    def view(i, k):
        if i == pieces:
            return (own_s, core_s, first_s, second_s, last_s)[k]
        v = (own, core, first, second, last)[k]
        j = i - nz if k == 0 else i
        if widths[i] == CUT:
            return v.at[j]
        return v.at[(j,) + (slice(None),) * (len(v.shape) - 2) + (pl.ds(0, widths[i]),)]

    def fetch(i):
        if i == pieces:
            return pltpu.make_async_copy(small_ref, own_s, sem.at[2, i])
        return pltpu.make_async_copy(
            dwz_ref.at[:, :, :, c, :, pl.ds(i * CUT, CUT)], own_z.at[i], sem.at[2, i]
        )

    def begin(i):
        if i < nz:
            src = dwz_ref.at[:, :, :, 1 - c, :, pl.ds(i * CUT, CUT)]
        else:
            src = view(i, 0).at[:, :, :, 1 - c]
        copy = remote(src, view(i, 1), sem.at[0, i], sem.at[1, i], device(z, y, x, 1 - c))
        copy.start()
        sent.append(copy)

    def x_goes_first(i):
        return i % 2 == 0

    def after_core(i):
        core_i = view(i, 1)
        if i < nz:
            fetch(i).wait()
        remote(core_i, core_i, sem.at[0, i], sem.at[1, i], device(z, y, x, 1 - c)).wait_recv()

        @pl.loop(0, NZ)
        def _(zz):
            for yy in range(2):
                for xx in range(2):
                    mine = own_z[i, zz, yy, xx] if i < nz else view(i, 0)[zz, yy, xx, c]
                    core_i[zz, yy, xx] = core_i[zz, yy, xx] + mine

        if x_goes_first(i):
            src, to = core_i.at[:, :, 1 - x], device(z, y, 1 - x, c)
        else:
            src, to = core_i.at[:, 1 - y], device(z, 1 - y, x, c)
        copy = remote(src, view(i, 2), sem.at[3, i], sem.at[4, i], to)
        copy.start()
        sent.append(copy)

    def after_first(i):
        core_i, first_i = view(i, 1), view(i, 2)
        remote(first_i, first_i, sem.at[3, i], sem.at[4, i], device(z, y, x, 1 - c)).wait_recv()

        @pl.loop(0, NZ)
        def _(zz):
            for o in range(2):
                mine = core_i[zz, o, x] if x_goes_first(i) else core_i[zz, y, o]
                first_i[zz, o] = first_i[zz, o] + mine

        if x_goes_first(i):
            src, to = first_i.at[:, 1 - y], device(z, 1 - y, x, c)
        else:
            src, to = first_i.at[:, 1 - x], device(z, y, 1 - x, c)
        copy = remote(src, view(i, 3), sem.at[5, i], sem.at[6, i], to)
        copy.start()
        sent.append(copy)

    def after_second(i):
        first_i, second_i, last_i = view(i, 2), view(i, 3), view(i, 4)
        remote(second_i, second_i, sem.at[5, i], sem.at[6, i], device(z, y, x, 1 - c)).wait_recv()

        @pl.loop(0, NZ)
        def _(zz):
            second_i[zz] = second_i[zz] + (first_i[zz, y] if x_goes_first(i) else first_i[zz, x])

        for d in range(1, NZ):
            zz = lax.rem(z + d, NZ)
            copy = remote(
                second_i.at[zz], last_i.at[z], semz.at[0, d, i], semz.at[1, d, i],
                device(zz, y, x, c),
            )
            copy.start()
            sent.append(copy)
        last_i[z] = second_i[z]

    def after_last(i):
        last_i = view(i, 4)
        for d in range(1, NZ):
            zz = lax.rem(z + NZ - d, NZ)
            remote(
                last_i.at[zz], last_i.at[zz], semz.at[0, d, i], semz.at[1, d, i],
                device(z, y, x, 1 - c),
            ).wait_recv()
        value = last_i[0].astype(f32)
        for zz in range(1, NZ):
            value = value + last_i[zz].astype(f32)
        if i == pieces:
            os_ref[...] = value
        elif i < nz:
            oz_ref[:, i * CUT : i * CUT + CUT] = value
        else:
            k = (i - nz) * CUT
            ox_ref[:, k : k + widths[i]] = value

    def weight_piece(j):
        k, w = j * CUT, widths[nz + j]
        own_i = view(nz + j, 0)
        depth = normed_ref.shape[1] // NZ

        @pl.loop(0, NZ)
        def _(zz):
            value = mm_tn(normed_ref[:, at(zz, depth)], dpx_ref[:, k : k + w])
            if nz + j == pieces - 1:
                lane = lax.broadcasted_iota(jnp.int32, (depth, w), 1)
                column = jnp.concatenate([spare[pl.ds(zz * depth, depth), :]] * (w // LANES), axis=1)
                value = jnp.where(lane + k < CHANNELS + HEADS, value, column)
            own_i[zz] = value.astype(bf16).reshape(2, 2, 2, CUT_ROWS, w)

    def weight_and_send(j):
        weight_piece(j)
        begin(nz + j)

    chunks = [(wz_ref, dz_ref, k, CUT) for k in range(0, wz_ref.shape[1], CUT)]
    chunks += [
        (wx_ref, dpx_ref, k, min(CUT, dpx_ref.shape[1] - k)) for k in range(0, dpx_ref.shape[1], CUT)
    ]

    def stream(q):
        w_ref, _left, k, w = chunks[q]
        return pltpu.make_async_copy(
            w_ref.at[:, pl.ds(k, w)], wbuf.at[q % 2, :, pl.ds(0, w)], wsem.at[q % 2]
        )

    def input_chunk(q):
        _w, left, k, w = chunks[q]
        stream(q).wait()
        weights = wbuf[q % 2, :, :w]
        rows = left.shape[0]
        value = mm_nt(left[:, k : k + w], weights)
        if q == 0:
            total[...] = jnp.zeros_like(total)
        total[:rows] += value
        if q + 2 < len(chunks):
            stream(q + 2).start()

    def tail_copy():
        return remote(
            total.at[pl.ds(count, 16)], back, tail_sem.at[0], tail_sem.at[1],
            {"seq": z * 2 + y, "ctx": before},
        )

    def scaled_rows(rows_ref, lo, hi):
        v = rows_ref[lo:hi].astype(f32)
        r = lax.rsqrt(jnp.mean(v * v, axis=1, keepdims=True) + EPSILON)
        return v, r

    def norm_weights():
        tail_copy().start()
        sums = jnp.zeros((normed_ref.shape[1], LANES), f32)
        ones = jnp.ones((LANES, LANES), bf16)
        for lo in range(0, count, LANES):
            v, r = scaled_rows(x_ref, lo, lo + LANES)
            product = v * r * total[lo : lo + LANES]
            high = product.astype(bf16)
            rest = (product - high.astype(f32)).astype(bf16)
            sums = sums + mm_tn(high, ones) + mm_tn(rest, ones)
        v, r = scaled_rows(tail_ref, 0, 16)
        product = v * r * total[count : count + 16]
        high = product.astype(bf16)
        rest = (product - high.astype(f32)).astype(bf16)
        sums = sums + mm_tn(high, ones[:16]) + mm_tn(rest, ones[:16])
        spare[...] = sums

    def norm_rows():
        tail_copy().wait()
        seqs = tail_ref.shape[0] // 8
        length = count // seqs
        for s in range(seqs):
            total[(s + 1) * length - 8 : (s + 1) * length] += back[8 * s : 8 * s + 8]
        for lo in range(0, count, LANES):
            v, r = scaled_rows(x_ref, lo, lo + LANES)
            scaled = gain_ref[0:1] * total[lo : lo + LANES]
            mean = jnp.mean(v * scaled, axis=1, keepdims=True)
            value = g_ref[lo : lo + LANES].astype(f32) + r * (scaled - v * (r * r) * mean)
            grad_ref[lo : lo + LANES] = value.astype(bf16)

    for i in range(nz):
        fetch(i).start()
    fetch(pieces).start()
    stream(0).start()
    stream(1).start()
    order = [pieces, *range(pieces)]
    for i in range(nz):
        begin(i)
    fetch(pieces).wait()
    begin(pieces)
    work = [[partial(weight_and_send, j)] for j in range(pieces - nz - 1)]
    step = -(-len(chunks) // 5)
    work += [
        [partial(input_chunk, q) for q in range(k, min(k + step, len(chunks)))]
        for k in range(0, len(chunks), step)
    ]
    work += [[norm_weights, partial(weight_and_send, pieces - nz - 1)], [norm_rows]]
    stages = list(zip((after_core, after_first, after_second, after_last), lead))
    for t in range(len(order) + lead[-1]):
        for job in work[t] if t < len(work) else []:
            job()
        for stage, skew in reversed(stages):
            if 0 <= t - skew < len(order):
                stage(order[t - skew])
    for copy in sent:
        copy.wait_send()


def finish(dw_z, small, dpx, normed, dz, w_x, w_z, x, tail, gain, g, lead=(0, 5, 7, 9)):
    dw_z = dw_z.reshape((NZ, 2, 2, 2, -1, dw_z.shape[-1]))
    small = small.reshape((NZ, 2, 2, 2, -1, small.shape[-1]))
    nz = dw_z.shape[-1] // CUT
    p = nz + pl.cdiv(dpx.shape[1], CUT)
    ss = small.shape[-2:]
    dims = [(NZ, 2, 2, 2), (NZ, 2, 2), (NZ, 2), (NZ,), (NZ,)]
    far, near = pl.BlockSpec(memory_space=pl.ANY), pl.BlockSpec(memory_space=pltpu.VMEM)
    return pl.pallas_call(
        partial(finish_kernel, tuple(lead)),
        out_shape=[
            jax.ShapeDtypeStruct((CUT_ROWS, dw_z.shape[-1]), f32),
            jax.ShapeDtypeStruct((CUT_ROWS, dpx.shape[1]), f32),
            jax.ShapeDtypeStruct(ss, f32),
            jax.ShapeDtypeStruct(g.shape, bf16),
        ],
        in_specs=[far, far, near, near, near, far, far, near, near, near, near],
        out_specs=[near] * 4,
        scratch_shapes=[pltpu.VMEM((nz,) + dims[1] + (CUT_ROWS, CUT), bf16)]
        + [pltpu.VMEM((n,) + d + (CUT_ROWS, CUT), bf16) for n, d in zip((p - nz, p, p, p, p), dims)]
        + [pltpu.VMEM(d + ss, f32) for d in dims]
        + [
            pltpu.VMEM((2, w_x.shape[0], CUT), bf16), pltpu.VMEM(normed.shape, f32),
            pltpu.VMEM(tail.shape, f32), pltpu.VMEM((normed.shape[1], LANES), f32),
            pltpu.SemaphoreType.DMA((7, p + 1)), pltpu.SemaphoreType.DMA((2, NZ, p + 1)),
            pltpu.SemaphoreType.DMA((2,)), pltpu.SemaphoreType.DMA((2,)),
        ],
        compiler_params=pltpu.CompilerParams(
            collective_id=1, has_side_effects=True, vmem_limit_bytes=FINISH_VMEM
        ),
    )(dw_z, small, dpx, normed, dz, w_x, w_z, x, tail, gain, g)


def local(tokens, norm_gain, input_weight, conv_w, conv_b, dt_bias, a_log, d_skip, gate_gain,
          output_weight, segments, cotangent):
    seqs, length, width = tokens.shape
    n_ctx = lax.axis_size("ctx")
    n_all = n_ctx * lax.axis_size("seq")
    count = seqs * length
    shares = [norm_gain.shape[0], gate_gain.shape[0], CONV * conv_b.shape[0], conv_b.shape[0]]
    cuts = [sum(shares[: i + 1]) for i in range(3)]
    packed = jnp.concatenate([norm_gain, gate_gain, conv_w.reshape(-1), conv_b])
    onward = [(i, i + 1) for i in range(n_ctx - 1)]
    tail = jnp.pad(tokens[:, length - (CONV - 1) :], ((0, 0), (8 - (CONV - 1), 0), (0, 0)))
    tail_ids = jnp.pad(
        segments[:, length - (CONV - 1) :].astype(bf16), ((0, 0), (0, width - (CONV - 1)))
    )
    tail = jnp.concatenate([tail_ids[:, None], tail[:, 1:]], axis=1).reshape(seqs * 8, width)
    torus = lax.axis_size("seq") == 2 * NZ and n_ctx == 4 and norm_gain.shape[0] == CUT_ROWS
    spare = ((0, 0), (0, LANES - HEADS))
    w_z, w_x = input_weight[:, :INNER], jnp.pad(input_weight[:, INNER:], spare)
    if torus:
        size = packed.shape[0]
        small = jnp.pad(packed, (0, 16 * LANES - size)).reshape(16, LANES)
        w_out = lax.all_gather(output_weight, BOTH, axis=0, tiled=True)
        w_z = lax.all_gather(w_z, BOTH, axis=0, tiled=True)
        w_x, packed, tail = gather_all(
            [w_x, small], tail,
            [(1, 0, 16, True)]
            + [(0, 16 * k, 16, k % 2 == 0) for k in range(3)]
,
        )
        w_x, w_z, w_out = (w.reshape(-1, w.shape[-1]) for w in (w_x, w_z, w_out))
        packed = packed.reshape(n_all, -1)[:, :size]
    else:
        packed = lax.all_gather(packed, BOTH, axis=0)
        tail = lax.ppermute(tail, "ctx", onward)
        w_in, w_out = (
            lax.all_gather(w, BOTH, axis=0, tiled=True) for w in (input_weight, output_weight)
        )
        w_z, w_x = w_in[:, :INNER], jnp.pad(w_in[:, INNER:], spare)
    norm_full, gate_full, conv_w_full, conv_b_full = jnp.split(packed.astype(f32), cuts, axis=1)
    norm_full = norm_full.reshape(1, -1)
    gate_full = gate_full.reshape(1, -1)
    conv_b_full = conv_b_full.reshape(1, -1)
    conv_w_full = conv_w_full.reshape(n_all, CONV, -1).transpose(1, 0, 2).reshape(CONV, -1)

    tail = tail.reshape(seqs, 8, width)
    tail_ids = jnp.where(
        lax.axis_index("ctx") == 0, -1, tail[:, 0, : CONV - 1].astype(jnp.int32)
    )
    tail = jnp.pad(tail[:, 8 - (CONV - 1) :], ((0, 0), (8 - (CONV - 1), 0), (0, 0)))
    tail = jnp.where(lax.axis_index("ctx") == 0, 0, tail)
    tail = tail.reshape(seqs * 8, width)
    x_all = jnp.concatenate([tokens.reshape(count, width), tail])
    x_all = x_all.astype(f32)
    r_all = lax.rsqrt(jnp.mean(x_all * x_all, axis=-1, keepdims=True) + EPSILON)
    normed = (x_all * r_all * norm_full).astype(bf16)

    ids_ext = jnp.concatenate([tail_ids, segments], axis=1)
    flags = [
        segments == ids_ext[:, CONV - 1 - k : CONV - 1 - k + length] for k in range(1, CONV)
    ] + [segments == ids_ext[:, CONV - 2 : CONV - 1], segments == segments[:, -1:]]
    cols = jnp.stack([f.astype(f32) for f in flags] + [segments.astype(f32)], axis=-1)
    cols = jnp.pad(cols, ((0, 0), (0, 0), (0, LANES - cols.shape[-1])))
    rows = jnp.pad(segments.astype(f32)[:, None], ((0, 0), (0, 7), (0, 0)))
    heads = jnp.pad(jnp.stack([pad_lanes(dt_bias), pad_lanes(a_log)]), ((0, 6), (0, 0)))
    lanes = jnp.concatenate([gate_full, jnp.repeat(d_skip, HEADDIM)[None]])
    lanes = jnp.pad(lanes, ((0, 6), (0, 0)))
    conv_w8 = jnp.pad(conv_w_full, ((0, 8 - CONV), (0, 0)))
    conv_b8 = jnp.pad(conv_b_full, ((0, 7), (0, 0)))

    px = MM(normed, w_x).astype(bf16)
    px_width, used = CHANNELS + LANES, CHANNELS + HEADS
    tail_spec = pl.BlockSpec((16, px_width), lambda s: (count // 16, 0))
    act, tok, cst, fresh = call(
        before_kernel, seqs,
        [per_rows(length, px_width), tail_spec, whole((8, CHANNELS)), whole((8, CHANNELS)),
         per_seq(length, LANES), whole((8, LANES))],
        [(per_seq(length, CHANNELS), ((seqs, length, CHANNELS), f32)),
         (per_seq(length, 2 * LANES), ((seqs, length, 2 * LANES), f32)),
         (per_seq(HEADS, length), ((seqs, HEADS, length), f32)),
         (per_seq(INNER, STATE), ((seqs, INNER, STATE), f32))],
        [pltpu.VMEM((length + 8, LANES), f32)],
        px, px, conv_w8, conv_b8, cols, heads,
    )
    carried = cols[:, length - 1, 3]
    kept = jnp.exp(cst[:, :, length - 1]) * carried[:, None]
    kept = jnp.repeat(kept, HEADDIM, axis=1)[..., None]
    g2 = cotangent.reshape(count, width)

    def gate_gradient():
        return lax.dot_general(g2, w_out, (((1,), (1,)), ((), ())), preferred_element_type=f32)

    def within():
        [y] = call(
            within_kernel, seqs,
            [per_seq(length, CHANNELS), per_seq(length, 2 * LANES), per_seq(HEADS, length),
             per_seq(length, LANES), per_seq(8, length)],
            [(per_seq(length, INNER), ((seqs, length, INNER), f32))],
            [pltpu.VMEM((length, length), f32), pltpu.VMEM((length, length), f32)],
            act, tok, cst, cols, rows,
        )
        return y

    def gates():
        return MM(normed[:count], w_z).astype(bf16)

    entering, (dgn, y, pz) = chain(fresh, kept, onward, (gate_gradient, within, gates))
    stayed = kept * entering.astype(f32)
    gn, dz, dy, dstate, dqueries, ddecay, sums = call(
        gate_kernel, seqs,
        [per_rows(length, INNER), per_seq(length, CHANNELS), per_seq(length, 2 * LANES),
         per_seq(length, LANES), per_seq(length, INNER), per_seq(INNER, STATE),
         per_rows(length, INNER), whole((8, INNER))],
        [(per_rows(length, INNER), ((count, INNER), bf16)),
         (per_rows(length, INNER), ((count, INNER), bf16)),
         (per_seq(length, INNER), ((seqs, length, INNER), bf16)),
         (per_seq(INNER, STATE), ((seqs, INNER, STATE), f32)),
         (per_seq(length, STATE), ((seqs, length, STATE), f32)),
         (per_seq(length, LANES), ((seqs, length, LANES), f32)),
         (per_seq(8, INNER), ((seqs, 8, INNER), f32))],
        [pltpu.VMEM((length, INNER), f32), pltpu.VMEM((length, STATE), f32)],
        pz, act, tok, cols, y, entering, dgn, lanes,
    )
    tn = (((0,), (0,)), ((), ()))

    def products():
        out = (x_all[:count] + MM(gn, w_out)).astype(bf16)
        return out, lax.dot_general(gn, g2, tn, preferred_element_type=f32).astype(bf16)

    def scan_back():
        return call(
            scan_back_kernel, seqs,
            [per_seq(length, CHANNELS), per_seq(length, 2 * LANES), per_seq(HEADS, length),
             per_seq(length, LANES), per_seq(8, length), per_seq(length, INNER)],
            [(per_seq(length, INNER), ((seqs, length, INNER), f32)),
             (per_seq(length, 2 * STATE), ((seqs, length, 2 * STATE), f32))],
            [pltpu.VMEM((length, length), f32)] * 3,
            act, tok, cst, cols, rows, dy,
        )

    def gate_weights():
        return lax.dot_general(normed[:count], dz, tn, preferred_element_type=f32).astype(bf16)

    later, ((output, dw_out), (dx, dbc), dw_z) = chain(
        dstate, kept, [(b, a) for a, b in reversed(onward)], (products, scan_back, gate_weights)
    )
    dpx, edge, dconv, dheads = call(
        after_kernel, seqs,
        [per_rows(length, px_width), tail_spec, whole((8, CHANNELS)), whole((8, CHANNELS)),
         per_seq(length, LANES), whole((8, LANES)), per_seq(length, CHANNELS),
         per_seq(length, 2 * LANES), whole((8, INNER)), per_seq(length, INNER),
         per_seq(length, INNER), per_seq(length, 2 * STATE), per_seq(length, STATE),
         per_seq(length, LANES), per_seq(INNER, STATE), per_seq(INNER, STATE)],
        [(per_rows(length, px_width), ((count, px_width), bf16)),
         (per_seq(8, px_width), ((seqs, 8, px_width), f32)),
         (per_seq(8, CHANNELS), ((seqs, 8, CHANNELS), f32)),
         (per_seq(8, LANES), ((seqs, 8, LANES), f32))],
        [pltpu.VMEM((length + 8, LANES), f32), pltpu.VMEM((CONV - 1, length + 16, LANES), f32),
         pltpu.VMEM((length, CHANNELS), f32), pltpu.VMEM((length, LANES), f32),
         pltpu.VMEM((length, LANES), f32), pltpu.VMEM((length, STATE), f32), pltpu.VMEM((LANES, LANES), f32),
         pltpu.VMEM((8, INNER), f32)],
        px, px, conv_w8, conv_b8, cols, heads, act, tok, lanes, dy, dx, dbc, dqueries, ddecay,
        later, stayed,
    )
    dpx_all = jnp.concatenate([dpx, edge.reshape(seqs * 8, px_width).astype(bf16)])
    sums = jnp.sum(sums, axis=0)
    dconv = jnp.sum(dconv, axis=0)
    dheads = jnp.sum(dheads, axis=0)
    d_skip_sum = jnp.sum(sums[1].reshape(HEADS, HEADDIM), axis=1)
    split = [sums[0].reshape(n_all, -1),
             dconv[:CONV].reshape(CONV, n_all, -1).transpose(1, 0, 2).reshape(n_all, -1),
             dconv[CONV].reshape(n_all, -1)]
    shared = jnp.concatenate([dheads[0, :HEADS], dheads[1, :HEADS], d_skip_sum])
    split = jnp.concatenate(split, axis=1)
    share = split.shape[1]
    if torus:
        fill = 8 * LANES - share - shared.shape[0]
        split = [split, jnp.broadcast_to(shared, (n_all,) + shared.shape), jnp.zeros((n_all, fill), f32)]
        dw_z, dw_x, mine, input_grad = finish(
            dw_z, jnp.concatenate(split, axis=1).reshape(n_all, 8, LANES), dpx_all, normed, dz,
            w_x, w_z, tokens.reshape(count, width), tail, jnp.pad(norm_full, ((0, 7), (0, 0))), g2,
        )
        dw_out = lax.psum_scatter(dw_out, BOTH, scatter_dimension=0, tiled=True).astype(f32)
        dw_in = jnp.concatenate([dw_z, dw_x[:, :used]], axis=1)
        d_norm = dw_x[:, used]
        mine = mine.reshape(-1)
        mine, shared = mine[:share], mine[share : share + shared.shape[0]]
    else:
        nt = (((1,), (1,)), ((), ()))
        dnormed_x = lax.dot_general(dpx_all, w_x, nt, preferred_element_type=f32)
        dnormed = dnormed_x[:count] + lax.dot_general(dz, w_z, nt, preferred_element_type=f32)
        back = dnormed_x[count:].reshape(seqs, 8, width)[:, 8 - (CONV - 1) :].astype(bf16)
        back = lax.ppermute(back, "ctx", [(b, a) for a, b in onward])
        dw_x = lax.dot_general(normed, dpx_all, tn, preferred_element_type=f32).astype(bf16)
        x, r = x_all[:count], r_all[:count]
        d_gain = jnp.sum(x * r * dnormed, axis=0) + jnp.sum(
            x_all[count:] * r_all[count:] * dnormed_x[count:], axis=0
        )
        back, d_gain, dw_x = lax.optimization_barrier((back, d_gain, dw_x))
        back = jnp.pad(back.astype(f32), ((0, 0), (length - (CONV - 1), 0), (0, 0)))
        scaled = norm_full * (dnormed + back.reshape(count, width))
        dx_in = r * (scaled - x * (r * r) * jnp.mean(x * scaled, axis=-1, keepdims=True))
        input_grad = (g2.astype(f32) + dx_in).astype(bf16)
        dw_in = jnp.concatenate([dw_z, dw_x[:, :used]], axis=1)
        dw_out, dw_in = (
            lax.psum_scatter(v.astype(f32), BOTH, scatter_dimension=0, tiled=True)
            for v in (dw_out, dw_in)
        )
        every = lax.psum(jnp.concatenate([split.reshape(-1), shared, d_gain]), BOTH)
        me = lax.axis_index("seq") * n_ctx + lax.axis_index("ctx")
        d_norm = lax.dynamic_slice(every[-width:], (me * shares[0],), (shares[0],))
        mine = lax.dynamic_slice(every, (me * share,), (share,))
        shared = every[n_all * share : n_all * share + shared.shape[0]]
    d_gate, d_conv_w, d_conv_b = jnp.split(mine, [v - cuts[0] for v in cuts[1:]])
    d_bias, d_alog, d_skips = jnp.split(shared, 3)
    return (
        output.reshape(tokens.shape), input_grad.reshape(tokens.shape), d_norm, dw_in,
        d_conv_w.reshape(CONV, -1), d_conv_b, d_bias, d_alog, d_skips, d_gate, dw_out,
    )


def solution(mesh):
    split = P(BOTH)
    rows = P(BOTH, None)
    seq = P("seq", "ctx", None)
    in_specs = (seq, split, rows, P(None, BOTH), split, P(), P(), P(), split, rows,
                P("seq", "ctx"), seq)
    out_specs = (seq, seq, split, rows, P(None, BOTH), split, P(), P(), P(), split, rows)
    return jax.shard_map(local, mesh=mesh, in_specs=in_specs, out_specs=out_specs, check_vma=False)
```

```python
from functools import partial

import jax
import jax.numpy as jnp
from jax import lax
from jax.experimental import pallas as pl
from jax.experimental.pallas import tpu as pltpu
from jax.sharding import PartitionSpec as P

HEADS = 48
STATE = 128
HEADDIM = 64
CONV = 4
INNER = HEADS * HEADDIM
CHANNELS = INNER + 2 * STATE
GROUP = 8
GROUPS = HEADS // GROUP
WIDTH = GROUP * HEADDIM
LANES = 128
EPSILON = 1e-05
VMEM = 60 * 1024 * 1024
FINISH_VMEM = 62 * 1024 * 1024 - 512 * 1024
BOTH = ("seq", "ctx")
FAR = -1e30
f32 = jnp.float32
bf16 = jnp.bfloat16
MM = partial(jnp.dot, preferred_element_type=f32)


def mm_nt(a, b):
    return lax.dot_general(a, b, (((1,), (1,)), ((), ())), preferred_element_type=f32)


def mm_tn(a, b):
    return lax.dot_general(a, b, (((0,), (0,)), ((), ())), preferred_element_type=f32)


def sigmoid(v):
    return 0.5 + 0.5 * jnp.tanh(0.5 * v)


def at(j, width):
    return pl.ds(pl.multiple_of(j * width, width), width)


def low_half(rows):
    return lax.broadcasted_iota(jnp.int32, (rows, LANES), 1) < HEADDIM


def to_front(columns, g):
    return pltpu.roll(columns, lax.rem(LANES - GROUP * g, LANES), 1)


def spread(front, pair, low):
    return jnp.where(low, front[:, 2 * pair : 2 * pair + 1], front[:, 2 * pair + 1 : 2 * pair + 2])


def head_sums(product, g):
    lane = lax.broadcasted_iota(jnp.int32, (WIDTH, LANES), 1)
    row = lax.broadcasted_iota(jnp.int32, (WIDTH, LANES), 0)
    pick = jnp.where(lane == row // HEADDIM, 1.0, 0.0).astype(bf16)
    high = product.astype(bf16)
    rest = (product - high.astype(f32)).astype(bf16)
    return pltpu.roll(MM(high, pick) + MM(rest, pick), GROUP * g, 1)


def taps(px_ref, tail, j, w_ref, b_ref, masks, ext):
    here = at(j, LANES)
    length = px_ref.shape[0]
    own = px_ref[:, here].astype(f32)
    ext[0:8, :] = tail
    ext[8 : 8 + length, :] = own
    inputs = [own] + [
        masks[k - 1] * ext[8 - k : 8 - k + length, :] for k in range(1, CONV)
    ]
    out = b_ref[0:1, here]
    for k in range(CONV):
        out = out + w_ref[k : k + 1, here] * inputs[k]
    return out, inputs


def tail_of(tail_ref, s, here):
    both = tail_ref[:, here].astype(f32)
    return jnp.where(s == 0, both[0:8], both[8:16])


def lane_masks(cols_ref, length):
    return [
        jnp.broadcast_to(cols_ref[0, :, k : k + 1], (length, LANES)) for k in range(CONV - 1)
    ]


NZ = 4


def place():
    seq, ctx = lax.axis_index("seq"), lax.axis_index("ctx")
    return seq // 2, lax.rem(seq, 2), ctx // 2, lax.rem(ctx, 2)


def device(z, y, x, c):
    return {"seq": z * 2 + y, "ctx": x * 2 + c}


def greet(z, y, x, c, more=0):
    barrier = pltpu.get_barrier_semaphore()
    others = [device(z, y, x, 1 - c), device(z, y, 1 - x, c), device(z, 1 - y, x, c)]
    others += [device(lax.rem(z + d, NZ), y, x, c) for d in range(1, NZ)]
    for other in others:
        pl.semaphore_signal(barrier, inc=1, device_id=other, device_id_type=pl.DeviceIdType.MESH)
    pl.semaphore_wait(barrier, len(others) + more)


def remote(src, dst, send, recv, target):
    return pltpu.make_async_remote_copy(
        src_ref=src, dst_ref=dst, send_sem=send, recv_sem=recv, device_id=target,
        device_id_type=pl.DeviceIdType.MESH,
    )


def gather_kernel(units, n, *refs):
    ins, outs, land, (tail_land, send, recv, local, store, tail_sem) = (
        refs[: n + 1], refs[n + 1 : 2 * n + 2], refs[2 * n + 2 : 3 * n + 2], refs[3 * n + 2 :]
    )
    x_first = [first for _array, _row, _rows, first in units]
    z, y, x, c = place()
    ctx = x * 2 + c
    after, before = lax.rem(ctx + 1, 4), lax.rem(ctx + 3, 4)
    barrier = pltpu.get_barrier_semaphore()
    for other in (after, before):
        pl.semaphore_signal(
            barrier, inc=1, device_id={"seq": z * 2 + y, "ctx": other},
            device_id_type=pl.DeviceIdType.MESH,
        )
    greet(z, y, x, c, 2)
    started, stored = [], []

    def shard(u):
        a, row, rows, _first = units[u]
        return ins[a].at[pl.ds(row, rows)]

    def slot_of(u, *at, into=None):
        a, row, rows, _first = units[u]
        return (land if into is None else into)[a].at[at + (pl.ds(row, rows),)]

    def number(u, kind, index):
        first = "x" if x_first[u] else "y"
        base = 0 if kind == "z" else 3 if kind == first else 15 if kind == "c" else 7
        return base + (index - 1 if kind == "z" else index)

    def push(u, zz, yy, xx, kind, index):
        slot = slot_of(u, zz, yy, xx, c)
        if kind == "z":
            target = device(lax.rem(z + index, NZ), y, x, c)
        else:
            flip = [1 - v if k == kind else v for k, v in (("y", y), ("x", x), ("c", c))]
            target = device(z, *flip)
        k = number(u, kind, index)
        copy = remote(slot, slot, send.at[u, k], recv.at[u, k], target)
        copy.start()
        started.append(copy)

    def came(u, zz, yy, xx, cc, kind, index):
        slot = slot_of(u, zz, yy, xx, cc)
        k = number(u, kind, index)
        remote(slot, slot, send.at[u, k], recv.at[u, k], device(z, y, x, 1 - c)).wait_recv()
        keep = pltpu.make_async_copy(slot, slot_of(u, zz, yy, xx, cc, into=outs), store.at[u, k])
        keep.start()
        stored.append(keep)

    back = [lax.rem(z + NZ - d, NZ) for d in range(NZ)]
    axes = [("x", "y") if first else ("y", "x") for first in x_first]
    every = range(len(units))
    ring = remote(
        ins[n], tail_land, tail_sem.at[0], tail_sem.at[1], {"seq": z * 2 + y, "ctx": after}
    )
    ring.start()
    for u in every:
        pltpu.make_async_copy(shard(u), slot_of(u, z, y, x, c), local.at[u]).start()

    def open_unit(u):
        a, b = axes[u]
        slot = slot_of(u, z, y, x, c)
        pltpu.make_async_copy(shard(u), slot, local.at[u]).wait()
        for d in (1, 3, 2):
            push(u, z, y, x, "z", d)
        for kind in (b, a, "c"):
            push(u, z, y, x, kind, 0)
        keep = pltpu.make_async_copy(slot, slot_of(u, z, y, x, c, into=outs), local.at[u])
        keep.start()
        stored.append(keep)

    def pass_on(u):
        a, b = axes[u]
        yy, xx = (y, 1 - x) if a == "x" else (1 - y, x)
        for d in range(1, NZ + 1):
            if d < NZ:
                came(u, back[d], y, x, c, "z", d)
                for kind in (b, a, "c"):
                    push(u, back[d], y, x, kind, d)
            came(u, back[d - 1], yy, xx, c, a, d - 1)
            push(u, back[d - 1], yy, xx, b, NZ + d - 1)
            push(u, back[d - 1], yy, xx, "c", NZ + d - 1)

    def cross(u):
        a, b = axes[u]
        for half in range(2):
            yy, xx = (1 - y, x) if b == "y" else (y, 1 - x)
            if half:
                yy, xx = 1 - y, 1 - x
            for d in range(NZ):
                came(u, back[d], yy, xx, c, b, NZ * half + d)
                push(u, back[d], yy, xx, "c", 2 * NZ + NZ * half + d)

    def finish(u):
        a, b = axes[u]
        for k in range(16):
            away = {a: (k // NZ) % 2, b: k // (2 * NZ)}
            came(u, back[k % NZ], 1 - y if away["y"] else y, 1 - x if away["x"] else x, 1 - c, "c", k)

    for t in range(-AHEAD, len(units) + 4):
        if 0 <= t + AHEAD < len(units):
            open_unit(t + AHEAD)
        if 0 <= t < len(units):
            pass_on(t)
        if 0 <= t - 2 < len(units):
            cross(t - 2)
        if 0 <= t - 4 < len(units):
            finish(t - 4)
    ring.wait_recv()
    keep = pltpu.make_async_copy(tail_land, outs[n], tail_sem.at[2])
    keep.start()
    keep.wait()
    ring.wait_send()
    for copy in started:
        copy.wait_send()
    for keep in stored:
        keep.wait()


def gather_all(shards, tail, units):
    n, m = len(shards), len(units)
    full = [(NZ, 2, 2, 2) + v.shape for v in shards]
    return pl.pallas_call(
        partial(gather_kernel, tuple(units), n),
        out_shape=[jax.ShapeDtypeStruct(f, v.dtype) for f, v in zip(full, shards)]
        + [jax.ShapeDtypeStruct(tail.shape, tail.dtype)],
        in_specs=[pl.BlockSpec(memory_space=pl.ANY)] * (n + 1),
        out_specs=[pl.BlockSpec(memory_space=pl.ANY)] * (n + 1),
        scratch_shapes=[pltpu.VMEM(f, v.dtype) for f, v in zip(full, shards)] + [
            pltpu.VMEM(tail.shape, tail.dtype),
            pltpu.SemaphoreType.DMA((m, 31)), pltpu.SemaphoreType.DMA((m, 31)),
            pltpu.SemaphoreType.DMA((m,)), pltpu.SemaphoreType.DMA((m, 31)),
            pltpu.SemaphoreType.DMA((3,)),
        ],
        compiler_params=pltpu.CompilerParams(
            collective_id=0, has_side_effects=True, vmem_limit_bytes=VMEM
        ),
    )(*shards, tail)


CUT_ROWS, CUT = 48, 512
SLOTS = 3
LEAD = (0, 5, 7, 9)
AHEAD = 4


def meet(place_of, ring):
    z, y, x, c = place_of
    if ring:
        barrier = pltpu.get_barrier_semaphore()
        for step in (1, 3):
            pl.semaphore_signal(
                barrier, inc=1, device_id={"seq": z * 2 + y, "ctx": lax.rem(x * 2 + c + step, 4)},
                device_id_type=pl.DeviceIdType.MESH,
            )
    greet(z, y, x, c, 2 if ring else 0)


class Reduction:
    def __init__(self, place_of, source, own, buffers, result, sem, semz):
        self.place, self.source, self.own, self.buffers = place_of, source, own, buffers
        self.result, self.sem, self.semz = result, sem, semz

    def copies(self, i, stage):
        z, y, x, c = self.place
        core, first, second, last = self.buffers(i)
        x_first = i % 2 == 0
        along_x, along_y = device(z, y, 1 - x, c), device(z, 1 - y, x, c)
        if stage == 0:
            moves = [(self.source(i, 1 - c), core, device(z, y, x, 1 - c))]
        elif stage == 1:
            src = core.at[:, :, 1 - x] if x_first else core.at[:, 1 - y]
            moves = [(src, first, along_x if x_first else along_y)]
        elif stage == 2:
            src = first.at[:, 1 - y] if x_first else first.at[:, 1 - x]
            moves = [(src, second, along_y if x_first else along_x)]
        else:
            moves = []
            for d in range(1, NZ):
                zz = lax.rem(z + d, NZ)
                moves.append((second.at[zz], last.at[z], device(zz, y, x, c)))
        made = []
        for d, (src, dst, to) in enumerate(moves):
            if stage < 3:
                sems = self.sem.at[2 * stage, i], self.sem.at[2 * stage + 1, i]
            else:
                sems = self.semz.at[0, d, i], self.semz.at[1, d, i]
            made.append(remote(src, dst, *sems, to))
        return made

    def send(self, i, stage):
        for copy in self.copies(i, stage):
            copy.start()

    def drain(self, i):
        for stage in range(4):
            for copy in self.copies(i, stage):
                copy.wait_send()

    def arrive(self, i, stage):
        z, y, x, c = self.place
        core, first, second, last = self.buffers(i)
        x_first = i % 2 == 0
        if stage < 3:
            landed = (core, first, second)[stage]
            remote(
                landed, landed, self.sem.at[2 * stage, i], self.sem.at[2 * stage + 1, i],
                device(z, y, x, 1 - c),
            ).wait_recv()
        if stage == 0:
            own = self.own(i)

            @pl.loop(0, NZ)
            def _(zz):
                for yy in range(2):
                    for xx in range(2):
                        core[zz, yy, xx] = core[zz, yy, xx] + own(zz, yy, xx)

        elif stage == 1:

            @pl.loop(0, NZ)
            def _(zz):
                for o in range(2):
                    first[zz, o] = first[zz, o] + (core[zz, o, x] if x_first else core[zz, y, o])

        elif stage == 2:

            @pl.loop(0, NZ)
            def _(zz):
                second[zz] = second[zz] + (first[zz, y] if x_first else first[zz, x])

            last[z] = second[z]
        else:
            for d in range(1, NZ):
                landed = last.at[lax.rem(z + NZ - d, NZ)]
                remote(
                    landed, landed, self.semz.at[0, d - 1, i], self.semz.at[1, d - 1, i],
                    device(z, y, x, 1 - c),
                ).wait_recv()
            value = last[0].astype(f32)
            for zz in range(1, NZ):
                value = value + last[zz].astype(f32)
            self.result(i, value)
        if stage < 3:
            self.send(i, stage + 1)


def reduction_buffers(count, shape, dtype):
    return [pltpu.VMEM((count,) + d + shape, dtype) for d in ((NZ, 2, 2), (NZ, 2), (NZ,), (NZ,))]


def reduction_semaphores(count):
    return [pltpu.SemaphoreType.DMA((6, count)), pltpu.SemaphoreType.DMA((2, NZ - 1, count))]


def cut_to(width, ref):
    if ref.shape[-1] == width:
        return ref
    return ref.at[(slice(None),) * (len(ref.shape) - 1) + (pl.ds(0, width),)]


def before_kernel(px_ref, tail_ref, w_ref, b_ref, cols_ref, heads_ref,
                  act_ref, tok_ref, cst_ref, fresh_ref, ext):
    s = pl.program_id(0)
    length = px_ref.shape[0]
    masks = lane_masks(cols_ref, length)

    @pl.loop(0, CHANNELS // LANES)
    def _(j):
        here = at(j, LANES)
        conv, _unused = taps(px_ref, tail_of(tail_ref, s, here), j, w_ref, b_ref, masks, ext)
        act_ref[0, :, here] = conv * sigmoid(conv)

    raw = px_ref[:, CHANNELS : CHANNELS + HEADS].astype(f32) + heads_ref[0:1, :HEADS]
    step = jnp.maximum(raw, 0.0) + jnp.log1p(jnp.exp(-jnp.abs(raw)))
    step = jnp.concatenate([step, jnp.zeros((length, LANES - HEADS), f32)], axis=1)
    rate = -step * jnp.exp(heads_ref[1:2, :])
    before = (
        lax.broadcasted_iota(jnp.int32, (length, length), 0)
        >= lax.broadcasted_iota(jnp.int32, (length, length), 1)
    ).astype(f32)
    decay = jnp.dot(before, rate, precision=lax.Precision.HIGHEST, preferred_element_type=f32)
    tok_ref[0, :, 0:LANES] = step
    tok_ref[0, :, LANES : 2 * LANES] = decay
    cst_ref[0] = decay.T[:HEADS]
    toward = jnp.exp(decay[length - 1 : length] - decay) * step * cols_ref[0, :, 4:5]
    keys = act_ref[0, :, INNER : INNER + STATE].astype(bf16)
    low = low_half(length)

    @pl.loop(0, GROUPS)
    def _(g):
        front = to_front(toward, g)
        scaled = []
        for pair in range(GROUP // 2):
            here = pl.ds(pl.multiple_of(g * WIDTH + pair * LANES, LANES), LANES)
            scaled.append((act_ref[0, :, here] * spread(front, pair, low)).astype(bf16))
        fresh_ref[0, at(g, WIDTH), :] = mm_tn(jnp.concatenate(scaled, axis=1), keys)


def bias_of(ids_col, ids_row, transposed):
    shape = (ids_col.shape[0], ids_row.shape[1])
    down = lax.broadcasted_iota(jnp.int32, shape, 0)
    across = lax.broadcasted_iota(jnp.int32, shape, 1)
    order = (down <= across) if transposed else (down >= across)
    return jnp.where(order & (ids_col == ids_row), 0.0, FAR)


def within_kernel(act_ref, tok_ref, cst_ref, cols_ref, rows_ref, y_ref, cross, bias):
    length = act_ref.shape[1]
    half = length // 2
    cross[...] = mm_nt(
        act_ref[0, :, INNER + STATE :].astype(bf16),
        act_ref[0, :, INNER : INNER + STATE].astype(bf16),
    )
    bias[...] = bias_of(cols_ref[0, :, 5:6], rows_ref[0, 0:1, :], False)
    low = low_half(length)

    @pl.loop(0, GROUPS)
    def _(g):
        step = to_front(tok_ref[0, :, 0:LANES], g)
        decay = to_front(tok_ref[0, :, LANES : 2 * LANES], g)
        rows = cst_ref[0, at(g, GROUP), :]
        for pair in range(GROUP // 2):
            here = pl.ds(pl.multiple_of(g * WIDTH + pair * LANES, LANES), LANES)
            scaled = act_ref[0, :, here] * spread(step, pair, low)
            top, bottom = 0.0, 0.0
            for which in range(2):
                h = 2 * pair + which
                mine = jnp.where(low == (which == 0), scaled, 0.0).astype(bf16)
                col, row = decay[:, h : h + 1], rows[h : h + 1, :]
                w = jnp.exp(col[:half] - row[:, :half] + bias[:half, :half])
                top = top + MM((cross[:half, :half] * w).astype(bf16), mine[:half])
                w = jnp.exp(col[half:] - row + bias[half:, :])
                bottom = bottom + MM((cross[half:, :] * w).astype(bf16), mine)
            y_ref[0, :half, here] = top
            y_ref[0, half:, here] = bottom


def gate_kernel(z_ref, act_ref, tok_ref, cols_ref, y_ref, state_ref, dgn_ref, lanes_ref,
                gn_ref, dz_ref, dy_ref, dstate_ref, q_ref, dq_ref, sums_ref, total, queries_acc):
    length = act_ref.shape[1]
    low = low_half(length)
    enter = jnp.exp(tok_ref[0, :, LANES : 2 * LANES]) * cols_ref[0, :, 3:4]
    queries = act_ref[0, :, INNER + STATE :].astype(bf16)

    def first(g, carry):
        square, inner = carry
        front = to_front(enter, g)
        group_far = mm_nt(queries, state_ref[0, at(g, WIDTH), :])
        for pair in range(GROUP // 2):
            here = pl.ds(pl.multiple_of(g * WIDTH + pair * LANES, LANES), LANES)
            far = group_far[:, pair * LANES : (pair + 1) * LANES]
            y = y_ref[0, :, here] + spread(front, pair, low) * far
            total[:, here] = y
            y = y + lanes_ref[1:2, here] * act_ref[0, :, here]
            z = z_ref[:, here].astype(f32)
            gated = y * (z * sigmoid(z))
            square = square + gated * gated
            inner = inner + lanes_ref[0:1, here] * dgn_ref[:, here] * gated
        return square, inner

    zero = jnp.zeros((length, LANES), f32)
    square, inner = lax.fori_loop(0, GROUPS, first, (zero, zero))
    scale = lax.rsqrt(jnp.sum(square, axis=1, keepdims=True) * (1.0 / INNER) + EPSILON)
    back = scale * scale * scale * (jnp.sum(inner, axis=1, keepdims=True) * (1.0 / INNER))
    scale = jnp.broadcast_to(scale, (length, LANES))
    back = jnp.broadcast_to(back, (length, LANES))
    queries_acc[...] = jnp.zeros_like(queries_acc)
    dq_ref[0] = jnp.zeros_like(dq_ref[0])

    @pl.loop(0, GROUPS)
    def _(g):
        front = to_front(enter, g)
        products, entered = [], []
        for pair in range(GROUP // 2):
            here = pl.ds(pl.multiple_of(g * WIDTH + pair * LANES, LANES), LANES)
            xs = act_ref[0, :, here]
            inside = total[:, here]
            y = inside + lanes_ref[1:2, here] * xs
            z = z_ref[:, here].astype(f32)
            sg = sigmoid(z)
            gate = z * sg
            gated = y * gate
            gain = lanes_ref[0:1, here]
            dgn = dgn_ref[:, here]
            gn = gated * scale
            gn_ref[:, here] = (gn * gain).astype(bf16)
            dgated = scale * (gain * dgn) - gated * back
            dy = dgated * gate
            dz_ref[:, here] = (dgated * y * (sg * (1.0 + z * (1.0 - sg)))).astype(bf16)
            rounded = dy.astype(bf16)
            dy_ref[0, :, here] = rounded
            sums_ref[0, 0:1, here] = jnp.sum(dgn * gn, axis=0, keepdims=True)
            sums_ref[0, 1:2, here] = jnp.sum(dy * xs, axis=0, keepdims=True)
            rounded = rounded.astype(f32)
            entered.append((rounded * spread(front, pair, low)).astype(bf16))
            products.append(rounded * inside)
        entered = jnp.concatenate(entered, axis=1)
        dstate_ref[0, at(g, WIDTH), :] = mm_tn(entered, queries)
        queries_acc[...] += MM(entered, state_ref[0, at(g, WIDTH), :])
        dq_ref[0] += head_sums(jnp.concatenate(products, axis=1), g)

    q_ref[0] = queries_acc[...]


def scan_back_kernel(act_ref, tok_ref, cst_ref, cols_ref, rows_ref, dy_ref,
                     dx_ref, dbc_ref, cross, bias, dcross):
    length = act_ref.shape[1]
    half = length // 2
    keys = act_ref[0, :, INNER : INNER + STATE].astype(bf16)
    queries = act_ref[0, :, INNER + STATE :].astype(bf16)
    cross[...] = mm_nt(keys, queries)
    bias[...] = bias_of(cols_ref[0, :, 5:6], rows_ref[0, 0:1, :], True)
    dcross[...] = jnp.zeros_like(dcross)
    low = low_half(length)

    @pl.loop(0, GROUPS)
    def _(g):
        step = to_front(tok_ref[0, :, 0:LANES], g)
        decay = to_front(tok_ref[0, :, LANES : 2 * LANES], g)
        rows = cst_ref[0, at(g, GROUP), :]
        for pair in range(GROUP // 2):
            here = pl.ds(pl.multiple_of(g * WIDTH + pair * LANES, LANES), LANES)
            scaled = (act_ref[0, :, here] * spread(step, pair, low)).astype(bf16)
            dy = dy_ref[0, :, here].astype(f32)
            top, bottom = 0.0, 0.0
            for which in range(2):
                h = 2 * pair + which
                mine = jnp.where(low == (which == 0), dy, 0.0).astype(bf16)
                col, row = decay[:, h : h + 1], rows[h : h + 1, :]
                w = jnp.exp(row - col[:half] + bias[:half, :])
                dcross[:half, :] += mm_nt(scaled[:half], mine) * w
                top = top + MM((cross[:half, :] * w).astype(bf16), mine)
                w = jnp.exp(row[:, half:] - col[half:] + bias[half:, half:])
                dcross[half:, half:] += mm_nt(scaled[half:], mine[half:]) * w
                bottom = bottom + MM((cross[half:, half:] * w).astype(bf16), mine[half:])
            dx_ref[0, :half, here] = top
            dx_ref[0, half:, here] = bottom

    d = dcross[...].astype(bf16)
    dbc_ref[0, :, :STATE] = MM(d, queries)
    dbc_ref[0, :, STATE:] = mm_tn(d, keys)


def after_kernel(px_ref, tail_ref, w_ref, b_ref, cols_ref, heads_ref, act_ref, tok_ref, lanes_ref,
                 dy_ref, dx_ref, dbc_ref, q_ref, dq_ref, later_ref, kept_ref,
                 dpx_ref, dconv_ref, dheads_ref, ext, moved, grad, dstep_acc, dcol_acc, keys_acc, ends, sent, edges):
    s = pl.program_id(0)
    length = act_ref.shape[1]
    low = low_half(length)
    step = tok_ref[0, :, 0:LANES]
    decay = tok_ref[0, :, LANES : 2 * LANES]
    leave = jnp.exp(decay[length - 1 : length] - decay) * cols_ref[0, :, 4:5]
    keys = act_ref[0, :, INNER : INNER + STATE].astype(bf16)
    dstep_acc[...] = jnp.zeros_like(dstep_acc)
    dcol_acc[...] = jnp.zeros_like(dcol_acc)
    sent[...] = jnp.zeros_like(sent)
    keys_acc[...] = dbc_ref[0, :, :STATE]
    ends[...] = jnp.zeros_like(ends)

    @pl.loop(0, GROUPS)
    def _(g):
        step_front, leave_front = to_front(step, g), to_front(leave, g)
        products, columns, leaves = [], [], []
        group_through = mm_nt(keys, later_ref[0, at(g, WIDTH), :])
        for pair in range(GROUP // 2):
            here = pl.ds(pl.multiple_of(g * WIDTH + pair * LANES, LANES), LANES)
            later = later_ref[0, here, :]
            xs = act_ref[0, :, here]
            steps = spread(step_front, pair, low)
            leaving = spread(leave_front, pair, low)
            through = leaving * group_through[:, pair * LANES : (pair + 1) * LANES]
            dscaled = dx_ref[0, :, here] + through
            scaled = steps * xs
            rounded = scaled.astype(bf16).astype(f32)
            leaves.append((leaving * scaled).astype(bf16))
            products.append(xs * dscaled)
            columns.append(rounded * dscaled)
            sent[0:1, here] = jnp.sum(rounded * through, axis=0, keepdims=True)
            grad[:, here] = steps * dscaled + lanes_ref[1:2, here] * dy_ref[0, :, here].astype(f32)
            both = later.astype(f32) * kept_ref[0, here, :]
            at_row = GROUP * g + 2 * pair
            ends[pl.ds(at_row, 1), :] = jnp.sum(both[:HEADDIM], axis=0, keepdims=True)
            ends[pl.ds(at_row + 1, 1), :] = jnp.sum(both[HEADDIM:], axis=0, keepdims=True)
        keys_acc[...] += MM(jnp.concatenate(leaves, axis=1), later_ref[0, at(g, WIDTH), :])
        dstep_acc[...] += head_sums(jnp.concatenate(products, axis=1), g)
        dcol_acc[...] += head_sums(jnp.concatenate(columns, axis=1), g)

    grad[:, INNER : INNER + STATE] = keys_acc[...]
    grad[:, INNER + STATE :] = dbc_ref[0, :, STATE:] + q_ref[0]
    dstep = dstep_acc[...]
    at_end = jnp.sum(ends[...].T, axis=0, keepdims=True)
    for g in range(GROUPS):
        at_end = at_end + head_sums(sent[:, g * WIDTH : (g + 1) * WIDTH], g)[0:1]
    row = lax.broadcasted_iota(jnp.int32, (length, LANES), 0)
    ddecay = dq_ref[0] - dcol_acc[...] + jnp.where(row == length - 1, at_end, 0.0)
    onward = (
        lax.broadcasted_iota(jnp.int32, (length, length), 0)
        <= lax.broadcasted_iota(jnp.int32, (length, length), 1)
    ).astype(f32)
    drate = jnp.dot(onward, ddecay, precision=lax.Precision.HIGHEST, preferred_element_type=f32)
    speed = jnp.exp(heads_ref[1:2, :])
    raw = px_ref[:, CHANNELS : CHANNELS + HEADS].astype(f32) + heads_ref[0:1, :HEADS]
    draw = (dstep - drate * speed)[:, :HEADS] * sigmoid(raw)
    mine = pl.ds(pl.multiple_of(s * length, length), length)
    dpx_ref[mine, CHANNELS:] = jnp.concatenate(
        [draw, jnp.zeros((length, LANES - HEADS), f32)], axis=1
    ).astype(bf16)
    edges[s, :, CHANNELS:] = jnp.zeros((8, LANES), f32)
    dheads_ref[0] = jnp.zeros((8, LANES), f32)
    dheads_ref[0, 0:1, :HEADS] = jnp.sum(draw, axis=0, keepdims=True)
    dheads_ref[0, 1:2, :] = jnp.sum(drate * (-step * speed), axis=0, keepdims=True)

    masks = lane_masks(cols_ref, length)
    moved[...] = jnp.zeros_like(moved)
    dconv_ref[0] = jnp.zeros((8, CHANNELS), f32)

    @pl.loop(0, CHANNELS // LANES)
    def _(j):
        here = at(j, LANES)
        conv, inputs = taps(px_ref, tail_of(tail_ref, s, here), j, w_ref, b_ref, masks, ext)
        sg = sigmoid(conv)
        dconv = grad[:, here] * (sg * (1.0 + conv * (1.0 - sg)))
        for k in range(CONV):
            dconv_ref[0, k : k + 1, here] = jnp.sum(dconv * inputs[k], axis=0, keepdims=True)
        dconv_ref[0, CONV : CONV + 1, here] = jnp.sum(dconv, axis=0, keepdims=True)
        dx = w_ref[0:1, here] * dconv
        edge = jnp.zeros((8, LANES), f32)
        for k in range(1, CONV):
            moved[k - 1, 8 : 8 + length, :] = dconv * masks[k - 1]
            dx = dx + w_ref[k : k + 1, here] * moved[k - 1, 8 + k : 8 + k + length, :]
            edge = edge + w_ref[k : k + 1, here] * moved[k - 1, k : 8 + k, :]
        dpx_ref[mine, here] = dx.astype(bf16)
        edges[s, :, here] = edge

    @pl.when(s == pl.num_programs(0) - 1)
    def _():
        rows = edges.shape[0] * 8
        dpx_ref[dpx_ref.shape[0] - rows :, :] = edges[...].reshape(rows, edges.shape[2]).astype(bf16)


def whole(shape):
    return pl.BlockSpec(shape, lambda s: (0,) * len(shape))


def per_seq(*tail):
    return pl.BlockSpec((1,) + tail, lambda s: (s,) + (0,) * len(tail))


def per_rows(rows, width):
    return pl.BlockSpec((rows, width), lambda s: (s, 0))


def call(kernel, count, in_specs, outs, scratch, *args):
    return pl.pallas_call(
        kernel,
        grid=(count,),
        in_specs=in_specs,
        out_specs=[spec for spec, _unused in outs],
        out_shape=[jax.ShapeDtypeStruct(*made) for _unused, made in outs],
        scratch_shapes=scratch,
        compiler_params=pltpu.CompilerParams(vmem_limit_bytes=VMEM),
    )(*args)


def chain(own, factor, steps, beside):
    entered = jnp.zeros(own.shape, bf16)
    results = []
    for k, (source, target) in enumerate(steps):
        sent = own.astype(bf16) if k == 0 else (own + factor * entered.astype(f32)).astype(bf16)
        came = lax.ppermute(sent, "ctx", [(source, target)])
        for work in beside[k :: len(steps)]:
            results.append(work())
            came, results[-1] = lax.optimization_barrier((came, results[-1]))
        entered = came if k == 0 else entered + came
    return entered, results


def pad_lanes(v):
    return jnp.pad(v, (0, LANES - v.shape[0]))


def finish_kernel(lead, small_ref, dwz_ref, dpx_ref, normed_ref, dz_ref, wx_ref, wz_ref, x_ref, tail_ref, gain_ref, g_ref,
                  gn_ref, wo_ref, oz_ref, ox_ref, os_ref, og_ref, grad_ref, out_ref, *scratch):
    own_z, own, buffers, own_s, buffers_s = scratch[0], scratch[1], scratch[2:6], scratch[6], scratch[7:11]
    own_g, buffers_g = scratch[11], scratch[12:16]
    rows, wbuf, total, back, sem, semz, zsem, wsem, rsem, tail_sem, own_sem = scratch[16:]
    place_of = place()
    z, y, x, c = place_of
    meet(place_of, True)
    count = g_ref.shape[0]
    nz = dwz_ref.shape[-1] // CUT
    widths = [CUT] * nz + [
        min(CUT, dpx_ref.shape[1] - k) for k in range(0, dpx_ref.shape[1], CUT)
    ]
    small, gain = len(widths), len(widths) + 1

    def whole_own(i):
        return {small: own_s, gain: own_g}[i] if i >= small else cut_to(widths[i], own.at[i - nz])

    def own_of(i):
        if i < nz:
            return lambda zz, yy, xx: own_z[i % SLOTS, zz, yy, xx]
        ref = whole_own(i)
        return lambda zz, yy, xx: ref[zz, yy, xx, c]

    def source(i, core):
        if i < nz:
            return dwz_ref.at[:, :, :, core, :, pl.ds(i * CUT, CUT)]
        return whole_own(i).at[:, :, :, core]

    def result(i, value):
        if i >= small:
            {small: os_ref, gain: og_ref}[i][...] = value
        elif i < nz:
            oz_ref[:, i * CUT : (i + 1) * CUT] = value
        else:
            k = (i - nz) * CUT
            ox_ref[:, k : k + widths[i]] = value

    def buffers_of(i):
        if i >= small:
            return [v.at[0] for v in (buffers_s if i == small else buffers_g)]
        return [cut_to(widths[i], v.at[i]) for v in buffers]

    red = Reduction(place_of, source, own_of, buffers_of, result, sem, semz)

    def fetch(i):
        return pltpu.make_async_copy(
            dwz_ref.at[:, :, :, c, :, pl.ds(i * CUT, CUT)], own_z.at[i % SLOTS], zsem.at[i % SLOTS]
        )

    def arrive(i, stage):
        if stage == 0 and i < nz:
            fetch(i).wait()
        red.arrive(i, stage)
        if stage == 0 and i + SLOTS < nz:
            fetch(i + SLOTS).start()

    def weight_and_send(j):
        k, w = j * CUT, widths[nz + j]
        own_j = whole_own(nz + j)
        depth = normed_ref.shape[1] // NZ

        @pl.loop(0, NZ)
        def _(zz):
            value = mm_tn(normed_ref[:, at(zz, depth)], dpx_ref[:, k : k + w])
            own_j[zz] = value.astype(bf16).reshape(2, 2, 2, CUT_ROWS, w)

        red.send(nz + j, 0)

    chunks = [(wz_ref, rows, k, CUT) for k in range(0, wz_ref.shape[1], CUT)]
    chunks += [(wx_ref, dpx_ref, k * CUT, w) for k, w in enumerate(widths[nz:])]

    def stream(q):
        w_ref, _left, k, w = chunks[q]
        return pltpu.make_async_copy(
            w_ref.at[:, pl.ds(k, w)], wbuf.at[q % 2, :, pl.ds(0, w)], wsem.at[q % 2]
        )

    depth_out = wo_ref.shape[0] // 2
    outs = wo_ref.shape[1] // CUT

    def stream_out(q, half):
        return pltpu.make_async_copy(
            wo_ref.at[pl.ds(half * depth_out, depth_out), pl.ds(q * CUT, CUT)], wbuf.at[half],
            wsem.at[half],
        )

    def load_rows(source_ref):
        return pltpu.make_async_copy(source_ref, rows, rsem.at[0])

    def input_chunk(q):
        _w, left, k, w = chunks[q]
        if q == 0:
            load_rows(dz_ref).wait()
            total[...] = jnp.zeros_like(total)
        stream(q).wait()
        total[: left.shape[0]] += mm_nt(left[:, k : k + w], wbuf[q % 2, :, :w])
        if q + 2 < len(chunks):
            stream(q + 2).start()
        if q == nz - 1:
            load_rows(gn_ref).start()

    def output_chunk(q):
        here = slice(q * CUT, (q + 1) * CUT)
        if q == 0:
            load_rows(gn_ref).wait()
            for half in range(2):
                stream_out(q, half).start()
        value = x_ref[:, here].astype(f32)
        for half in range(2):
            stream_out(q, half).wait()
            value = value + MM(rows[:, half * depth_out : (half + 1) * depth_out], wbuf[half])
            if q + 1 < outs:
                stream_out(q + 1, half).start()
        out_ref[:, here] = value.astype(bf16)

    def tail_copy():
        return remote(
            total.at[pl.ds(count, 16)], back, tail_sem.at[0], tail_sem.at[1],
            {"seq": z * 2 + y, "ctx": lax.rem(x * 2 + c + 3, 4)},
        )

    def scaled_rows(rows_ref, lo, hi):
        v = rows_ref[lo:hi].astype(f32)
        return v, lax.rsqrt(jnp.mean(v * v, axis=1, keepdims=True) + EPSILON)

    def norm_weights():
        tail_copy().start()
        sums = jnp.zeros((normed_ref.shape[1], LANES), f32)
        ones = jnp.ones((LANES, LANES), bf16)
        for lo in range(0, count + 16, LANES):
            size = min(LANES, count + 16 - lo)
            v, r = scaled_rows(x_ref, lo, lo + LANES) if lo < count else scaled_rows(tail_ref, 0, 16)
            product = v * r * total[lo : lo + size]
            high = product.astype(bf16)
            rest = (product - high.astype(f32)).astype(bf16)
            sums = sums + mm_tn(high, ones[:size]) + mm_tn(rest, ones[:size])
        own_g[...] = sums.astype(bf16).reshape(own_g.shape)
        red.send(gain, 0)

    def norm_rows():
        tail_copy().wait()
        seqs = tail_ref.shape[0] // 8
        length = count // seqs
        for s in range(seqs):
            total[(s + 1) * length - 8 : (s + 1) * length] += back[8 * s : 8 * s + 8]
        for lo in range(0, count, LANES):
            v, r = scaled_rows(x_ref, lo, lo + LANES)
            scaled = gain_ref[0:1] * total[lo : lo + LANES]
            mean = jnp.mean(v * scaled, axis=1, keepdims=True)
            value = g_ref[lo : lo + LANES].astype(f32) + r * (scaled - v * (r * r) * mean)
            grad_ref[lo : lo + LANES] = value.astype(bf16)

    for i in range(nz):
        red.send(i, 0)
    for i in range(SLOTS):
        fetch(i).start()
    small_copy = pltpu.make_async_copy(small_ref, own_s, own_sem.at[0])
    small_copy.start()
    load_rows(dz_ref).start()
    for q in range(2):
        stream(q).start()
    order = [*range(gain + 1)]
    work = [[partial(weight_and_send, j)] for j in range(small - nz)]
    step = -(-len(chunks) // 5)
    work += [
        [partial(input_chunk, q) for q in range(k, min(k + step, len(chunks)))]
        for k in range(0, len(chunks), step)
    ]
    work += [[norm_weights], [norm_rows]] + [[partial(output_chunk, q)] for q in range(outs)]
    work[1] = work[1] + [small_copy.wait, partial(red.send, small, 0)]
    for t in range(max(len(order) + lead[-1], len(work))):
        for job in work[t] if t < len(work) else []:
            job()
        for stage in reversed(range(4)):
            if 0 <= t - lead[stage] < len(order):
                arrive(order[t - lead[stage]], stage)
    for i in order:
        red.drain(i)


def finish(small, dw_z, dpx, normed, dz, w_x, w_z, x, tail, gain, g, gn, w_out, lead=LEAD):
    small = small.reshape((NZ, 2, 2, 2, -1, small.shape[-1]))
    dw_z = dw_z.reshape((NZ, 2, 2, 2, -1, dw_z.shape[-1]))
    nx = pl.cdiv(dpx.shape[1], CUT)
    p = nx + dw_z.shape[-1] // CUT
    ss = small.shape[-2:]
    far, near = pl.BlockSpec(memory_space=pl.ANY), pl.BlockSpec(memory_space=pltpu.VMEM)
    return pl.pallas_call(
        partial(finish_kernel, tuple(lead)),
        out_shape=[
            jax.ShapeDtypeStruct((CUT_ROWS, dw_z.shape[-1]), f32),
            jax.ShapeDtypeStruct((CUT_ROWS, dpx.shape[1]), f32),
            jax.ShapeDtypeStruct(ss, f32),
            jax.ShapeDtypeStruct((CUT_ROWS, LANES), f32),
            jax.ShapeDtypeStruct(g.shape, bf16),
            jax.ShapeDtypeStruct(g.shape, bf16),
        ],
        in_specs=[far, far, near, near, far, far, far, near, near, near, near, far, far],
        out_specs=[near] * 6,
        scratch_shapes=[
            pltpu.VMEM((SLOTS, NZ, 2, 2, CUT_ROWS, CUT), bf16),
            pltpu.VMEM((nx, NZ, 2, 2, 2, CUT_ROWS, CUT), bf16),
        ]
        + reduction_buffers(p, (CUT_ROWS, CUT), bf16)
        + [pltpu.VMEM(small.shape, f32)] + reduction_buffers(1, ss, f32)
        + [pltpu.VMEM((NZ, 2, 2, 2, CUT_ROWS, LANES), bf16)]
        + reduction_buffers(1, (CUT_ROWS, LANES), bf16)
        + [
            pltpu.VMEM(dz.shape, bf16), pltpu.VMEM((2, w_x.shape[0], CUT), bf16),
            pltpu.VMEM(normed.shape, f32), pltpu.VMEM(tail.shape, f32),
        ]
        + reduction_semaphores(p + 2)
        + [pltpu.SemaphoreType.DMA((SLOTS,)), pltpu.SemaphoreType.DMA((2,)),
           pltpu.SemaphoreType.DMA((1,)), pltpu.SemaphoreType.DMA((2,)), pltpu.SemaphoreType.DMA((1,))],
        compiler_params=pltpu.CompilerParams(
            collective_id=1, has_side_effects=True, vmem_limit_bytes=FINISH_VMEM
        ),
    )(small, dw_z, dpx, normed, dz, w_x, w_z, x, tail, gain, g, gn, w_out)


def local(tokens, norm_gain, input_weight, conv_w, conv_b, dt_bias, a_log, d_skip, gate_gain,
          output_weight, segments, cotangent):
    seqs, length, width = tokens.shape
    n_ctx = lax.axis_size("ctx")
    n_all = n_ctx * lax.axis_size("seq")
    count = seqs * length
    shares = [norm_gain.shape[0], gate_gain.shape[0], CONV * conv_b.shape[0], conv_b.shape[0]]
    cuts = [sum(shares[: i + 1]) for i in range(3)]
    packed = jnp.concatenate([norm_gain, gate_gain, conv_w.reshape(-1), conv_b])
    onward = [(i, i + 1) for i in range(n_ctx - 1)]
    tail = jnp.pad(tokens[:, length - (CONV - 1) :], ((0, 0), (8 - (CONV - 1), 0), (0, 0)))
    tail_ids = jnp.pad(
        segments[:, length - (CONV - 1) :].astype(bf16), ((0, 0), (0, width - (CONV - 1)))
    )
    tail = jnp.concatenate([tail_ids[:, None], tail[:, 1:]], axis=1).reshape(seqs * 8, width)
    torus = lax.axis_size("seq") == 2 * NZ and n_ctx == 4 and norm_gain.shape[0] == CUT_ROWS
    spare = ((0, 0), (0, LANES - HEADS))
    w_z, w_x = input_weight[:, :INNER], jnp.pad(input_weight[:, INNER:], spare)
    if torus:
        size = packed.shape[0]
        small = jnp.pad(packed, (0, 16 * LANES - size)).reshape(16, LANES)
        w_out = lax.all_gather(output_weight, BOTH, axis=0, tiled=True)
        w_z = lax.all_gather(w_z, BOTH, axis=0, tiled=True)
        w_x, packed, tail = gather_all(
            [w_x, small], tail,
            [(1, 0, 16, True)]
            + [(0, 16 * k, 16, k % 2 == 0) for k in range(3)]
,
        )
        w_x, w_z, w_out = (w.reshape(-1, w.shape[-1]) for w in (w_x, w_z, w_out))
        packed = packed.reshape(n_all, -1)[:, :size]
    else:
        packed = lax.all_gather(packed, BOTH, axis=0)
        tail = lax.ppermute(tail, "ctx", onward)
        w_in, w_out = (
            lax.all_gather(w, BOTH, axis=0, tiled=True) for w in (input_weight, output_weight)
        )
        w_z, w_x = w_in[:, :INNER], jnp.pad(w_in[:, INNER:], spare)
    norm_full, gate_full, conv_w_full, conv_b_full = jnp.split(packed.astype(f32), cuts, axis=1)
    norm_full = norm_full.reshape(1, -1)
    gate_full = gate_full.reshape(1, -1)
    conv_b_full = conv_b_full.reshape(1, -1)
    conv_w_full = conv_w_full.reshape(n_all, CONV, -1).transpose(1, 0, 2).reshape(CONV, -1)

    tail = tail.reshape(seqs, 8, width)
    tail_ids = jnp.where(
        lax.axis_index("ctx") == 0, -1, tail[:, 0, : CONV - 1].astype(jnp.int32)
    )
    tail = jnp.pad(tail[:, 8 - (CONV - 1) :], ((0, 0), (8 - (CONV - 1), 0), (0, 0)))
    tail = jnp.where(lax.axis_index("ctx") == 0, 0, tail)
    tail = tail.reshape(seqs * 8, width)
    x_all = jnp.concatenate([tokens.reshape(count, width), tail])
    x_all = x_all.astype(f32)
    r_all = lax.rsqrt(jnp.mean(x_all * x_all, axis=-1, keepdims=True) + EPSILON)
    normed = (x_all * r_all * norm_full).astype(bf16)

    ids_ext = jnp.concatenate([tail_ids, segments], axis=1)
    flags = [
        segments == ids_ext[:, CONV - 1 - k : CONV - 1 - k + length] for k in range(1, CONV)
    ] + [segments == ids_ext[:, CONV - 2 : CONV - 1], segments == segments[:, -1:]]
    cols = jnp.stack([f.astype(f32) for f in flags] + [segments.astype(f32)], axis=-1)
    cols = jnp.pad(cols, ((0, 0), (0, 0), (0, LANES - cols.shape[-1])))
    rows = jnp.pad(segments.astype(f32)[:, None], ((0, 0), (0, 7), (0, 0)))
    heads = jnp.pad(jnp.stack([pad_lanes(dt_bias), pad_lanes(a_log)]), ((0, 6), (0, 0)))
    lanes = jnp.concatenate([gate_full, jnp.repeat(d_skip, HEADDIM)[None]])
    lanes = jnp.pad(lanes, ((0, 6), (0, 0)))
    conv_w8 = jnp.pad(conv_w_full, ((0, 8 - CONV), (0, 0)))
    conv_b8 = jnp.pad(conv_b_full, ((0, 7), (0, 0)))

    px = MM(normed, w_x).astype(bf16)
    px_width, used = CHANNELS + LANES, CHANNELS + HEADS
    tail_spec = pl.BlockSpec((16, px_width), lambda s: (count // 16, 0))
    act, tok, cst, fresh = call(
        before_kernel, seqs,
        [per_rows(length, px_width), tail_spec, whole((8, CHANNELS)), whole((8, CHANNELS)),
         per_seq(length, LANES), whole((8, LANES))],
        [(per_seq(length, CHANNELS), ((seqs, length, CHANNELS), f32)),
         (per_seq(length, 2 * LANES), ((seqs, length, 2 * LANES), f32)),
         (per_seq(HEADS, length), ((seqs, HEADS, length), f32)),
         (per_seq(INNER, STATE), ((seqs, INNER, STATE), f32))],
        [pltpu.VMEM((length + 8, LANES), f32)],
        px, px, conv_w8, conv_b8, cols, heads,
    )
    carried = cols[:, length - 1, 3]
    kept = jnp.exp(cst[:, :, length - 1]) * carried[:, None]
    kept = jnp.repeat(kept, HEADDIM, axis=1)[..., None]
    g2 = cotangent.reshape(count, width)

    def gate_gradient():
        return lax.dot_general(g2, w_out, (((1,), (1,)), ((), ())), preferred_element_type=f32)

    def within():
        [y] = call(
            within_kernel, seqs,
            [per_seq(length, CHANNELS), per_seq(length, 2 * LANES), per_seq(HEADS, length),
             per_seq(length, LANES), per_seq(8, length)],
            [(per_seq(length, INNER), ((seqs, length, INNER), f32))],
            [pltpu.VMEM((length, length), f32), pltpu.VMEM((length, length), f32)],
            act, tok, cst, cols, rows,
        )
        return y

    def gates():
        return MM(normed[:count], w_z).astype(bf16)

    entering, (dgn, y, pz) = chain(fresh, kept, onward, (gate_gradient, within, gates))
    stayed = kept * entering.astype(f32)
    gn, dz, dy, dstate, dqueries, ddecay, sums = call(
        gate_kernel, seqs,
        [per_rows(length, INNER), per_seq(length, CHANNELS), per_seq(length, 2 * LANES),
         per_seq(length, LANES), per_seq(length, INNER), per_seq(INNER, STATE),
         per_rows(length, INNER), whole((8, INNER))],
        [(per_rows(length, INNER), ((count, INNER), bf16)),
         (per_rows(length, INNER), ((count, INNER), bf16)),
         (per_seq(length, INNER), ((seqs, length, INNER), bf16)),
         (per_seq(INNER, STATE), ((seqs, INNER, STATE), f32)),
         (per_seq(length, STATE), ((seqs, length, STATE), f32)),
         (per_seq(length, LANES), ((seqs, length, LANES), f32)),
         (per_seq(8, INNER), ((seqs, 8, INNER), f32))],
        [pltpu.VMEM((length, INNER), f32), pltpu.VMEM((length, STATE), f32)],
        pz, act, tok, cols, y, entering, dgn, lanes,
    )
    tn = (((0,), (0,)), ((), ()))

    def output_weights():
        return lax.dot_general(gn, g2, tn, preferred_element_type=f32).astype(bf16)

    def scan_back():
        return call(
            scan_back_kernel, seqs,
            [per_seq(length, CHANNELS), per_seq(length, 2 * LANES), per_seq(HEADS, length),
             per_seq(length, LANES), per_seq(8, length), per_seq(length, INNER)],
            [(per_seq(length, INNER), ((seqs, length, INNER), f32)),
             (per_seq(length, 2 * STATE), ((seqs, length, 2 * STATE), f32))],
            [pltpu.VMEM((length, length), f32)] * 3,
            act, tok, cst, cols, rows, dy,
        )

    def gate_weights():
        return lax.dot_general(normed[:count], dz, tn, preferred_element_type=f32).astype(bf16)

    later, (dw_out, (dx, dbc), dw_z) = chain(
        dstate, kept, [(b, a) for a, b in reversed(onward)], (output_weights, scan_back, gate_weights)
    )
    dpx, dconv, dheads = call(
        after_kernel, seqs,
        [per_rows(length, px_width), tail_spec, whole((8, CHANNELS)), whole((8, CHANNELS)),
         per_seq(length, LANES), whole((8, LANES)), per_seq(length, CHANNELS),
         per_seq(length, 2 * LANES), whole((8, INNER)), per_seq(length, INNER),
         per_seq(length, INNER), per_seq(length, 2 * STATE), per_seq(length, STATE),
         per_seq(length, LANES), per_seq(INNER, STATE), per_seq(INNER, STATE)],
        [(whole((count + seqs * 8, px_width)), ((count + seqs * 8, px_width), bf16)),
         (per_seq(8, CHANNELS), ((seqs, 8, CHANNELS), f32)),
         (per_seq(8, LANES), ((seqs, 8, LANES), f32))],
        [pltpu.VMEM((length + 8, LANES), f32), pltpu.VMEM((CONV - 1, length + 16, LANES), f32),
         pltpu.VMEM((length, CHANNELS), f32), pltpu.VMEM((length, LANES), f32),
         pltpu.VMEM((length, LANES), f32), pltpu.VMEM((length, STATE), f32), pltpu.VMEM((LANES, LANES), f32),
         pltpu.VMEM((8, INNER), f32), pltpu.VMEM((seqs, 8, px_width), f32)],
        px, px, conv_w8, conv_b8, cols, heads, act, tok, lanes, dy, dx, dbc, dqueries, ddecay,
        later, stayed,
    )
    sums = jnp.sum(sums, axis=0)
    dconv = jnp.sum(dconv, axis=0)
    dheads = jnp.sum(dheads, axis=0)
    d_skip_sum = jnp.sum(sums[1].reshape(HEADS, HEADDIM), axis=1)
    split = [sums[0].reshape(n_all, -1),
             dconv[:CONV].reshape(CONV, n_all, -1).transpose(1, 0, 2).reshape(n_all, -1),
             dconv[CONV].reshape(n_all, -1)]
    shared = jnp.concatenate([dheads[0, :HEADS], dheads[1, :HEADS], d_skip_sum])
    split = jnp.concatenate(split, axis=1)
    share = split.shape[1]
    if torus:
        fill = 8 * LANES - share - shared.shape[0]
        split = [split, jnp.broadcast_to(shared, (n_all,) + shared.shape), jnp.zeros((n_all, fill), f32)]
        dw_z, dw_x, mine, d_norm, input_grad, output = finish(
            jnp.concatenate(split, axis=1).reshape(n_all, 8, LANES), dw_z, dpx, normed, dz,
            w_x, w_z, tokens.reshape(count, width), tail, jnp.pad(norm_full, ((0, 7), (0, 0))), g2,
            gn, w_out,
        )
        d_norm = d_norm[:, 0]
        dw_out = lax.psum_scatter(dw_out, BOTH, scatter_dimension=0, tiled=True).astype(f32)
        dw_in = jnp.concatenate([dw_z, dw_x[:, :used]], axis=1)
        mine = mine.reshape(-1)
        mine, shared = mine[:share], mine[share : share + shared.shape[0]]
    else:
        nt = (((1,), (1,)), ((), ()))
        dnormed_x = lax.dot_general(dpx, w_x, nt, preferred_element_type=f32)
        dnormed = dnormed_x[:count] + lax.dot_general(dz, w_z, nt, preferred_element_type=f32)
        back = dnormed_x[count:].reshape(seqs, 8, width)[:, 8 - (CONV - 1) :].astype(bf16)
        back = lax.ppermute(back, "ctx", [(b, a) for a, b in onward])
        dw_x = lax.dot_general(normed, dpx, tn, preferred_element_type=f32).astype(bf16)
        x, r = x_all[:count], r_all[:count]
        d_gain = jnp.sum(x * r * dnormed, axis=0) + jnp.sum(
            x_all[count:] * r_all[count:] * dnormed_x[count:], axis=0
        )
        back, d_gain, dw_x = lax.optimization_barrier((back, d_gain, dw_x))
        back = jnp.pad(back.astype(f32), ((0, 0), (length - (CONV - 1), 0), (0, 0)))
        scaled = norm_full * (dnormed + back.reshape(count, width))
        dx_in = r * (scaled - x * (r * r) * jnp.mean(x * scaled, axis=-1, keepdims=True))
        input_grad = (g2.astype(f32) + dx_in).astype(bf16)
        output = (x_all[:count] + MM(gn, w_out)).astype(bf16)
        dw_in = jnp.concatenate([dw_z, dw_x[:, :used]], axis=1)
        dw_out, dw_in = (
            lax.psum_scatter(v.astype(f32), BOTH, scatter_dimension=0, tiled=True)
            for v in (dw_out, dw_in)
        )
        every = lax.psum(jnp.concatenate([split.reshape(-1), shared, d_gain]), BOTH)
        me = lax.axis_index("seq") * n_ctx + lax.axis_index("ctx")
        d_norm = lax.dynamic_slice(every[-width:], (me * shares[0],), (shares[0],))
        mine = lax.dynamic_slice(every, (me * share,), (share,))
        shared = every[n_all * share : n_all * share + shared.shape[0]]
    d_gate, d_conv_w, d_conv_b = jnp.split(mine, [v - cuts[0] for v in cuts[1:]])
    d_bias, d_alog, d_skips = jnp.split(shared, 3)
    return (
        output.reshape(tokens.shape), input_grad.reshape(tokens.shape), d_norm, dw_in,
        d_conv_w.reshape(CONV, -1), d_conv_b, d_bias, d_alog, d_skips, d_gate, dw_out,
    )


def solution(mesh):
    split = P(BOTH)
    rows = P(BOTH, None)
    seq = P("seq", "ctx", None)
    in_specs = (seq, split, rows, P(None, BOTH), split, P(), P(), P(), split, rows,
                P("seq", "ctx"), seq)
    out_specs = (seq, seq, split, rows, P(None, BOTH), split, P(), P(), P(), split, rows)
    return jax.shard_map(local, mesh=mesh, in_specs=in_specs, out_specs=out_specs, check_vma=False)
```

```python
from functools import partial

import jax
import jax.numpy as jnp
from jax import lax
from jax.experimental import pallas as pl
from jax.experimental.pallas import tpu as pltpu
from jax.sharding import PartitionSpec as P

HEADS = 48
STATE = 128
HEADDIM = 64
CONV = 4
INNER = HEADS * HEADDIM
CHANNELS = INNER + 2 * STATE
GROUP = 8
GROUPS = HEADS // GROUP
WIDTH = GROUP * HEADDIM
LANES = 128
EPSILON = 1e-05
VMEM = 60 * 1024 * 1024
FINISH_VMEM = 62 * 1024 * 1024 - 512 * 1024
BOTH = ("seq", "ctx")
FAR = -1e30
f32 = jnp.float32
bf16 = jnp.bfloat16
MM = partial(jnp.dot, preferred_element_type=f32)


def mm_nt(a, b):
    return lax.dot_general(a, b, (((1,), (1,)), ((), ())), preferred_element_type=f32)


def mm_tn(a, b):
    return lax.dot_general(a, b, (((0,), (0,)), ((), ())), preferred_element_type=f32)


def sigmoid(v):
    return 0.5 + 0.5 * jnp.tanh(0.5 * v)


def at(j, width):
    return pl.ds(pl.multiple_of(j * width, width), width)


def low_half(rows):
    return lax.broadcasted_iota(jnp.int32, (rows, LANES), 1) < HEADDIM


def to_front(columns, g):
    return pltpu.roll(columns, lax.rem(LANES - GROUP * g, LANES), 1)


def spread(front, pair, low):
    return jnp.where(low, front[:, 2 * pair : 2 * pair + 1], front[:, 2 * pair + 1 : 2 * pair + 2])


def head_sums(product, g):
    lane = lax.broadcasted_iota(jnp.int32, (WIDTH, LANES), 1)
    row = lax.broadcasted_iota(jnp.int32, (WIDTH, LANES), 0)
    pick = jnp.where(lane == row // HEADDIM, 1.0, 0.0).astype(bf16)
    high = product.astype(bf16)
    rest = (product - high.astype(f32)).astype(bf16)
    return pltpu.roll(MM(high, pick) + MM(rest, pick), GROUP * g, 1)


def taps(px_ref, tail, j, w_ref, b_ref, masks, ext):
    here = at(j, LANES)
    length = px_ref.shape[0]
    own = px_ref[:, here].astype(f32)
    ext[0:8, :] = tail
    ext[8 : 8 + length, :] = own
    inputs = [own] + [
        masks[k - 1] * ext[8 - k : 8 - k + length, :] for k in range(1, CONV)
    ]
    out = b_ref[0:1, here]
    for k in range(CONV):
        out = out + w_ref[k : k + 1, here] * inputs[k]
    return out, inputs


def tail_of(tail_ref, s, here):
    both = tail_ref[:, here].astype(f32)
    return jnp.where(s == 0, both[0:8], both[8:16])


def lane_masks(cols_ref, length):
    return [
        jnp.broadcast_to(cols_ref[0, :, k : k + 1], (length, LANES)) for k in range(CONV - 1)
    ]


NZ = 4


def place():
    seq, ctx = lax.axis_index("seq"), lax.axis_index("ctx")
    return seq // 2, lax.rem(seq, 2), ctx // 2, lax.rem(ctx, 2)


def device(z, y, x, c):
    return {"seq": z * 2 + y, "ctx": x * 2 + c}


def greet(z, y, x, c, more=0):
    barrier = pltpu.get_barrier_semaphore()
    others = [device(z, y, x, 1 - c), device(z, y, 1 - x, c), device(z, 1 - y, x, c)]
    others += [device(lax.rem(z + d, NZ), y, x, c) for d in range(1, NZ)]
    for other in others:
        pl.semaphore_signal(barrier, inc=1, device_id=other, device_id_type=pl.DeviceIdType.MESH)
    pl.semaphore_wait(barrier, len(others) + more)


def remote(src, dst, send, recv, target):
    return pltpu.make_async_remote_copy(
        src_ref=src, dst_ref=dst, send_sem=send, recv_sem=recv, device_id=target,
        device_id_type=pl.DeviceIdType.MESH,
    )


def gather_kernel(units, n, *refs):
    ins, outs, land, (tail_land, send, recv, local, store, tail_sem) = (
        refs[: n + 1], refs[n + 1 : 2 * n + 2], refs[2 * n + 2 : 3 * n + 2], refs[3 * n + 2 :]
    )
    x_first = [first for _array, _row, _rows, first in units]
    z, y, x, c = place()
    ctx = x * 2 + c
    after, before = lax.rem(ctx + 1, 4), lax.rem(ctx + 3, 4)
    barrier = pltpu.get_barrier_semaphore()
    for other in (after, before):
        pl.semaphore_signal(
            barrier, inc=1, device_id={"seq": z * 2 + y, "ctx": other},
            device_id_type=pl.DeviceIdType.MESH,
        )
    greet(z, y, x, c, 2)
    started, stored = [], []

    def shard(u):
        a, row, rows, _first = units[u]
        return ins[a].at[pl.ds(row, rows)]

    def slot_of(u, *at, into=None):
        a, row, rows, _first = units[u]
        return (land if into is None else into)[a].at[at + (pl.ds(row, rows),)]

    def number(u, kind, index):
        first = "x" if x_first[u] else "y"
        base = 0 if kind == "z" else 3 if kind == first else 15 if kind == "c" else 7
        return base + (index - 1 if kind == "z" else index)

    def push(u, zz, yy, xx, kind, index):
        slot = slot_of(u, zz, yy, xx, c)
        if kind == "z":
            target = device(lax.rem(z + index, NZ), y, x, c)
        else:
            flip = [1 - v if k == kind else v for k, v in (("y", y), ("x", x), ("c", c))]
            target = device(z, *flip)
        k = number(u, kind, index)
        copy = remote(slot, slot, send.at[u, k], recv.at[u, k], target)
        copy.start()
        started.append(copy)

    def came(u, zz, yy, xx, cc, kind, index):
        slot = slot_of(u, zz, yy, xx, cc)
        k = number(u, kind, index)
        remote(slot, slot, send.at[u, k], recv.at[u, k], device(z, y, x, 1 - c)).wait_recv()
        keep = pltpu.make_async_copy(slot, slot_of(u, zz, yy, xx, cc, into=outs), store.at[u, k])
        keep.start()
        stored.append(keep)

    back = [lax.rem(z + NZ - d, NZ) for d in range(NZ)]
    axes = [("x", "y") if first else ("y", "x") for first in x_first]
    every = range(len(units))
    ring = remote(
        ins[n], tail_land, tail_sem.at[0], tail_sem.at[1], {"seq": z * 2 + y, "ctx": after}
    )
    ring.start()
    for u in every:
        pltpu.make_async_copy(shard(u), slot_of(u, z, y, x, c), local.at[u]).start()

    def open_unit(u):
        a, b = axes[u]
        slot = slot_of(u, z, y, x, c)
        pltpu.make_async_copy(shard(u), slot, local.at[u]).wait()
        for d in (1, 3, 2):
            push(u, z, y, x, "z", d)
        for kind in (b, a, "c"):
            push(u, z, y, x, kind, 0)
        keep = pltpu.make_async_copy(slot, slot_of(u, z, y, x, c, into=outs), local.at[u])
        keep.start()
        stored.append(keep)

    def pass_on(u):
        a, b = axes[u]
        yy, xx = (y, 1 - x) if a == "x" else (1 - y, x)
        for d in range(1, NZ + 1):
            if d < NZ:
                came(u, back[d], y, x, c, "z", d)
                for kind in (b, a, "c"):
                    push(u, back[d], y, x, kind, d)
            came(u, back[d - 1], yy, xx, c, a, d - 1)
            push(u, back[d - 1], yy, xx, b, NZ + d - 1)
            push(u, back[d - 1], yy, xx, "c", NZ + d - 1)

    def cross(u):
        a, b = axes[u]
        for half in range(2):
            yy, xx = (1 - y, x) if b == "y" else (y, 1 - x)
            if half:
                yy, xx = 1 - y, 1 - x
            for d in range(NZ):
                came(u, back[d], yy, xx, c, b, NZ * half + d)
                push(u, back[d], yy, xx, "c", 2 * NZ + NZ * half + d)

    def finish(u):
        a, b = axes[u]
        for k in range(16):
            away = {a: (k // NZ) % 2, b: k // (2 * NZ)}
            came(u, back[k % NZ], 1 - y if away["y"] else y, 1 - x if away["x"] else x, 1 - c, "c", k)

    for t in range(-AHEAD, len(units) + 4):
        if 0 <= t + AHEAD < len(units):
            open_unit(t + AHEAD)
        if 0 <= t < len(units):
            pass_on(t)
        if 0 <= t - 2 < len(units):
            cross(t - 2)
        if 0 <= t - 4 < len(units):
            finish(t - 4)
    ring.wait_recv()
    keep = pltpu.make_async_copy(tail_land, outs[n], tail_sem.at[2])
    keep.start()
    keep.wait()
    ring.wait_send()
    for copy in started:
        copy.wait_send()
    for keep in stored:
        keep.wait()


def gather_all(shards, tail, units):
    n, m = len(shards), len(units)
    full = [(NZ, 2, 2, 2) + v.shape for v in shards]
    return pl.pallas_call(
        partial(gather_kernel, tuple(units), n),
        out_shape=[jax.ShapeDtypeStruct(f, v.dtype) for f, v in zip(full, shards)]
        + [jax.ShapeDtypeStruct(tail.shape, tail.dtype)],
        in_specs=[pl.BlockSpec(memory_space=pl.ANY)] * (n + 1),
        out_specs=[pl.BlockSpec(memory_space=pl.ANY)] * (n + 1),
        scratch_shapes=[pltpu.VMEM(f, v.dtype) for f, v in zip(full, shards)] + [
            pltpu.VMEM(tail.shape, tail.dtype),
            pltpu.SemaphoreType.DMA((m, 31)), pltpu.SemaphoreType.DMA((m, 31)),
            pltpu.SemaphoreType.DMA((m,)), pltpu.SemaphoreType.DMA((m, 31)),
            pltpu.SemaphoreType.DMA((3,)),
        ],
        compiler_params=pltpu.CompilerParams(
            collective_id=0, has_side_effects=True, vmem_limit_bytes=VMEM
        ),
    )(*shards, tail)


CUT_ROWS, CUT = 48, 512
SLOTS = 3
LEAD = (0, 5, 7, 9)
AHEAD = 4


def meet(place_of, ring):
    z, y, x, c = place_of
    if ring:
        barrier = pltpu.get_barrier_semaphore()
        for step in (1, 3):
            pl.semaphore_signal(
                barrier, inc=1, device_id={"seq": z * 2 + y, "ctx": lax.rem(x * 2 + c + step, 4)},
                device_id_type=pl.DeviceIdType.MESH,
            )
    greet(z, y, x, c, 2 if ring else 0)


class Reduction:
    def __init__(self, place_of, source, own, buffers, result, sem, semz):
        self.place, self.source, self.own, self.buffers = place_of, source, own, buffers
        self.result, self.sem, self.semz = result, sem, semz

    def copies(self, i, stage):
        z, y, x, c = self.place
        core, first, second, last = self.buffers(i)
        x_first = i % 2 == 0
        along_x, along_y = device(z, y, 1 - x, c), device(z, 1 - y, x, c)
        if stage == 0:
            moves = [(self.source(i, 1 - c), core, device(z, y, x, 1 - c))]
        elif stage == 1:
            src = core.at[:, :, 1 - x] if x_first else core.at[:, 1 - y]
            moves = [(src, first, along_x if x_first else along_y)]
        elif stage == 2:
            src = first.at[:, 1 - y] if x_first else first.at[:, 1 - x]
            moves = [(src, second, along_y if x_first else along_x)]
        else:
            moves = []
            for d in range(1, NZ):
                zz = lax.rem(z + d, NZ)
                moves.append((second.at[zz], last.at[z], device(zz, y, x, c)))
        made = []
        for d, (src, dst, to) in enumerate(moves):
            if stage < 3:
                sems = self.sem.at[2 * stage, i], self.sem.at[2 * stage + 1, i]
            else:
                sems = self.semz.at[0, d, i], self.semz.at[1, d, i]
            made.append(remote(src, dst, *sems, to))
        return made

    def send(self, i, stage):
        for copy in self.copies(i, stage):
            copy.start()

    def drain(self, i):
        for stage in range(4):
            for copy in self.copies(i, stage):
                copy.wait_send()

    def arrive(self, i, stage):
        z, y, x, c = self.place
        core, first, second, last = self.buffers(i)
        x_first = i % 2 == 0
        if stage < 3:
            landed = (core, first, second)[stage]
            remote(
                landed, landed, self.sem.at[2 * stage, i], self.sem.at[2 * stage + 1, i],
                device(z, y, x, 1 - c),
            ).wait_recv()
        if stage == 0:
            own = self.own(i)

            @pl.loop(0, NZ)
            def _(zz):
                for yy in range(2):
                    for xx in range(2):
                        core[zz, yy, xx] = core[zz, yy, xx] + own(zz, yy, xx)

        elif stage == 1:

            @pl.loop(0, NZ)
            def _(zz):
                for o in range(2):
                    first[zz, o] = first[zz, o] + (core[zz, o, x] if x_first else core[zz, y, o])

        elif stage == 2:

            @pl.loop(0, NZ)
            def _(zz):
                second[zz] = second[zz] + (first[zz, y] if x_first else first[zz, x])

            last[z] = second[z]
        else:
            for d in range(1, NZ):
                landed = last.at[lax.rem(z + NZ - d, NZ)]
                remote(
                    landed, landed, self.semz.at[0, d - 1, i], self.semz.at[1, d - 1, i],
                    device(z, y, x, 1 - c),
                ).wait_recv()
            value = last[0].astype(f32)
            for zz in range(1, NZ):
                value = value + last[zz].astype(f32)
            self.result(i, value)
        if stage < 3:
            self.send(i, stage + 1)


def reduction_buffers(count, shape, dtype):
    return [pltpu.VMEM((count,) + d + shape, dtype) for d in ((NZ, 2, 2), (NZ, 2), (NZ,), (NZ,))]


def reduction_semaphores(count):
    return [pltpu.SemaphoreType.DMA((6, count)), pltpu.SemaphoreType.DMA((2, NZ - 1, count))]


def cut_to(width, ref):
    if ref.shape[-1] == width:
        return ref
    return ref.at[(slice(None),) * (len(ref.shape) - 1) + (pl.ds(0, width),)]


def before_kernel(px_ref, tail_ref, w_ref, b_ref, cols_ref, heads_ref,
                  act_ref, tok_ref, cst_ref, fresh_ref, ext):
    s = pl.program_id(0)
    length = px_ref.shape[0]
    masks = lane_masks(cols_ref, length)

    @pl.loop(0, CHANNELS // LANES)
    def _(j):
        here = at(j, LANES)
        conv, _unused = taps(px_ref, tail_of(tail_ref, s, here), j, w_ref, b_ref, masks, ext)
        act_ref[0, :, here] = conv * sigmoid(conv)

    raw = px_ref[:, CHANNELS : CHANNELS + HEADS].astype(f32) + heads_ref[0:1, :HEADS]
    step = jnp.maximum(raw, 0.0) + jnp.log1p(jnp.exp(-jnp.abs(raw)))
    step = jnp.concatenate([step, jnp.zeros((length, LANES - HEADS), f32)], axis=1)
    rate = -step * jnp.exp(heads_ref[1:2, :])
    before = (
        lax.broadcasted_iota(jnp.int32, (length, length), 0)
        >= lax.broadcasted_iota(jnp.int32, (length, length), 1)
    ).astype(f32)
    decay = jnp.dot(before, rate, precision=lax.Precision.HIGHEST, preferred_element_type=f32)
    tok_ref[0, :, 0:LANES] = step
    tok_ref[0, :, LANES : 2 * LANES] = decay
    cst_ref[0] = decay.T[:HEADS]
    toward = jnp.exp(decay[length - 1 : length] - decay) * step * cols_ref[0, :, 4:5]
    keys = act_ref[0, :, INNER : INNER + STATE].astype(bf16)
    low = low_half(length)

    @pl.loop(0, GROUPS)
    def _(g):
        front = to_front(toward, g)
        scaled = []
        for pair in range(GROUP // 2):
            here = pl.ds(pl.multiple_of(g * WIDTH + pair * LANES, LANES), LANES)
            scaled.append((act_ref[0, :, here] * spread(front, pair, low)).astype(bf16))
        left = mm_tn(jnp.concatenate(scaled, axis=1), keys)
        fresh_ref[0, at(g, WIDTH), :] = left.astype(bf16)


def bias_of(ids_col, ids_row, transposed):
    shape = (ids_col.shape[0], ids_row.shape[1])
    down = lax.broadcasted_iota(jnp.int32, shape, 0)
    across = lax.broadcasted_iota(jnp.int32, shape, 1)
    order = (down <= across) if transposed else (down >= across)
    return jnp.where(order & (ids_col == ids_row), 0.0, FAR)


def within_kernel(act_ref, tok_ref, cst_ref, cols_ref, rows_ref, y_ref, cross, bias):
    length = act_ref.shape[1]
    half = length // 2
    cross[...] = mm_nt(
        act_ref[0, :, INNER + STATE :].astype(bf16),
        act_ref[0, :, INNER : INNER + STATE].astype(bf16),
    )
    bias[...] = bias_of(cols_ref[0, :, 5:6], rows_ref[0, 0:1, :], False)
    low = low_half(length)

    @pl.loop(0, GROUPS)
    def _(g):
        step = to_front(tok_ref[0, :, 0:LANES], g)
        decay = to_front(tok_ref[0, :, LANES : 2 * LANES], g)
        rows = cst_ref[0, at(g, GROUP), :]
        for pair in range(GROUP // 2):
            here = pl.ds(pl.multiple_of(g * WIDTH + pair * LANES, LANES), LANES)
            scaled = act_ref[0, :, here] * spread(step, pair, low)
            top, bottom = 0.0, 0.0
            for which in range(2):
                h = 2 * pair + which
                mine = jnp.where(low == (which == 0), scaled, 0.0).astype(bf16)
                col, row = decay[:, h : h + 1], rows[h : h + 1, :]
                w = jnp.exp(col[:half] - row[:, :half] + bias[:half, :half])
                top = top + MM((cross[:half, :half] * w).astype(bf16), mine[:half])
                w = jnp.exp(col[half:] - row + bias[half:, :])
                bottom = bottom + MM((cross[half:, :] * w).astype(bf16), mine)
            y_ref[0, :half, here] = top
            y_ref[0, half:, here] = bottom


def gate_kernel(z_ref, act_ref, tok_ref, cols_ref, y_ref, state_ref, dgn_ref, lanes_ref,
                gn_ref, dz_ref, dy_ref, dstate_ref, q_ref, dq_ref, sums_ref, total, queries_acc):
    length = act_ref.shape[1]
    low = low_half(length)
    enter = jnp.exp(tok_ref[0, :, LANES : 2 * LANES]) * cols_ref[0, :, 3:4]
    queries = act_ref[0, :, INNER + STATE :].astype(bf16)

    def first(g, carry):
        square, inner = carry
        front = to_front(enter, g)
        group_far = mm_nt(queries, state_ref[0, at(g, WIDTH), :])
        for pair in range(GROUP // 2):
            here = pl.ds(pl.multiple_of(g * WIDTH + pair * LANES, LANES), LANES)
            far = group_far[:, pair * LANES : (pair + 1) * LANES]
            y = y_ref[0, :, here] + spread(front, pair, low) * far
            total[:, here] = y
            y = y + lanes_ref[1:2, here] * act_ref[0, :, here]
            z = z_ref[:, here].astype(f32)
            gated = y * (z * sigmoid(z))
            square = square + gated * gated
            inner = inner + lanes_ref[0:1, here] * dgn_ref[:, here].astype(f32) * gated
        return square, inner

    zero = jnp.zeros((length, LANES), f32)
    square, inner = lax.fori_loop(0, GROUPS, first, (zero, zero))
    scale = lax.rsqrt(jnp.sum(square, axis=1, keepdims=True) * (1.0 / INNER) + EPSILON)
    back = scale * scale * scale * (jnp.sum(inner, axis=1, keepdims=True) * (1.0 / INNER))
    scale = jnp.broadcast_to(scale, (length, LANES))
    back = jnp.broadcast_to(back, (length, LANES))
    queries_acc[...] = jnp.zeros_like(queries_acc)
    dq_ref[0] = jnp.zeros_like(dq_ref[0])

    @pl.loop(0, GROUPS)
    def _(g):
        front = to_front(enter, g)
        products, entered = [], []
        for pair in range(GROUP // 2):
            here = pl.ds(pl.multiple_of(g * WIDTH + pair * LANES, LANES), LANES)
            xs = act_ref[0, :, here]
            inside = total[:, here]
            y = inside + lanes_ref[1:2, here] * xs
            z = z_ref[:, here].astype(f32)
            sg = sigmoid(z)
            gate = z * sg
            gated = y * gate
            gain = lanes_ref[0:1, here]
            dgn = dgn_ref[:, here].astype(f32)
            gn = gated * scale
            gn_ref[:, here] = (gn * gain).astype(bf16)
            dgated = scale * (gain * dgn) - gated * back
            dy = dgated * gate
            dz_ref[:, here] = (dgated * y * (sg * (1.0 + z * (1.0 - sg)))).astype(bf16)
            rounded = dy.astype(bf16)
            dy_ref[0, :, here] = rounded
            sums_ref[0, 0:1, here] = jnp.sum(dgn * gn, axis=0, keepdims=True)
            sums_ref[0, 1:2, here] = jnp.sum(dy * xs, axis=0, keepdims=True)
            rounded = rounded.astype(f32)
            entered.append((rounded * spread(front, pair, low)).astype(bf16))
            products.append(rounded * inside)
        entered = jnp.concatenate(entered, axis=1)
        dstate_ref[0, at(g, WIDTH), :] = mm_tn(entered, queries).astype(bf16)
        queries_acc[...] += MM(entered, state_ref[0, at(g, WIDTH), :])
        dq_ref[0] += head_sums(jnp.concatenate(products, axis=1), g)

    q_ref[0] = queries_acc[...]


def scan_back_kernel(act_ref, tok_ref, cst_ref, cols_ref, rows_ref, dy_ref,
                     dx_ref, dbc_ref, cross, bias, dcross):
    length = act_ref.shape[1]
    half = length // 2
    keys = act_ref[0, :, INNER : INNER + STATE].astype(bf16)
    queries = act_ref[0, :, INNER + STATE :].astype(bf16)
    cross[...] = mm_nt(keys, queries)
    bias[...] = bias_of(cols_ref[0, :, 5:6], rows_ref[0, 0:1, :], True)
    dcross[...] = jnp.zeros_like(dcross)
    low = low_half(length)

    @pl.loop(0, GROUPS)
    def _(g):
        step = to_front(tok_ref[0, :, 0:LANES], g)
        decay = to_front(tok_ref[0, :, LANES : 2 * LANES], g)
        rows = cst_ref[0, at(g, GROUP), :]
        for pair in range(GROUP // 2):
            here = pl.ds(pl.multiple_of(g * WIDTH + pair * LANES, LANES), LANES)
            scaled = (act_ref[0, :, here] * spread(step, pair, low)).astype(bf16)
            dy = dy_ref[0, :, here].astype(f32)
            top, bottom = 0.0, 0.0
            for which in range(2):
                h = 2 * pair + which
                mine = jnp.where(low == (which == 0), dy, 0.0).astype(bf16)
                col, row = decay[:, h : h + 1], rows[h : h + 1, :]
                w = jnp.exp(row - col[:half] + bias[:half, :])
                dcross[:half, :] += mm_nt(scaled[:half], mine) * w
                top = top + MM((cross[:half, :] * w).astype(bf16), mine)
                w = jnp.exp(row[:, half:] - col[half:] + bias[half:, half:])
                dcross[half:, half:] += mm_nt(scaled[half:], mine[half:]) * w
                bottom = bottom + MM((cross[half:, half:] * w).astype(bf16), mine[half:])
            dx_ref[0, :half, here] = top
            dx_ref[0, half:, here] = bottom

    d = dcross[...].astype(bf16)
    dbc_ref[0, :, :STATE] = MM(d, queries)
    dbc_ref[0, :, STATE:] = mm_tn(d, keys)


def after_kernel(px_ref, tail_ref, w_ref, b_ref, cols_ref, heads_ref, act_ref, tok_ref, lanes_ref,
                 dy_ref, dx_ref, dbc_ref, q_ref, dq_ref, later_ref, state_ref,
                 dpx_ref, dconv_ref, dheads_ref, ext, moved, grad, dstep_acc, dcol_acc, keys_acc, ends, sent, edges):
    s = pl.program_id(0)
    length = act_ref.shape[1]
    low = low_half(length)
    step = tok_ref[0, :, 0:LANES]
    decay = tok_ref[0, :, LANES : 2 * LANES]
    leave = jnp.exp(decay[length - 1 : length] - decay) * cols_ref[0, :, 4:5]
    keys = act_ref[0, :, INNER : INNER + STATE].astype(bf16)
    dstep_acc[...] = jnp.zeros_like(dstep_acc)
    dcol_acc[...] = jnp.zeros_like(dcol_acc)
    sent[...] = jnp.zeros_like(sent)
    keys_acc[...] = dbc_ref[0, :, :STATE]
    ends[...] = jnp.zeros_like(ends)

    @pl.loop(0, GROUPS)
    def _(g):
        step_front, leave_front = to_front(step, g), to_front(leave, g)
        products, columns, leaves = [], [], []
        group_through = mm_nt(keys, later_ref[0, at(g, WIDTH), :])
        for pair in range(GROUP // 2):
            here = pl.ds(pl.multiple_of(g * WIDTH + pair * LANES, LANES), LANES)
            later = later_ref[0, here, :]
            xs = act_ref[0, :, here]
            steps = spread(step_front, pair, low)
            leaving = spread(leave_front, pair, low)
            through = leaving * group_through[:, pair * LANES : (pair + 1) * LANES]
            dscaled = dx_ref[0, :, here] + through
            scaled = steps * xs
            rounded = scaled.astype(bf16).astype(f32)
            leaves.append((leaving * scaled).astype(bf16))
            products.append(xs * dscaled)
            columns.append(rounded * dscaled)
            sent[0:1, here] = jnp.sum(rounded * through, axis=0, keepdims=True)
            grad[:, here] = steps * dscaled + lanes_ref[1:2, here] * dy_ref[0, :, here].astype(f32)
            both = later.astype(f32) * state_ref[0, here, :].astype(f32)
            at_row = GROUP * g + 2 * pair
            ends[pl.ds(at_row, 1), :] = jnp.sum(both[:HEADDIM], axis=0, keepdims=True)
            ends[pl.ds(at_row + 1, 1), :] = jnp.sum(both[HEADDIM:], axis=0, keepdims=True)
        keys_acc[...] += MM(jnp.concatenate(leaves, axis=1), later_ref[0, at(g, WIDTH), :])
        dstep_acc[...] += head_sums(jnp.concatenate(products, axis=1), g)
        dcol_acc[...] += head_sums(jnp.concatenate(columns, axis=1), g)

    grad[:, INNER : INNER + STATE] = keys_acc[...]
    grad[:, INNER + STATE :] = dbc_ref[0, :, STATE:] + q_ref[0]
    dstep = dstep_acc[...]
    kept = jnp.exp(decay[length - 1 : length]) * cols_ref[0, length - 1 : length, 3:4]
    at_end = kept * jnp.sum(ends[...].T, axis=0, keepdims=True)
    for g in range(GROUPS):
        at_end = at_end + head_sums(sent[:, g * WIDTH : (g + 1) * WIDTH], g)[0:1]
    row = lax.broadcasted_iota(jnp.int32, (length, LANES), 0)
    ddecay = dq_ref[0] - dcol_acc[...] + jnp.where(row == length - 1, at_end, 0.0)
    onward = (
        lax.broadcasted_iota(jnp.int32, (length, length), 0)
        <= lax.broadcasted_iota(jnp.int32, (length, length), 1)
    ).astype(f32)
    drate = jnp.dot(onward, ddecay, precision=lax.Precision.HIGHEST, preferred_element_type=f32)
    speed = jnp.exp(heads_ref[1:2, :])
    raw = px_ref[:, CHANNELS : CHANNELS + HEADS].astype(f32) + heads_ref[0:1, :HEADS]
    draw = (dstep - drate * speed)[:, :HEADS] * sigmoid(raw)
    mine = pl.ds(pl.multiple_of(s * length, length), length)
    dpx_ref[mine, CHANNELS:] = jnp.concatenate(
        [draw, jnp.zeros((length, LANES - HEADS), f32)], axis=1
    ).astype(bf16)
    edges[s, :, CHANNELS:] = jnp.zeros((8, LANES), f32)
    dheads_ref[0] = jnp.zeros((8, LANES), f32)
    dheads_ref[0, 0:1, :HEADS] = jnp.sum(draw, axis=0, keepdims=True)
    dheads_ref[0, 1:2, :] = jnp.sum(drate * (-step * speed), axis=0, keepdims=True)

    masks = lane_masks(cols_ref, length)
    moved[...] = jnp.zeros_like(moved)
    dconv_ref[0] = jnp.zeros((8, CHANNELS), f32)

    @pl.loop(0, CHANNELS // LANES)
    def _(j):
        here = at(j, LANES)
        conv, inputs = taps(px_ref, tail_of(tail_ref, s, here), j, w_ref, b_ref, masks, ext)
        sg = sigmoid(conv)
        dconv = grad[:, here] * (sg * (1.0 + conv * (1.0 - sg)))
        for k in range(CONV):
            dconv_ref[0, k : k + 1, here] = jnp.sum(dconv * inputs[k], axis=0, keepdims=True)
        dconv_ref[0, CONV : CONV + 1, here] = jnp.sum(dconv, axis=0, keepdims=True)
        dx = w_ref[0:1, here] * dconv
        edge = jnp.zeros((8, LANES), f32)
        for k in range(1, CONV):
            moved[k - 1, 8 : 8 + length, :] = dconv * masks[k - 1]
            dx = dx + w_ref[k : k + 1, here] * moved[k - 1, 8 + k : 8 + k + length, :]
            edge = edge + w_ref[k : k + 1, here] * moved[k - 1, k : 8 + k, :]
        dpx_ref[mine, here] = dx.astype(bf16)
        edges[s, :, here] = edge

    @pl.when(s == pl.num_programs(0) - 1)
    def _():
        rows = edges.shape[0] * 8
        dpx_ref[dpx_ref.shape[0] - rows :, :] = edges[...].reshape(rows, edges.shape[2]).astype(bf16)


def whole(shape):
    return pl.BlockSpec(shape, lambda s: (0,) * len(shape))


def per_seq(*tail):
    return pl.BlockSpec((1,) + tail, lambda s: (s,) + (0,) * len(tail))


def per_rows(rows, width):
    return pl.BlockSpec((rows, width), lambda s: (s, 0))


def call(kernel, count, in_specs, outs, scratch, *args):
    return pl.pallas_call(
        kernel,
        grid=(count,),
        in_specs=in_specs,
        out_specs=[spec for spec, _unused in outs],
        out_shape=[jax.ShapeDtypeStruct(*made) for _unused, made in outs],
        scratch_shapes=scratch,
        compiler_params=pltpu.CompilerParams(vmem_limit_bytes=VMEM),
    )(*args)


def chain(own, factor, steps, beside):
    entered = jnp.zeros(own.shape, bf16)
    results = []
    for k, (source, target) in enumerate(steps):
        sent = own if k == 0 else (own.astype(f32) + factor * entered.astype(f32)).astype(bf16)
        came = lax.ppermute(sent, "ctx", [(source, target)])
        for work in beside[k :: len(steps)]:
            results.append(work())
            came, results[-1] = lax.optimization_barrier((came, results[-1]))
        entered = came if k == 0 else entered + came
    return entered, results


def pad_lanes(v):
    return jnp.pad(v, (0, LANES - v.shape[0]))


def finish_kernel(lead, small_ref, dwz_ref, dpx_ref, normed_ref, dz_ref, wx_ref, wz_ref, x_ref, tail_ref, gain_ref, g_ref,
                  gn_ref, wo_ref, oz_ref, ox_ref, os_ref, og_ref, grad_ref, out_ref, *scratch):
    own_z, own, buffers, own_s, buffers_s = scratch[0], scratch[1], scratch[2:6], scratch[6], scratch[7:11]
    own_g, buffers_g = scratch[11], scratch[12:16]
    rows, wbuf, total, back, sem, semz, zsem, wsem, rsem, tail_sem, own_sem = scratch[16:]
    place_of = place()
    z, y, x, c = place_of
    meet(place_of, True)
    count = g_ref.shape[0]
    nz = dwz_ref.shape[-1] // CUT
    widths = [CUT] * nz + [
        min(CUT, dpx_ref.shape[1] - k) for k in range(0, dpx_ref.shape[1], CUT)
    ]
    small, gain = len(widths), len(widths) + 1

    def whole_own(i):
        return {small: own_s, gain: own_g}[i] if i >= small else cut_to(widths[i], own.at[i - nz])

    def own_of(i):
        if i < nz:
            return lambda zz, yy, xx: own_z[i % SLOTS, zz, yy, xx]
        ref = whole_own(i)
        return lambda zz, yy, xx: ref[zz, yy, xx, c]

    def source(i, core):
        if i < nz:
            return dwz_ref.at[:, :, :, core, :, pl.ds(i * CUT, CUT)]
        return whole_own(i).at[:, :, :, core]

    def result(i, value):
        if i >= small:
            {small: os_ref, gain: og_ref}[i][...] = value
        elif i < nz:
            oz_ref[:, i * CUT : (i + 1) * CUT] = value
        else:
            k = (i - nz) * CUT
            ox_ref[:, k : k + widths[i]] = value

    def buffers_of(i):
        if i >= small:
            return [v.at[0] for v in (buffers_s if i == small else buffers_g)]
        return [cut_to(widths[i], v.at[i]) for v in buffers]

    red = Reduction(place_of, source, own_of, buffers_of, result, sem, semz)

    def fetch(i):
        return pltpu.make_async_copy(
            dwz_ref.at[:, :, :, c, :, pl.ds(i * CUT, CUT)], own_z.at[i % SLOTS], zsem.at[i % SLOTS]
        )

    def arrive(i, stage):
        if stage == 0 and i < nz:
            fetch(i).wait()
        red.arrive(i, stage)
        if stage == 0 and i + SLOTS < nz:
            fetch(i + SLOTS).start()

    def weight_and_send(j):
        k, w = j * CUT, widths[nz + j]
        own_j = whole_own(nz + j)
        depth = normed_ref.shape[1] // NZ

        @pl.loop(0, NZ)
        def _(zz):
            value = mm_tn(normed_ref[:, at(zz, depth)], dpx_ref[:, k : k + w])
            own_j[zz] = value.astype(bf16).reshape(2, 2, 2, CUT_ROWS, w)

        red.send(nz + j, 0)

    chunks = [(wz_ref, rows, k, CUT) for k in range(0, wz_ref.shape[1], CUT)]
    chunks += [(wx_ref, dpx_ref, k * CUT, w) for k, w in enumerate(widths[nz:])]

    def stream(q):
        w_ref, _left, k, w = chunks[q]
        return pltpu.make_async_copy(
            w_ref.at[:, pl.ds(k, w)], wbuf.at[q % 2, :, pl.ds(0, w)], wsem.at[q % 2]
        )

    depth_out = wo_ref.shape[0] // 2
    outs = wo_ref.shape[1] // CUT

    def stream_out(q, half):
        return pltpu.make_async_copy(
            wo_ref.at[pl.ds(half * depth_out, depth_out), pl.ds(q * CUT, CUT)], wbuf.at[half],
            wsem.at[half],
        )

    def load_rows(source_ref):
        return pltpu.make_async_copy(source_ref, rows, rsem.at[0])

    def input_chunk(q):
        _w, left, k, w = chunks[q]
        if q == 0:
            load_rows(dz_ref).wait()
            total[...] = jnp.zeros_like(total)
        stream(q).wait()
        total[: left.shape[0]] += mm_nt(left[:, k : k + w], wbuf[q % 2, :, :w])
        if q + 2 < len(chunks):
            stream(q + 2).start()
        if q == nz - 1:
            load_rows(gn_ref).start()

    def output_chunk(q):
        here = slice(q * CUT, (q + 1) * CUT)
        if q == 0:
            load_rows(gn_ref).wait()
            for half in range(2):
                stream_out(q, half).start()
        value = x_ref[:, here].astype(f32)
        for half in range(2):
            stream_out(q, half).wait()
            value = value + MM(rows[:, half * depth_out : (half + 1) * depth_out], wbuf[half])
            if q + 1 < outs:
                stream_out(q + 1, half).start()
        out_ref[:, here] = value.astype(bf16)

    def tail_copy():
        return remote(
            total.at[pl.ds(count, 16)], back, tail_sem.at[0], tail_sem.at[1],
            {"seq": z * 2 + y, "ctx": lax.rem(x * 2 + c + 3, 4)},
        )

    def scaled_rows(rows_ref, lo, hi):
        v = rows_ref[lo:hi].astype(f32)
        return v, lax.rsqrt(jnp.mean(v * v, axis=1, keepdims=True) + EPSILON)

    def norm_weights():
        tail_copy().start()
        sums = jnp.zeros((normed_ref.shape[1], LANES), f32)
        ones = jnp.ones((LANES, LANES), bf16)
        for lo in range(0, count + 16, LANES):
            size = min(LANES, count + 16 - lo)
            v, r = scaled_rows(x_ref, lo, lo + LANES) if lo < count else scaled_rows(tail_ref, 0, 16)
            product = v * r * total[lo : lo + size]
            high = product.astype(bf16)
            rest = (product - high.astype(f32)).astype(bf16)
            sums = sums + mm_tn(high, ones[:size]) + mm_tn(rest, ones[:size])
        own_g[...] = sums.astype(bf16).reshape(own_g.shape)
        red.send(gain, 0)

    def norm_rows():
        tail_copy().wait()
        seqs = tail_ref.shape[0] // 8
        length = count // seqs
        for s in range(seqs):
            total[(s + 1) * length - 8 : (s + 1) * length] += back[8 * s : 8 * s + 8]
        for lo in range(0, count, LANES):
            v, r = scaled_rows(x_ref, lo, lo + LANES)
            scaled = gain_ref[0:1] * total[lo : lo + LANES]
            mean = jnp.mean(v * scaled, axis=1, keepdims=True)
            value = g_ref[lo : lo + LANES].astype(f32) + r * (scaled - v * (r * r) * mean)
            grad_ref[lo : lo + LANES] = value.astype(bf16)

    for i in range(nz):
        red.send(i, 0)
    for i in range(SLOTS):
        fetch(i).start()
    small_copy = pltpu.make_async_copy(small_ref, own_s, own_sem.at[0])
    small_copy.start()
    load_rows(dz_ref).start()
    for q in range(2):
        stream(q).start()
    order = [*range(gain + 1)]
    work = [[partial(weight_and_send, j)] for j in range(small - nz)]
    step = -(-len(chunks) // 5)
    work += [
        [partial(input_chunk, q) for q in range(k, min(k + step, len(chunks)))]
        for k in range(0, len(chunks), step)
    ]
    work += [[norm_weights], [norm_rows]] + [[partial(output_chunk, q)] for q in range(outs)]
    work[1] = work[1] + [small_copy.wait, partial(red.send, small, 0)]
    for t in range(max(len(order) + lead[-1], len(work))):
        for job in work[t] if t < len(work) else []:
            job()
        for stage in reversed(range(4)):
            if 0 <= t - lead[stage] < len(order):
                arrive(order[t - lead[stage]], stage)
    for i in order:
        red.drain(i)


def finish(small, dw_z, dpx, normed, dz, w_x, w_z, x, tail, gain, g, gn, w_out, lead=LEAD):
    small = small.reshape((NZ, 2, 2, 2, -1, small.shape[-1]))
    dw_z = dw_z.reshape((NZ, 2, 2, 2, -1, dw_z.shape[-1]))
    nx = pl.cdiv(dpx.shape[1], CUT)
    p = nx + dw_z.shape[-1] // CUT
    ss = small.shape[-2:]
    far, near = pl.BlockSpec(memory_space=pl.ANY), pl.BlockSpec(memory_space=pltpu.VMEM)
    return pl.pallas_call(
        partial(finish_kernel, tuple(lead)),
        out_shape=[
            jax.ShapeDtypeStruct((CUT_ROWS, dw_z.shape[-1]), f32),
            jax.ShapeDtypeStruct((CUT_ROWS, dpx.shape[1]), f32),
            jax.ShapeDtypeStruct(ss, f32),
            jax.ShapeDtypeStruct((CUT_ROWS, LANES), f32),
            jax.ShapeDtypeStruct(g.shape, bf16),
            jax.ShapeDtypeStruct(g.shape, bf16),
        ],
        in_specs=[far, far, near, near, far, far, far, near, near, near, near, far, far],
        out_specs=[near] * 6,
        scratch_shapes=[
            pltpu.VMEM((SLOTS, NZ, 2, 2, CUT_ROWS, CUT), bf16),
            pltpu.VMEM((nx, NZ, 2, 2, 2, CUT_ROWS, CUT), bf16),
        ]
        + reduction_buffers(p, (CUT_ROWS, CUT), bf16)
        + [pltpu.VMEM(small.shape, f32)] + reduction_buffers(1, ss, f32)
        + [pltpu.VMEM((NZ, 2, 2, 2, CUT_ROWS, LANES), bf16)]
        + reduction_buffers(1, (CUT_ROWS, LANES), bf16)
        + [
            pltpu.VMEM(dz.shape, bf16), pltpu.VMEM((2, w_x.shape[0], CUT), bf16),
            pltpu.VMEM(normed.shape, f32), pltpu.VMEM(tail.shape, f32),
        ]
        + reduction_semaphores(p + 2)
        + [pltpu.SemaphoreType.DMA((SLOTS,)), pltpu.SemaphoreType.DMA((2,)),
           pltpu.SemaphoreType.DMA((1,)), pltpu.SemaphoreType.DMA((2,)), pltpu.SemaphoreType.DMA((1,))],
        compiler_params=pltpu.CompilerParams(
            collective_id=1, has_side_effects=True, vmem_limit_bytes=FINISH_VMEM
        ),
    )(small, dw_z, dpx, normed, dz, w_x, w_z, x, tail, gain, g, gn, w_out)


def local(tokens, norm_gain, input_weight, conv_w, conv_b, dt_bias, a_log, d_skip, gate_gain,
          output_weight, segments, cotangent):
    seqs, length, width = tokens.shape
    n_ctx = lax.axis_size("ctx")
    n_all = n_ctx * lax.axis_size("seq")
    count = seqs * length
    shares = [norm_gain.shape[0], gate_gain.shape[0], CONV * conv_b.shape[0], conv_b.shape[0]]
    cuts = [sum(shares[: i + 1]) for i in range(3)]
    packed = jnp.concatenate([norm_gain, gate_gain, conv_w.reshape(-1), conv_b])
    onward = [(i, i + 1) for i in range(n_ctx - 1)]
    tail = jnp.pad(tokens[:, length - (CONV - 1) :], ((0, 0), (8 - (CONV - 1), 0), (0, 0)))
    tail_ids = jnp.pad(
        segments[:, length - (CONV - 1) :].astype(bf16), ((0, 0), (0, width - (CONV - 1)))
    )
    tail = jnp.concatenate([tail_ids[:, None], tail[:, 1:]], axis=1).reshape(seqs * 8, width)
    torus = lax.axis_size("seq") == 2 * NZ and n_ctx == 4 and norm_gain.shape[0] == CUT_ROWS
    spare = ((0, 0), (0, LANES - HEADS))
    w_z, w_x = input_weight[:, :INNER], jnp.pad(input_weight[:, INNER:], spare)
    if torus:
        size = packed.shape[0]
        small = jnp.pad(packed, (0, 16 * LANES - size)).reshape(16, LANES)
        w_out = lax.all_gather(output_weight, BOTH, axis=0, tiled=True)
        w_z = lax.all_gather(w_z, BOTH, axis=0, tiled=True)
        w_x, packed, tail = gather_all(
            [w_x, small], tail,
            [(1, 0, 16, True)]
            + [(0, 16 * k, 16, k % 2 == 0) for k in range(3)]
,
        )
        w_x, w_z, w_out = (w.reshape(-1, w.shape[-1]) for w in (w_x, w_z, w_out))
        packed = packed.reshape(n_all, -1)[:, :size]
    else:
        packed = lax.all_gather(packed, BOTH, axis=0)
        tail = lax.ppermute(tail, "ctx", onward)
        w_in, w_out = (
            lax.all_gather(w, BOTH, axis=0, tiled=True) for w in (input_weight, output_weight)
        )
        w_z, w_x = w_in[:, :INNER], jnp.pad(w_in[:, INNER:], spare)
    norm_full, gate_full, conv_w_full, conv_b_full = jnp.split(packed.astype(f32), cuts, axis=1)
    norm_full = norm_full.reshape(1, -1)
    gate_full = gate_full.reshape(1, -1)
    conv_b_full = conv_b_full.reshape(1, -1)
    conv_w_full = conv_w_full.reshape(n_all, CONV, -1).transpose(1, 0, 2).reshape(CONV, -1)

    tail = tail.reshape(seqs, 8, width)
    tail_ids = jnp.where(
        lax.axis_index("ctx") == 0, -1, tail[:, 0, : CONV - 1].astype(jnp.int32)
    )
    tail = jnp.pad(tail[:, 8 - (CONV - 1) :], ((0, 0), (8 - (CONV - 1), 0), (0, 0)))
    tail = jnp.where(lax.axis_index("ctx") == 0, 0, tail)
    tail = tail.reshape(seqs * 8, width)
    x_all = jnp.concatenate([tokens.reshape(count, width), tail])
    x_all = x_all.astype(f32)
    r_all = lax.rsqrt(jnp.mean(x_all * x_all, axis=-1, keepdims=True) + EPSILON)
    normed = (x_all * r_all * norm_full).astype(bf16)

    ids_ext = jnp.concatenate([tail_ids, segments], axis=1)
    flags = [
        segments == ids_ext[:, CONV - 1 - k : CONV - 1 - k + length] for k in range(1, CONV)
    ] + [segments == ids_ext[:, CONV - 2 : CONV - 1], segments == segments[:, -1:]]
    cols = jnp.stack([f.astype(f32) for f in flags] + [segments.astype(f32)], axis=-1)
    cols = jnp.pad(cols, ((0, 0), (0, 0), (0, LANES - cols.shape[-1])))
    rows = jnp.pad(segments.astype(f32)[:, None], ((0, 0), (0, 7), (0, 0)))
    heads = jnp.pad(jnp.stack([pad_lanes(dt_bias), pad_lanes(a_log)]), ((0, 6), (0, 0)))
    lanes = jnp.concatenate([gate_full, jnp.repeat(d_skip, HEADDIM)[None]])
    lanes = jnp.pad(lanes, ((0, 6), (0, 0)))
    conv_w8 = jnp.pad(conv_w_full, ((0, 8 - CONV), (0, 0)))
    conv_b8 = jnp.pad(conv_b_full, ((0, 7), (0, 0)))

    px = MM(normed, w_x).astype(bf16)
    px_width, used = CHANNELS + LANES, CHANNELS + HEADS
    tail_spec = pl.BlockSpec((16, px_width), lambda s: (count // 16, 0))
    act, tok, cst, fresh = call(
        before_kernel, seqs,
        [per_rows(length, px_width), tail_spec, whole((8, CHANNELS)), whole((8, CHANNELS)),
         per_seq(length, LANES), whole((8, LANES))],
        [(per_seq(length, CHANNELS), ((seqs, length, CHANNELS), f32)),
         (per_seq(length, 2 * LANES), ((seqs, length, 2 * LANES), f32)),
         (per_seq(HEADS, length), ((seqs, HEADS, length), f32)),
         (per_seq(INNER, STATE), ((seqs, INNER, STATE), bf16))],
        [pltpu.VMEM((length + 8, LANES), f32)],
        px, px, conv_w8, conv_b8, cols, heads,
    )
    carried = cols[:, length - 1, 3]
    kept = jnp.exp(cst[:, :, length - 1]) * carried[:, None]
    kept = jnp.repeat(kept, HEADDIM, axis=1)[..., None]
    g2 = cotangent.reshape(count, width)

    def gate_gradient():
        dims = (((1,), (1,)), ((), ()))
        return lax.dot_general(g2, w_out, dims, preferred_element_type=f32).astype(bf16)

    def within():
        [y] = call(
            within_kernel, seqs,
            [per_seq(length, CHANNELS), per_seq(length, 2 * LANES), per_seq(HEADS, length),
             per_seq(length, LANES), per_seq(8, length)],
            [(per_seq(length, INNER), ((seqs, length, INNER), f32))],
            [pltpu.VMEM((length, length), f32), pltpu.VMEM((length, length), f32)],
            act, tok, cst, cols, rows,
        )
        return y

    def gates():
        return MM(normed[:count], w_z).astype(bf16)

    entering, (dgn, y, pz) = chain(fresh, kept, onward, (gate_gradient, within, gates))
    gn, dz, dy, dstate, dqueries, ddecay, sums = call(
        gate_kernel, seqs,
        [per_rows(length, INNER), per_seq(length, CHANNELS), per_seq(length, 2 * LANES),
         per_seq(length, LANES), per_seq(length, INNER), per_seq(INNER, STATE),
         per_rows(length, INNER), whole((8, INNER))],
        [(per_rows(length, INNER), ((count, INNER), bf16)),
         (per_rows(length, INNER), ((count, INNER), bf16)),
         (per_seq(length, INNER), ((seqs, length, INNER), bf16)),
         (per_seq(INNER, STATE), ((seqs, INNER, STATE), bf16)),
         (per_seq(length, STATE), ((seqs, length, STATE), f32)),
         (per_seq(length, LANES), ((seqs, length, LANES), f32)),
         (per_seq(8, INNER), ((seqs, 8, INNER), f32))],
        [pltpu.VMEM((length, INNER), f32), pltpu.VMEM((length, STATE), f32)],
        pz, act, tok, cols, y, entering, dgn, lanes,
    )
    tn = (((0,), (0,)), ((), ()))

    def output_weights():
        return lax.dot_general(gn, g2, tn, preferred_element_type=f32).astype(bf16)

    def scan_back():
        return call(
            scan_back_kernel, seqs,
            [per_seq(length, CHANNELS), per_seq(length, 2 * LANES), per_seq(HEADS, length),
             per_seq(length, LANES), per_seq(8, length), per_seq(length, INNER)],
            [(per_seq(length, INNER), ((seqs, length, INNER), f32)),
             (per_seq(length, 2 * STATE), ((seqs, length, 2 * STATE), f32))],
            [pltpu.VMEM((length, length), f32)] * 3,
            act, tok, cst, cols, rows, dy,
        )

    def gate_weights():
        return lax.dot_general(normed[:count], dz, tn, preferred_element_type=f32).astype(bf16)

    later, (dw_out, (dx, dbc), dw_z) = chain(
        dstate, kept, [(b, a) for a, b in reversed(onward)], (output_weights, scan_back, gate_weights)
    )
    dpx, dconv, dheads = call(
        after_kernel, seqs,
        [per_rows(length, px_width), tail_spec, whole((8, CHANNELS)), whole((8, CHANNELS)),
         per_seq(length, LANES), whole((8, LANES)), per_seq(length, CHANNELS),
         per_seq(length, 2 * LANES), whole((8, INNER)), per_seq(length, INNER),
         per_seq(length, INNER), per_seq(length, 2 * STATE), per_seq(length, STATE),
         per_seq(length, LANES), per_seq(INNER, STATE), per_seq(INNER, STATE)],
        [(whole((count + seqs * 8, px_width)), ((count + seqs * 8, px_width), bf16)),
         (per_seq(8, CHANNELS), ((seqs, 8, CHANNELS), f32)),
         (per_seq(8, LANES), ((seqs, 8, LANES), f32))],
        [pltpu.VMEM((length + 8, LANES), f32), pltpu.VMEM((CONV - 1, length + 16, LANES), f32),
         pltpu.VMEM((length, CHANNELS), f32), pltpu.VMEM((length, LANES), f32),
         pltpu.VMEM((length, LANES), f32), pltpu.VMEM((length, STATE), f32), pltpu.VMEM((LANES, LANES), f32),
         pltpu.VMEM((8, INNER), f32), pltpu.VMEM((seqs, 8, px_width), f32)],
        px, px, conv_w8, conv_b8, cols, heads, act, tok, lanes, dy, dx, dbc, dqueries, ddecay,
        later, entering,
    )
    sums = jnp.sum(sums, axis=0)
    dconv = jnp.sum(dconv, axis=0)
    dheads = jnp.sum(dheads, axis=0)
    d_skip_sum = jnp.sum(sums[1].reshape(HEADS, HEADDIM), axis=1)
    split = [sums[0].reshape(n_all, -1),
             dconv[:CONV].reshape(CONV, n_all, -1).transpose(1, 0, 2).reshape(n_all, -1),
             dconv[CONV].reshape(n_all, -1)]
    shared = jnp.concatenate([dheads[0, :HEADS], dheads[1, :HEADS], d_skip_sum])
    split = jnp.concatenate(split, axis=1)
    share = split.shape[1]
    if torus:
        fill = 8 * LANES - share - shared.shape[0]
        split = [split, jnp.broadcast_to(shared, (n_all,) + shared.shape), jnp.zeros((n_all, fill), f32)]
        dw_z, dw_x, mine, d_norm, input_grad, output = finish(
            jnp.concatenate(split, axis=1).reshape(n_all, 8, LANES), dw_z, dpx, normed, dz,
            w_x, w_z, tokens.reshape(count, width), tail, jnp.pad(norm_full, ((0, 7), (0, 0))), g2,
            gn, w_out,
        )
        d_norm = d_norm[:, 0]
        dw_out = lax.psum_scatter(dw_out, BOTH, scatter_dimension=0, tiled=True).astype(f32)
        dw_in = jnp.concatenate([dw_z, dw_x[:, :used]], axis=1)
        mine = mine.reshape(-1)
        mine, shared = mine[:share], mine[share : share + shared.shape[0]]
    else:
        nt = (((1,), (1,)), ((), ()))
        dnormed_x = lax.dot_general(dpx, w_x, nt, preferred_element_type=f32)
        dnormed = dnormed_x[:count] + lax.dot_general(dz, w_z, nt, preferred_element_type=f32)
        back = dnormed_x[count:].reshape(seqs, 8, width)[:, 8 - (CONV - 1) :].astype(bf16)
        back = lax.ppermute(back, "ctx", [(b, a) for a, b in onward])
        dw_x = lax.dot_general(normed, dpx, tn, preferred_element_type=f32).astype(bf16)
        x, r = x_all[:count], r_all[:count]
        d_gain = jnp.sum(x * r * dnormed, axis=0) + jnp.sum(
            x_all[count:] * r_all[count:] * dnormed_x[count:], axis=0
        )
        back, d_gain, dw_x = lax.optimization_barrier((back, d_gain, dw_x))
        back = jnp.pad(back.astype(f32), ((0, 0), (length - (CONV - 1), 0), (0, 0)))
        scaled = norm_full * (dnormed + back.reshape(count, width))
        dx_in = r * (scaled - x * (r * r) * jnp.mean(x * scaled, axis=-1, keepdims=True))
        input_grad = (g2.astype(f32) + dx_in).astype(bf16)
        output = (x_all[:count] + MM(gn, w_out)).astype(bf16)
        dw_in = jnp.concatenate([dw_z, dw_x[:, :used]], axis=1)
        dw_out, dw_in = (
            lax.psum_scatter(v.astype(f32), BOTH, scatter_dimension=0, tiled=True)
            for v in (dw_out, dw_in)
        )
        every = lax.psum(jnp.concatenate([split.reshape(-1), shared, d_gain]), BOTH)
        me = lax.axis_index("seq") * n_ctx + lax.axis_index("ctx")
        d_norm = lax.dynamic_slice(every[-width:], (me * shares[0],), (shares[0],))
        mine = lax.dynamic_slice(every, (me * share,), (share,))
        shared = every[n_all * share : n_all * share + shared.shape[0]]
    d_gate, d_conv_w, d_conv_b = jnp.split(mine, [v - cuts[0] for v in cuts[1:]])
    d_bias, d_alog, d_skips = jnp.split(shared, 3)
    return (
        output.reshape(tokens.shape), input_grad.reshape(tokens.shape), d_norm, dw_in,
        d_conv_w.reshape(CONV, -1), d_conv_b, d_bias, d_alog, d_skips, d_gate, dw_out,
    )


def solution(mesh):
    split = P(BOTH)
    rows = P(BOTH, None)
    seq = P("seq", "ctx", None)
    in_specs = (seq, split, rows, P(None, BOTH), split, P(), P(), P(), split, rows,
                P("seq", "ctx"), seq)
    out_specs = (seq, seq, split, rows, P(None, BOTH), split, P(), P(), P(), split, rows)
    return jax.shard_map(local, mesh=mesh, in_specs=in_specs, out_specs=out_specs, check_vma=False)
```

```python
from functools import partial

import jax
import jax.numpy as jnp
from jax import lax
from jax.experimental import pallas as pl
from jax.experimental.pallas import tpu as pltpu
from jax.sharding import PartitionSpec as P

HEADS = 48
STATE = 128
HEADDIM = 64
CONV = 4
INNER = HEADS * HEADDIM
CHANNELS = INNER + 2 * STATE
GROUP = 8
GROUPS = HEADS // GROUP
WIDTH = GROUP * HEADDIM
LANES = 128
EPSILON = 1e-05
VMEM = 60 * 1024 * 1024
FINISH_VMEM = 62 * 1024 * 1024 - 512 * 1024
BOTH = ("seq", "ctx")
FAR = -1e30
f32 = jnp.float32
bf16 = jnp.bfloat16
MM = partial(jnp.dot, preferred_element_type=f32)


def mm_nt(a, b):
    return lax.dot_general(a, b, (((1,), (1,)), ((), ())), preferred_element_type=f32)


def mm_tn(a, b):
    return lax.dot_general(a, b, (((0,), (0,)), ((), ())), preferred_element_type=f32)


def sigmoid(v):
    return 0.5 + 0.5 * jnp.tanh(0.5 * v)


def at(j, width):
    return pl.ds(pl.multiple_of(j * width, width), width)


def low_half(rows):
    return lax.broadcasted_iota(jnp.int32, (rows, LANES), 1) < HEADDIM


def to_front(columns, g):
    return pltpu.roll(columns, lax.rem(LANES - GROUP * g, LANES), 1)


def spread(front, pair, low):
    return jnp.where(low, front[:, 2 * pair : 2 * pair + 1], front[:, 2 * pair + 1 : 2 * pair + 2])


def head_sums(product, g):
    lane = lax.broadcasted_iota(jnp.int32, (WIDTH, LANES), 1)
    row = lax.broadcasted_iota(jnp.int32, (WIDTH, LANES), 0)
    pick = jnp.where(lane == row // HEADDIM, 1.0, 0.0).astype(bf16)
    high = product.astype(bf16)
    rest = (product - high.astype(f32)).astype(bf16)
    return pltpu.roll(MM(high, pick) + MM(rest, pick), GROUP * g, 1)


def taps(px_ref, tail, j, w_ref, b_ref, masks, ext):
    here = at(j, LANES)
    length = px_ref.shape[0]
    own = px_ref[:, here].astype(f32)
    ext[0:8, :] = tail
    ext[8 : 8 + length, :] = own
    inputs = [own] + [
        masks[k - 1] * ext[8 - k : 8 - k + length, :] for k in range(1, CONV)
    ]
    out = b_ref[0:1, here]
    for k in range(CONV):
        out = out + w_ref[k : k + 1, here] * inputs[k]
    return out, inputs


def tail_of(tail_ref, s, here):
    both = tail_ref[:, here].astype(f32)
    return jnp.where(s == 0, both[0:8], both[8:16])


def lane_masks(cols_ref, length):
    return [
        jnp.broadcast_to(cols_ref[0, :, k : k + 1], (length, LANES)) for k in range(CONV - 1)
    ]


NZ = 4


def place():
    seq, ctx = lax.axis_index("seq"), lax.axis_index("ctx")
    return seq // 2, lax.rem(seq, 2), ctx // 2, lax.rem(ctx, 2)


def device(z, y, x, c):
    return {"seq": z * 2 + y, "ctx": x * 2 + c}


def greet(z, y, x, c, more=0):
    barrier = pltpu.get_barrier_semaphore()
    others = [device(z, y, x, 1 - c), device(z, y, 1 - x, c), device(z, 1 - y, x, c)]
    others += [device(lax.rem(z + d, NZ), y, x, c) for d in range(1, NZ)]
    for other in others:
        pl.semaphore_signal(barrier, inc=1, device_id=other, device_id_type=pl.DeviceIdType.MESH)
    pl.semaphore_wait(barrier, len(others) + more)


def remote(src, dst, send, recv, target):
    return pltpu.make_async_remote_copy(
        src_ref=src, dst_ref=dst, send_sem=send, recv_sem=recv, device_id=target,
        device_id_type=pl.DeviceIdType.MESH,
    )


def gather_kernel(units, n, *refs):
    ins, outs, land, (tail_land, send, recv, local, store, tail_sem) = (
        refs[: n + 1], refs[n + 1 : 2 * n + 2], refs[2 * n + 2 : 3 * n + 2], refs[3 * n + 2 :]
    )
    x_first = [first for _array, _row, _rows, first in units]
    z, y, x, c = place()
    ctx = x * 2 + c
    after, before = lax.rem(ctx + 1, 4), lax.rem(ctx + 3, 4)
    barrier = pltpu.get_barrier_semaphore()
    for other in (after, before):
        pl.semaphore_signal(
            barrier, inc=1, device_id={"seq": z * 2 + y, "ctx": other},
            device_id_type=pl.DeviceIdType.MESH,
        )
    greet(z, y, x, c, 2)
    started, stored = [], []

    def shard(u):
        a, row, rows, _first = units[u]
        return ins[a].at[pl.ds(row, rows)]

    def slot_of(u, *at, into=None):
        a, row, rows, _first = units[u]
        return (land if into is None else into)[a].at[at + (pl.ds(row, rows),)]

    def number(u, kind, index):
        first = "x" if x_first[u] else "y"
        base = 0 if kind == "z" else 3 if kind == first else 15 if kind == "c" else 7
        return base + (index - 1 if kind == "z" else index)

    def push(u, zz, yy, xx, kind, index):
        slot = slot_of(u, zz, yy, xx, c)
        if kind == "z":
            target = device(lax.rem(z + index, NZ), y, x, c)
        else:
            flip = [1 - v if k == kind else v for k, v in (("y", y), ("x", x), ("c", c))]
            target = device(z, *flip)
        k = number(u, kind, index)
        copy = remote(slot, slot, send.at[u, k], recv.at[u, k], target)
        copy.start()
        started.append(copy)

    def came(u, zz, yy, xx, cc, kind, index):
        slot = slot_of(u, zz, yy, xx, cc)
        k = number(u, kind, index)
        remote(slot, slot, send.at[u, k], recv.at[u, k], device(z, y, x, 1 - c)).wait_recv()
        keep = pltpu.make_async_copy(slot, slot_of(u, zz, yy, xx, cc, into=outs), store.at[u, k])
        keep.start()
        stored.append(keep)

    back = [lax.rem(z + NZ - d, NZ) for d in range(NZ)]
    axes = [("x", "y") if first else ("y", "x") for first in x_first]
    every = range(len(units))
    ring = remote(
        ins[n], tail_land, tail_sem.at[0], tail_sem.at[1], {"seq": z * 2 + y, "ctx": after}
    )
    ring.start()
    for u in every:
        pltpu.make_async_copy(shard(u), slot_of(u, z, y, x, c), local.at[u]).start()

    def open_unit(u):
        a, b = axes[u]
        slot = slot_of(u, z, y, x, c)
        pltpu.make_async_copy(shard(u), slot, local.at[u]).wait()
        for d in (1, 3, 2):
            push(u, z, y, x, "z", d)
        for kind in (b, a, "c"):
            push(u, z, y, x, kind, 0)
        keep = pltpu.make_async_copy(slot, slot_of(u, z, y, x, c, into=outs), local.at[u])
        keep.start()
        stored.append(keep)

    def pass_on(u):
        a, b = axes[u]
        yy, xx = (y, 1 - x) if a == "x" else (1 - y, x)
        for d in range(1, NZ + 1):
            if d < NZ:
                came(u, back[d], y, x, c, "z", d)
                for kind in (b, a, "c"):
                    push(u, back[d], y, x, kind, d)
            came(u, back[d - 1], yy, xx, c, a, d - 1)
            push(u, back[d - 1], yy, xx, b, NZ + d - 1)
            push(u, back[d - 1], yy, xx, "c", NZ + d - 1)

    def cross(u):
        a, b = axes[u]
        for half in range(2):
            yy, xx = (1 - y, x) if b == "y" else (y, 1 - x)
            if half:
                yy, xx = 1 - y, 1 - x
            for d in range(NZ):
                came(u, back[d], yy, xx, c, b, NZ * half + d)
                push(u, back[d], yy, xx, "c", 2 * NZ + NZ * half + d)

    def finish(u):
        a, b = axes[u]
        for k in range(16):
            away = {a: (k // NZ) % 2, b: k // (2 * NZ)}
            came(u, back[k % NZ], 1 - y if away["y"] else y, 1 - x if away["x"] else x, 1 - c, "c", k)

    for t in range(-AHEAD, len(units) + 4):
        if 0 <= t + AHEAD < len(units):
            open_unit(t + AHEAD)
        if 0 <= t < len(units):
            pass_on(t)
        if 0 <= t - 2 < len(units):
            cross(t - 2)
        if 0 <= t - 4 < len(units):
            finish(t - 4)
    ring.wait_recv()
    keep = pltpu.make_async_copy(tail_land, outs[n], tail_sem.at[2])
    keep.start()
    keep.wait()
    ring.wait_send()
    for copy in started:
        copy.wait_send()
    for keep in stored:
        keep.wait()


def gather_all(shards, tail, units):
    n, m = len(shards), len(units)
    full = [(NZ, 2, 2, 2) + v.shape for v in shards]
    return pl.pallas_call(
        partial(gather_kernel, tuple(units), n),
        out_shape=[jax.ShapeDtypeStruct(f, v.dtype) for f, v in zip(full, shards)]
        + [jax.ShapeDtypeStruct(tail.shape, tail.dtype)],
        in_specs=[pl.BlockSpec(memory_space=pl.ANY)] * (n + 1),
        out_specs=[pl.BlockSpec(memory_space=pl.ANY)] * (n + 1),
        scratch_shapes=[pltpu.VMEM(f, v.dtype) for f, v in zip(full, shards)] + [
            pltpu.VMEM(tail.shape, tail.dtype),
            pltpu.SemaphoreType.DMA((m, 31)), pltpu.SemaphoreType.DMA((m, 31)),
            pltpu.SemaphoreType.DMA((m,)), pltpu.SemaphoreType.DMA((m, 31)),
            pltpu.SemaphoreType.DMA((3,)),
        ],
        compiler_params=pltpu.CompilerParams(
            collective_id=0, has_side_effects=True, vmem_limit_bytes=VMEM
        ),
    )(*shards, tail)


CUT_ROWS, CUT = 48, 512
SLOTS = 3
LEAD = (0, 5, 7, 9)
AHEAD = 4


def meet(place_of, ring):
    z, y, x, c = place_of
    if ring:
        barrier = pltpu.get_barrier_semaphore()
        for step in (1, 3):
            pl.semaphore_signal(
                barrier, inc=1, device_id={"seq": z * 2 + y, "ctx": lax.rem(x * 2 + c + step, 4)},
                device_id_type=pl.DeviceIdType.MESH,
            )
    greet(z, y, x, c, 2 if ring else 0)


class Reduction:
    def __init__(self, place_of, source, own, buffers, result, sem, semz):
        self.place, self.source, self.own, self.buffers = place_of, source, own, buffers
        self.result, self.sem, self.semz = result, sem, semz

    def copies(self, i, stage):
        z, y, x, c = self.place
        core, first, second, last = self.buffers(i)
        x_first = i % 2 == 0
        along_x, along_y = device(z, y, 1 - x, c), device(z, 1 - y, x, c)
        if stage == 0:
            moves = [(self.source(i, 1 - c), core, device(z, y, x, 1 - c))]
        elif stage == 1:
            src = core.at[:, :, 1 - x] if x_first else core.at[:, 1 - y]
            moves = [(src, first, along_x if x_first else along_y)]
        elif stage == 2:
            src = first.at[:, 1 - y] if x_first else first.at[:, 1 - x]
            moves = [(src, second, along_y if x_first else along_x)]
        else:
            moves = []
            for d in range(1, NZ):
                zz = lax.rem(z + d, NZ)
                moves.append((second.at[zz], last.at[z], device(zz, y, x, c)))
        made = []
        for d, (src, dst, to) in enumerate(moves):
            if stage < 3:
                sems = self.sem.at[2 * stage, i], self.sem.at[2 * stage + 1, i]
            else:
                sems = self.semz.at[0, d, i], self.semz.at[1, d, i]
            made.append(remote(src, dst, *sems, to))
        return made

    def send(self, i, stage):
        for copy in self.copies(i, stage):
            copy.start()

    def drain(self, i):
        for stage in range(4):
            for copy in self.copies(i, stage):
                copy.wait_send()

    def arrive(self, i, stage):
        z, y, x, c = self.place
        core, first, second, last = self.buffers(i)
        x_first = i % 2 == 0
        if stage < 3:
            landed = (core, first, second)[stage]
            remote(
                landed, landed, self.sem.at[2 * stage, i], self.sem.at[2 * stage + 1, i],
                device(z, y, x, 1 - c),
            ).wait_recv()
        if stage == 0:
            own = self.own(i)

            @pl.loop(0, NZ)
            def _(zz):
                for yy in range(2):
                    for xx in range(2):
                        core[zz, yy, xx] = core[zz, yy, xx] + own(zz, yy, xx)

        elif stage == 1:

            @pl.loop(0, NZ)
            def _(zz):
                for o in range(2):
                    first[zz, o] = first[zz, o] + (core[zz, o, x] if x_first else core[zz, y, o])

        elif stage == 2:

            @pl.loop(0, NZ)
            def _(zz):
                second[zz] = second[zz] + (first[zz, y] if x_first else first[zz, x])

            last[z] = second[z]
        else:
            for d in range(1, NZ):
                landed = last.at[lax.rem(z + NZ - d, NZ)]
                remote(
                    landed, landed, self.semz.at[0, d - 1, i], self.semz.at[1, d - 1, i],
                    device(z, y, x, 1 - c),
                ).wait_recv()
            value = last[0].astype(f32)
            for zz in range(1, NZ):
                value = value + last[zz].astype(f32)
            self.result(i, value)
        if stage < 3:
            self.send(i, stage + 1)


def reduction_buffers(count, shape, dtype):
    return [pltpu.VMEM((count,) + d + shape, dtype) for d in ((NZ, 2, 2), (NZ, 2), (NZ,), (NZ,))]


def reduction_semaphores(count):
    return [pltpu.SemaphoreType.DMA((6, count)), pltpu.SemaphoreType.DMA((2, NZ - 1, count))]


def cut_to(width, ref):
    if ref.shape[-1] == width:
        return ref
    return ref.at[(slice(None),) * (len(ref.shape) - 1) + (pl.ds(0, width),)]


def before_kernel(px_ref, tail_ref, w_ref, b_ref, cols_ref, heads_ref,
                  act_ref, tok_ref, cst_ref, fresh_ref, ext):
    s = pl.program_id(0)
    length = px_ref.shape[0]
    masks = lane_masks(cols_ref, length)

    @pl.loop(0, CHANNELS // LANES)
    def _(j):
        here = at(j, LANES)
        conv, _unused = taps(px_ref, tail_of(tail_ref, s, here), j, w_ref, b_ref, masks, ext)
        act_ref[0, :, here] = conv * sigmoid(conv)

    raw = px_ref[:, CHANNELS : CHANNELS + HEADS].astype(f32) + heads_ref[0:1, :HEADS]
    step = jnp.maximum(raw, 0.0) + jnp.log1p(jnp.exp(-jnp.abs(raw)))
    step = jnp.concatenate([step, jnp.zeros((length, LANES - HEADS), f32)], axis=1)
    rate = -step * jnp.exp(heads_ref[1:2, :])
    before = (
        lax.broadcasted_iota(jnp.int32, (length, length), 0)
        >= lax.broadcasted_iota(jnp.int32, (length, length), 1)
    ).astype(f32)
    decay = jnp.dot(before, rate, precision=lax.Precision.HIGHEST, preferred_element_type=f32)
    tok_ref[0, :, 0:LANES] = step
    tok_ref[0, :, LANES : 2 * LANES] = decay
    cst_ref[0] = decay.T[:HEADS]
    toward = jnp.exp(decay[length - 1 : length] - decay) * step * cols_ref[0, :, 4:5]
    keys = act_ref[0, :, INNER : INNER + STATE].astype(bf16)
    low = low_half(length)

    @pl.loop(0, GROUPS)
    def _(g):
        front = to_front(toward, g)
        scaled = []
        for pair in range(GROUP // 2):
            here = pl.ds(pl.multiple_of(g * WIDTH + pair * LANES, LANES), LANES)
            scaled.append((act_ref[0, :, here] * spread(front, pair, low)).astype(bf16))
        left = mm_tn(jnp.concatenate(scaled, axis=1), keys)
        fresh_ref[0, at(g, WIDTH), :] = left.astype(bf16)


def bias_of(ids_col, ids_row, transposed):
    shape = (ids_col.shape[0], ids_row.shape[1])
    down = lax.broadcasted_iota(jnp.int32, shape, 0)
    across = lax.broadcasted_iota(jnp.int32, shape, 1)
    order = (down <= across) if transposed else (down >= across)
    return jnp.where(order & (ids_col == ids_row), 0.0, FAR)


def within_kernel(act_ref, tok_ref, cst_ref, cols_ref, rows_ref, y_ref, cross, bias):
    length = act_ref.shape[1]
    half = length // 2
    cross[...] = mm_nt(
        act_ref[0, :, INNER + STATE :].astype(bf16),
        act_ref[0, :, INNER : INNER + STATE].astype(bf16),
    )
    bias[...] = bias_of(cols_ref[0, :, 5:6], rows_ref[0, 0:1, :], False)
    low = low_half(length)

    @pl.loop(0, GROUPS)
    def _(g):
        step = to_front(tok_ref[0, :, 0:LANES], g)
        decay = to_front(tok_ref[0, :, LANES : 2 * LANES], g)
        rows = cst_ref[0, at(g, GROUP), :]
        for pair in range(GROUP // 2):
            here = pl.ds(pl.multiple_of(g * WIDTH + pair * LANES, LANES), LANES)
            scaled = act_ref[0, :, here] * spread(step, pair, low)
            top, bottom = 0.0, 0.0
            for which in range(2):
                h = 2 * pair + which
                mine = jnp.where(low == (which == 0), scaled, 0.0).astype(bf16)
                col, row = decay[:, h : h + 1], rows[h : h + 1, :]
                w = jnp.exp(col[:half] - row[:, :half] + bias[:half, :half])
                top = top + MM((cross[:half, :half] * w).astype(bf16), mine[:half])
                w = jnp.exp(col[half:] - row + bias[half:, :])
                bottom = bottom + MM((cross[half:, :] * w).astype(bf16), mine)
            y_ref[0, :half, here] = top
            y_ref[0, half:, here] = bottom


def gate_kernel(z_ref, act_ref, tok_ref, cols_ref, y_ref, state_ref, dgn_ref, lanes_ref,
                gn_ref, dz_ref, dy_ref, dstate_ref, q_ref, dq_ref, sums_ref, total, queries_acc):
    length = act_ref.shape[1]
    low = low_half(length)
    enter = jnp.exp(tok_ref[0, :, LANES : 2 * LANES]) * cols_ref[0, :, 3:4]
    queries = act_ref[0, :, INNER + STATE :].astype(bf16)

    def first(g, carry):
        square, inner = carry
        front = to_front(enter, g)
        group_far = mm_nt(queries, state_ref[0, at(g, WIDTH), :])
        for pair in range(GROUP // 2):
            here = pl.ds(pl.multiple_of(g * WIDTH + pair * LANES, LANES), LANES)
            far = group_far[:, pair * LANES : (pair + 1) * LANES]
            y = y_ref[0, :, here] + spread(front, pair, low) * far
            total[:, here] = y
            y = y + lanes_ref[1:2, here] * act_ref[0, :, here]
            z = z_ref[:, here].astype(f32)
            gated = y * (z * sigmoid(z))
            square = square + gated * gated
            inner = inner + lanes_ref[0:1, here] * dgn_ref[:, here].astype(f32) * gated
        return square, inner

    zero = jnp.zeros((length, LANES), f32)
    square, inner = lax.fori_loop(0, GROUPS, first, (zero, zero))
    scale = lax.rsqrt(jnp.sum(square, axis=1, keepdims=True) * (1.0 / INNER) + EPSILON)
    back = scale * scale * scale * (jnp.sum(inner, axis=1, keepdims=True) * (1.0 / INNER))
    scale = jnp.broadcast_to(scale, (length, LANES))
    back = jnp.broadcast_to(back, (length, LANES))
    queries_acc[...] = jnp.zeros_like(queries_acc)
    dq_ref[0] = jnp.zeros_like(dq_ref[0])

    @pl.loop(0, GROUPS)
    def _(g):
        front = to_front(enter, g)
        products, entered = [], []
        for pair in range(GROUP // 2):
            here = pl.ds(pl.multiple_of(g * WIDTH + pair * LANES, LANES), LANES)
            xs = act_ref[0, :, here]
            inside = total[:, here]
            y = inside + lanes_ref[1:2, here] * xs
            z = z_ref[:, here].astype(f32)
            sg = sigmoid(z)
            gate = z * sg
            gated = y * gate
            gain = lanes_ref[0:1, here]
            dgn = dgn_ref[:, here].astype(f32)
            gn = gated * scale
            gn_ref[:, here] = (gn * gain).astype(bf16)
            dgated = scale * (gain * dgn) - gated * back
            dy = dgated * gate
            dz_ref[:, here] = (dgated * y * (sg * (1.0 + z * (1.0 - sg)))).astype(bf16)
            rounded = dy.astype(bf16)
            dy_ref[0, :, here] = rounded
            sums_ref[0, 0:1, here] = jnp.sum(dgn * gn, axis=0, keepdims=True)
            sums_ref[0, 1:2, here] = jnp.sum(dy * xs, axis=0, keepdims=True)
            rounded = rounded.astype(f32)
            entered.append((rounded * spread(front, pair, low)).astype(bf16))
            products.append(rounded * inside)
        entered = jnp.concatenate(entered, axis=1)
        dstate_ref[0, at(g, WIDTH), :] = mm_tn(entered, queries).astype(bf16)
        queries_acc[...] += MM(entered, state_ref[0, at(g, WIDTH), :])
        dq_ref[0] += head_sums(jnp.concatenate(products, axis=1), g)

    q_ref[0] = queries_acc[...]


def scan_back_kernel(act_ref, tok_ref, cst_ref, cols_ref, rows_ref, dy_ref,
                     dx_ref, dbc_ref, cross, bias, dcross):
    length = act_ref.shape[1]
    half = length // 2
    keys = act_ref[0, :, INNER : INNER + STATE].astype(bf16)
    queries = act_ref[0, :, INNER + STATE :].astype(bf16)
    cross[...] = mm_nt(keys, queries)
    bias[...] = bias_of(cols_ref[0, :, 5:6], rows_ref[0, 0:1, :], True)
    dcross[...] = jnp.zeros_like(dcross)
    low = low_half(length)

    @pl.loop(0, GROUPS)
    def _(g):
        step = to_front(tok_ref[0, :, 0:LANES], g)
        decay = to_front(tok_ref[0, :, LANES : 2 * LANES], g)
        rows = cst_ref[0, at(g, GROUP), :]
        for pair in range(GROUP // 2):
            here = pl.ds(pl.multiple_of(g * WIDTH + pair * LANES, LANES), LANES)
            scaled = (act_ref[0, :, here] * spread(step, pair, low)).astype(bf16)
            dy = dy_ref[0, :, here].astype(f32)
            top, bottom = 0.0, 0.0
            for which in range(2):
                h = 2 * pair + which
                mine = jnp.where(low == (which == 0), dy, 0.0).astype(bf16)
                col, row = decay[:, h : h + 1], rows[h : h + 1, :]
                w = jnp.exp(row - col[:half] + bias[:half, :])
                dcross[:half, :] += mm_nt(scaled[:half], mine) * w
                top = top + MM((cross[:half, :] * w).astype(bf16), mine)
                w = jnp.exp(row[:, half:] - col[half:] + bias[half:, half:])
                dcross[half:, half:] += mm_nt(scaled[half:], mine[half:]) * w
                bottom = bottom + MM((cross[half:, half:] * w).astype(bf16), mine[half:])
            dx_ref[0, :half, here] = top
            dx_ref[0, half:, here] = bottom

    d = dcross[...].astype(bf16)
    dbc_ref[0, :, :STATE] = MM(d, queries)
    dbc_ref[0, :, STATE:] = mm_tn(d, keys)


def after_kernel(px_ref, tail_ref, w_ref, b_ref, cols_ref, heads_ref, act_ref, tok_ref, lanes_ref,
                 dy_ref, dx_ref, dbc_ref, q_ref, dq_ref, later_ref, state_ref,
                 dpx_ref, dconv_ref, dheads_ref, ext, moved, grad, dstep_acc, dcol_acc, keys_acc, ends, sent, edges):
    s = pl.program_id(0)
    length = act_ref.shape[1]
    low = low_half(length)
    step = tok_ref[0, :, 0:LANES]
    decay = tok_ref[0, :, LANES : 2 * LANES]
    leave = jnp.exp(decay[length - 1 : length] - decay) * cols_ref[0, :, 4:5]
    keys = act_ref[0, :, INNER : INNER + STATE].astype(bf16)
    dstep_acc[...] = jnp.zeros_like(dstep_acc)
    dcol_acc[...] = jnp.zeros_like(dcol_acc)
    sent[...] = jnp.zeros_like(sent)
    keys_acc[...] = dbc_ref[0, :, :STATE]
    ends[...] = jnp.zeros_like(ends)

    @pl.loop(0, GROUPS)
    def _(g):
        step_front, leave_front = to_front(step, g), to_front(leave, g)
        products, columns, leaves = [], [], []
        group_through = mm_nt(keys, later_ref[0, at(g, WIDTH), :])
        for pair in range(GROUP // 2):
            here = pl.ds(pl.multiple_of(g * WIDTH + pair * LANES, LANES), LANES)
            later = later_ref[0, here, :]
            xs = act_ref[0, :, here]
            steps = spread(step_front, pair, low)
            leaving = spread(leave_front, pair, low)
            through = leaving * group_through[:, pair * LANES : (pair + 1) * LANES]
            dscaled = dx_ref[0, :, here] + through
            scaled = steps * xs
            rounded = scaled.astype(bf16).astype(f32)
            leaves.append((leaving * scaled).astype(bf16))
            products.append(xs * dscaled)
            columns.append(rounded * dscaled)
            sent[0:1, here] = jnp.sum(rounded * through, axis=0, keepdims=True)
            grad[:, here] = steps * dscaled + lanes_ref[1:2, here] * dy_ref[0, :, here].astype(f32)
            both = later.astype(f32) * state_ref[0, here, :].astype(f32)
            at_row = GROUP * g + 2 * pair
            ends[pl.ds(at_row, 1), :] = jnp.sum(both[:HEADDIM], axis=0, keepdims=True)
            ends[pl.ds(at_row + 1, 1), :] = jnp.sum(both[HEADDIM:], axis=0, keepdims=True)
        keys_acc[...] += MM(jnp.concatenate(leaves, axis=1), later_ref[0, at(g, WIDTH), :])
        dstep_acc[...] += head_sums(jnp.concatenate(products, axis=1), g)
        dcol_acc[...] += head_sums(jnp.concatenate(columns, axis=1), g)

    grad[:, INNER : INNER + STATE] = keys_acc[...]
    grad[:, INNER + STATE :] = dbc_ref[0, :, STATE:] + q_ref[0]
    dstep = dstep_acc[...]
    kept = jnp.exp(decay[length - 1 : length]) * cols_ref[0, length - 1 : length, 3:4]
    at_end = kept * jnp.sum(ends[...].T, axis=0, keepdims=True)
    for g in range(GROUPS):
        at_end = at_end + head_sums(sent[:, g * WIDTH : (g + 1) * WIDTH], g)[0:1]
    row = lax.broadcasted_iota(jnp.int32, (length, LANES), 0)
    ddecay = dq_ref[0] - dcol_acc[...] + jnp.where(row == length - 1, at_end, 0.0)
    onward = (
        lax.broadcasted_iota(jnp.int32, (length, length), 0)
        <= lax.broadcasted_iota(jnp.int32, (length, length), 1)
    ).astype(f32)
    drate = jnp.dot(onward, ddecay, precision=lax.Precision.HIGHEST, preferred_element_type=f32)
    speed = jnp.exp(heads_ref[1:2, :])
    raw = px_ref[:, CHANNELS : CHANNELS + HEADS].astype(f32) + heads_ref[0:1, :HEADS]
    draw = (dstep - drate * speed)[:, :HEADS] * sigmoid(raw)
    mine = pl.ds(pl.multiple_of(s * length, length), length)
    dpx_ref[mine, CHANNELS:] = jnp.concatenate(
        [draw, jnp.zeros((length, LANES - HEADS), f32)], axis=1
    ).astype(bf16)
    edges[s, :, CHANNELS:] = jnp.zeros((8, LANES), f32)
    dheads_ref[0] = jnp.zeros((8, LANES), f32)
    dheads_ref[0, 0:1, :HEADS] = jnp.sum(draw, axis=0, keepdims=True)
    dheads_ref[0, 1:2, :] = jnp.sum(drate * (-step * speed), axis=0, keepdims=True)

    masks = lane_masks(cols_ref, length)
    moved[...] = jnp.zeros_like(moved)
    dconv_ref[0] = jnp.zeros((8, CHANNELS), f32)

    @pl.loop(0, CHANNELS // LANES)
    def _(j):
        here = at(j, LANES)
        conv, inputs = taps(px_ref, tail_of(tail_ref, s, here), j, w_ref, b_ref, masks, ext)
        sg = sigmoid(conv)
        dconv = grad[:, here] * (sg * (1.0 + conv * (1.0 - sg)))
        for k in range(CONV):
            dconv_ref[0, k : k + 1, here] = jnp.sum(dconv * inputs[k], axis=0, keepdims=True)
        dconv_ref[0, CONV : CONV + 1, here] = jnp.sum(dconv, axis=0, keepdims=True)
        dx = w_ref[0:1, here] * dconv
        edge = jnp.zeros((8, LANES), f32)
        for k in range(1, CONV):
            moved[k - 1, 8 : 8 + length, :] = dconv * masks[k - 1]
            dx = dx + w_ref[k : k + 1, here] * moved[k - 1, 8 + k : 8 + k + length, :]
            edge = edge + w_ref[k : k + 1, here] * moved[k - 1, k : 8 + k, :]
        dpx_ref[mine, here] = dx.astype(bf16)
        edges[s, :, here] = edge

    @pl.when(s == pl.num_programs(0) - 1)
    def _():
        rows = edges.shape[0] * 8
        dpx_ref[dpx_ref.shape[0] - rows :, :] = edges[...].reshape(rows, edges.shape[2]).astype(bf16)


def whole(shape):
    return pl.BlockSpec(shape, lambda s: (0,) * len(shape))


def per_seq(*tail):
    return pl.BlockSpec((1,) + tail, lambda s: (s,) + (0,) * len(tail))


def per_rows(rows, width):
    return pl.BlockSpec((rows, width), lambda s: (s, 0))


def call(kernel, count, in_specs, outs, scratch, *args, mib):
    return pl.pallas_call(
        kernel,
        grid=(count,),
        in_specs=in_specs,
        out_specs=[spec for spec, _unused in outs],
        out_shape=[jax.ShapeDtypeStruct(*made) for _unused, made in outs],
        scratch_shapes=scratch,
        compiler_params=pltpu.CompilerParams(vmem_limit_bytes=mib * 1024 * 1024),
    )(*args)


def chain(own, factor, steps, beside):
    entered = jnp.zeros(own.shape, bf16)
    results = []
    for k, (source, target) in enumerate(steps):
        sent = own if k == 0 else (own.astype(f32) + factor * entered.astype(f32)).astype(bf16)
        came = lax.ppermute(sent, "ctx", [(source, target)])
        for work in beside[k :: len(steps)]:
            results.append(work())
            came, results[-1] = lax.optimization_barrier((came, results[-1]))
        entered = came if k == 0 else entered + came
    return entered, results


def pad_lanes(v):
    return jnp.pad(v, (0, LANES - v.shape[0]))


def finish_kernel(lead, small_ref, dwz_ref, dpx_ref, normed_ref, dz_ref, wx_ref, wz_ref, x_ref, tail_ref, gain_ref, g_ref,
                  gn_ref, wo_ref, oz_ref, ox_ref, os_ref, og_ref, grad_ref, out_ref, *scratch):
    own_z, own, buffers, own_s, buffers_s = scratch[0], scratch[1], scratch[2:6], scratch[6], scratch[7:11]
    own_g, buffers_g = scratch[11], scratch[12:16]
    rows, wbuf, total, back, sem, semz, zsem, wsem, rsem, tail_sem, own_sem = scratch[16:]
    place_of = place()
    z, y, x, c = place_of
    meet(place_of, True)
    count = g_ref.shape[0]
    nz = dwz_ref.shape[-1] // CUT
    widths = [CUT] * nz + [
        min(CUT, dpx_ref.shape[1] - k) for k in range(0, dpx_ref.shape[1], CUT)
    ]
    small, gain = len(widths), len(widths) + 1

    def whole_own(i):
        return {small: own_s, gain: own_g}[i] if i >= small else cut_to(widths[i], own.at[i - nz])

    def own_of(i):
        if i < nz:
            return lambda zz, yy, xx: own_z[i % SLOTS, zz, yy, xx]
        ref = whole_own(i)
        return lambda zz, yy, xx: ref[zz, yy, xx, c]

    def source(i, core):
        if i < nz:
            return dwz_ref.at[:, :, :, core, :, pl.ds(i * CUT, CUT)]
        return whole_own(i).at[:, :, :, core]

    def result(i, value):
        if i >= small:
            {small: os_ref, gain: og_ref}[i][...] = value
        elif i < nz:
            oz_ref[:, i * CUT : (i + 1) * CUT] = value
        else:
            k = (i - nz) * CUT
            ox_ref[:, k : k + widths[i]] = value

    def buffers_of(i):
        if i >= small:
            return [v.at[0] for v in (buffers_s if i == small else buffers_g)]
        return [cut_to(widths[i], v.at[i]) for v in buffers]

    red = Reduction(place_of, source, own_of, buffers_of, result, sem, semz)

    def fetch(i):
        return pltpu.make_async_copy(
            dwz_ref.at[:, :, :, c, :, pl.ds(i * CUT, CUT)], own_z.at[i % SLOTS], zsem.at[i % SLOTS]
        )

    def arrive(i, stage):
        if stage == 0 and i < nz:
            fetch(i).wait()
        red.arrive(i, stage)
        if stage == 0 and i + SLOTS < nz:
            fetch(i + SLOTS).start()

    def weight_and_send(j):
        k, w = j * CUT, widths[nz + j]
        own_j = whole_own(nz + j)
        depth = normed_ref.shape[1] // NZ

        @pl.loop(0, NZ)
        def _(zz):
            value = mm_tn(normed_ref[:, at(zz, depth)], dpx_ref[:, k : k + w])
            own_j[zz] = value.astype(bf16).reshape(2, 2, 2, CUT_ROWS, w)

        red.send(nz + j, 0)

    chunks = [(wz_ref, rows, k, CUT) for k in range(0, wz_ref.shape[1], CUT)]
    chunks += [(wx_ref, dpx_ref, k * CUT, w) for k, w in enumerate(widths[nz:])]

    def stream(q):
        w_ref, _left, k, w = chunks[q]
        return pltpu.make_async_copy(
            w_ref.at[:, pl.ds(k, w)], wbuf.at[q % 2, :, pl.ds(0, w)], wsem.at[q % 2]
        )

    depth_out = wo_ref.shape[0] // 2
    outs = wo_ref.shape[1] // CUT

    def stream_out(q, half):
        return pltpu.make_async_copy(
            wo_ref.at[pl.ds(half * depth_out, depth_out), pl.ds(q * CUT, CUT)], wbuf.at[half],
            wsem.at[half],
        )

    def load_rows(source_ref):
        return pltpu.make_async_copy(source_ref, rows, rsem.at[0])

    def input_chunk(q):
        _w, left, k, w = chunks[q]
        if q == 0:
            load_rows(dz_ref).wait()
            total[...] = jnp.zeros_like(total)
        stream(q).wait()
        total[: left.shape[0]] += mm_nt(left[:, k : k + w], wbuf[q % 2, :, :w])
        if q + 2 < len(chunks):
            stream(q + 2).start()
        if q == nz - 1:
            load_rows(gn_ref).start()

    def output_chunk(q):
        here = slice(q * CUT, (q + 1) * CUT)
        if q == 0:
            load_rows(gn_ref).wait()
            for half in range(2):
                stream_out(q, half).start()
        value = x_ref[:, here].astype(f32)
        for half in range(2):
            stream_out(q, half).wait()
            value = value + MM(rows[:, half * depth_out : (half + 1) * depth_out], wbuf[half])
            if q + 1 < outs:
                stream_out(q + 1, half).start()
        out_ref[:, here] = value.astype(bf16)

    def tail_copy():
        return remote(
            total.at[pl.ds(count, 16)], back, tail_sem.at[0], tail_sem.at[1],
            {"seq": z * 2 + y, "ctx": lax.rem(x * 2 + c + 3, 4)},
        )

    def scaled_rows(rows_ref, lo, hi):
        v = rows_ref[lo:hi].astype(f32)
        return v, lax.rsqrt(jnp.mean(v * v, axis=1, keepdims=True) + EPSILON)

    def norm_weights():
        tail_copy().start()
        sums = jnp.zeros((normed_ref.shape[1], LANES), f32)
        ones = jnp.ones((LANES, LANES), bf16)
        for lo in range(0, count + 16, LANES):
            size = min(LANES, count + 16 - lo)
            v, r = scaled_rows(x_ref, lo, lo + LANES) if lo < count else scaled_rows(tail_ref, 0, 16)
            product = v * r * total[lo : lo + size]
            high = product.astype(bf16)
            rest = (product - high.astype(f32)).astype(bf16)
            sums = sums + mm_tn(high, ones[:size]) + mm_tn(rest, ones[:size])
        own_g[...] = sums.astype(bf16).reshape(own_g.shape)
        red.send(gain, 0)

    def norm_rows():
        tail_copy().wait()
        seqs = tail_ref.shape[0] // 8
        length = count // seqs
        for s in range(seqs):
            total[(s + 1) * length - 8 : (s + 1) * length] += back[8 * s : 8 * s + 8]
        for lo in range(0, count, LANES):
            v, r = scaled_rows(x_ref, lo, lo + LANES)
            scaled = gain_ref[0:1] * total[lo : lo + LANES]
            mean = jnp.mean(v * scaled, axis=1, keepdims=True)
            value = g_ref[lo : lo + LANES].astype(f32) + r * (scaled - v * (r * r) * mean)
            grad_ref[lo : lo + LANES] = value.astype(bf16)

    for i in range(nz):
        red.send(i, 0)
    for i in range(SLOTS):
        fetch(i).start()
    small_copy = pltpu.make_async_copy(small_ref, own_s, own_sem.at[0])
    small_copy.start()
    load_rows(dz_ref).start()
    for q in range(2):
        stream(q).start()
    order = [*range(gain + 1)]
    work = [[partial(weight_and_send, j)] for j in range(small - nz)]
    step = -(-len(chunks) // 5)
    work += [
        [partial(input_chunk, q) for q in range(k, min(k + step, len(chunks)))]
        for k in range(0, len(chunks), step)
    ]
    work += [[norm_weights], [norm_rows]] + [[partial(output_chunk, q)] for q in range(outs)]
    work[1] = work[1] + [small_copy.wait, partial(red.send, small, 0)]
    for t in range(max(len(order) + lead[-1], len(work))):
        for job in work[t] if t < len(work) else []:
            job()
        for stage in reversed(range(4)):
            if 0 <= t - lead[stage] < len(order):
                arrive(order[t - lead[stage]], stage)
    for i in order:
        red.drain(i)


def finish(small, dw_z, dpx, normed, dz, w_x, w_z, x, tail, gain, g, gn, w_out, lead=LEAD):
    small = small.reshape((NZ, 2, 2, 2, -1, small.shape[-1]))
    dw_z = dw_z.reshape((NZ, 2, 2, 2, -1, dw_z.shape[-1]))
    nx = pl.cdiv(dpx.shape[1], CUT)
    p = nx + dw_z.shape[-1] // CUT
    ss = small.shape[-2:]
    far, near = pl.BlockSpec(memory_space=pl.ANY), pl.BlockSpec(memory_space=pltpu.VMEM)
    return pl.pallas_call(
        partial(finish_kernel, tuple(lead)),
        out_shape=[
            jax.ShapeDtypeStruct((CUT_ROWS, dw_z.shape[-1]), f32),
            jax.ShapeDtypeStruct((CUT_ROWS, dpx.shape[1]), f32),
            jax.ShapeDtypeStruct(ss, f32),
            jax.ShapeDtypeStruct((CUT_ROWS, LANES), f32),
            jax.ShapeDtypeStruct(g.shape, bf16),
            jax.ShapeDtypeStruct(g.shape, bf16),
        ],
        in_specs=[far, far, near, near, far, far, far, near, near, near, near, far, far],
        out_specs=[near] * 6,
        scratch_shapes=[
            pltpu.VMEM((SLOTS, NZ, 2, 2, CUT_ROWS, CUT), bf16),
            pltpu.VMEM((nx, NZ, 2, 2, 2, CUT_ROWS, CUT), bf16),
        ]
        + reduction_buffers(p, (CUT_ROWS, CUT), bf16)
        + [pltpu.VMEM(small.shape, f32)] + reduction_buffers(1, ss, f32)
        + [pltpu.VMEM((NZ, 2, 2, 2, CUT_ROWS, LANES), bf16)]
        + reduction_buffers(1, (CUT_ROWS, LANES), bf16)
        + [
            pltpu.VMEM(dz.shape, bf16), pltpu.VMEM((2, w_x.shape[0], CUT), bf16),
            pltpu.VMEM(normed.shape, f32), pltpu.VMEM(tail.shape, f32),
        ]
        + reduction_semaphores(p + 2)
        + [pltpu.SemaphoreType.DMA((SLOTS,)), pltpu.SemaphoreType.DMA((2,)),
           pltpu.SemaphoreType.DMA((1,)), pltpu.SemaphoreType.DMA((2,)), pltpu.SemaphoreType.DMA((1,))],
        compiler_params=pltpu.CompilerParams(
            collective_id=1, has_side_effects=True, vmem_limit_bytes=FINISH_VMEM
        ),
    )(small, dw_z, dpx, normed, dz, w_x, w_z, x, tail, gain, g, gn, w_out)


def local(tokens, norm_gain, input_weight, conv_w, conv_b, dt_bias, a_log, d_skip, gate_gain,
          output_weight, segments, cotangent):
    seqs, length, width = tokens.shape
    n_ctx = lax.axis_size("ctx")
    n_all = n_ctx * lax.axis_size("seq")
    count = seqs * length
    shares = [norm_gain.shape[0], gate_gain.shape[0], CONV * conv_b.shape[0], conv_b.shape[0]]
    cuts = [sum(shares[: i + 1]) for i in range(3)]
    packed = jnp.concatenate([norm_gain, gate_gain, conv_w.reshape(-1), conv_b])
    onward = [(i, i + 1) for i in range(n_ctx - 1)]
    tail = jnp.pad(tokens[:, length - (CONV - 1) :], ((0, 0), (8 - (CONV - 1), 0), (0, 0)))
    tail_ids = jnp.pad(
        segments[:, length - (CONV - 1) :].astype(bf16), ((0, 0), (0, width - (CONV - 1)))
    )
    tail = jnp.concatenate([tail_ids[:, None], tail[:, 1:]], axis=1).reshape(seqs * 8, width)
    torus = lax.axis_size("seq") == 2 * NZ and n_ctx == 4 and norm_gain.shape[0] == CUT_ROWS
    spare = ((0, 0), (0, LANES - HEADS))
    w_z, w_x = input_weight[:, :INNER], jnp.pad(input_weight[:, INNER:], spare)
    if torus:
        size = packed.shape[0]
        small = jnp.pad(packed, (0, 16 * LANES - size)).reshape(16, LANES)
        w_out = lax.all_gather(output_weight, BOTH, axis=0, tiled=True)
        w_z = lax.all_gather(w_z, BOTH, axis=0, tiled=True)
        w_x, packed, tail = gather_all(
            [w_x, small], tail,
            [(1, 0, 16, True)]
            + [(0, 16 * k, 16, k % 2 == 0) for k in range(3)]
,
        )
        w_x, w_z, w_out = (w.reshape(-1, w.shape[-1]) for w in (w_x, w_z, w_out))
        packed = packed.reshape(n_all, -1)[:, :size]
    else:
        packed = lax.all_gather(packed, BOTH, axis=0)
        tail = lax.ppermute(tail, "ctx", onward)
        w_in, w_out = (
            lax.all_gather(w, BOTH, axis=0, tiled=True) for w in (input_weight, output_weight)
        )
        w_z, w_x = w_in[:, :INNER], jnp.pad(w_in[:, INNER:], spare)
    norm_full, gate_full, conv_w_full, conv_b_full = jnp.split(packed.astype(f32), cuts, axis=1)
    norm_full = norm_full.reshape(1, -1)
    gate_full = gate_full.reshape(1, -1)
    conv_b_full = conv_b_full.reshape(1, -1)
    conv_w_full = conv_w_full.reshape(n_all, CONV, -1).transpose(1, 0, 2).reshape(CONV, -1)

    tail = tail.reshape(seqs, 8, width)
    tail_ids = jnp.where(
        lax.axis_index("ctx") == 0, -1, tail[:, 0, : CONV - 1].astype(jnp.int32)
    )
    tail = jnp.pad(tail[:, 8 - (CONV - 1) :], ((0, 0), (8 - (CONV - 1), 0), (0, 0)))
    tail = jnp.where(lax.axis_index("ctx") == 0, 0, tail)
    tail = tail.reshape(seqs * 8, width)
    x_all = jnp.concatenate([tokens.reshape(count, width), tail])
    x_all = x_all.astype(f32)
    r_all = lax.rsqrt(jnp.mean(x_all * x_all, axis=-1, keepdims=True) + EPSILON)
    normed = (x_all * r_all * norm_full).astype(bf16)

    ids_ext = jnp.concatenate([tail_ids, segments], axis=1)
    flags = [
        segments == ids_ext[:, CONV - 1 - k : CONV - 1 - k + length] for k in range(1, CONV)
    ] + [segments == ids_ext[:, CONV - 2 : CONV - 1], segments == segments[:, -1:]]
    cols = jnp.stack([f.astype(f32) for f in flags] + [segments.astype(f32)], axis=-1)
    cols = jnp.pad(cols, ((0, 0), (0, 0), (0, LANES - cols.shape[-1])))
    rows = jnp.pad(segments.astype(f32)[:, None], ((0, 0), (0, 7), (0, 0)))
    heads = jnp.pad(jnp.stack([pad_lanes(dt_bias), pad_lanes(a_log)]), ((0, 6), (0, 0)))
    lanes = jnp.concatenate([gate_full, jnp.repeat(d_skip, HEADDIM)[None]])
    lanes = jnp.pad(lanes, ((0, 6), (0, 0)))
    conv_w8 = jnp.pad(conv_w_full, ((0, 8 - CONV), (0, 0)))
    conv_b8 = jnp.pad(conv_b_full, ((0, 7), (0, 0)))

    px = MM(normed, w_x).astype(bf16)
    px_width, used = CHANNELS + LANES, CHANNELS + HEADS
    tail_spec = pl.BlockSpec((16, px_width), lambda s: (count // 16, 0))
    act, tok, cst, fresh = call(
        before_kernel, seqs,
        [per_rows(length, px_width), tail_spec, whole((8, CHANNELS)), whole((8, CHANNELS)),
         per_seq(length, LANES), whole((8, LANES))],
        [(per_seq(length, CHANNELS), ((seqs, length, CHANNELS), f32)),
         (per_seq(length, 2 * LANES), ((seqs, length, 2 * LANES), f32)),
         (per_seq(HEADS, length), ((seqs, HEADS, length), f32)),
         (per_seq(INNER, STATE), ((seqs, INNER, STATE), bf16))],
        [pltpu.VMEM((length + 8, LANES), f32)],
        px, px, conv_w8, conv_b8, cols, heads, mib=24,
    )
    carried = cols[:, length - 1, 3]
    kept = jnp.exp(cst[:, :, length - 1]) * carried[:, None]
    kept = jnp.repeat(kept, HEADDIM, axis=1)[..., None]
    g2 = cotangent.reshape(count, width)

    def gate_gradient():
        dims = (((1,), (1,)), ((), ()))
        return lax.dot_general(g2, w_out, dims, preferred_element_type=f32).astype(bf16)

    def within():
        [y] = call(
            within_kernel, seqs,
            [per_seq(length, CHANNELS), per_seq(length, 2 * LANES), per_seq(HEADS, length),
             per_seq(length, LANES), per_seq(8, length)],
            [(per_seq(length, INNER), ((seqs, length, INNER), f32))],
            [pltpu.VMEM((length, length), f32), pltpu.VMEM((length, length), f32)],
            act, tok, cst, cols, rows, mib=24,
        )
        return y

    def gates():
        return MM(normed[:count], w_z).astype(bf16)

    entering, (dgn, y, pz) = chain(fresh, kept, onward, (gate_gradient, within, gates))
    gn, dz, dy, dstate, dqueries, ddecay, sums = call(
        gate_kernel, seqs,
        [per_rows(length, INNER), per_seq(length, CHANNELS), per_seq(length, 2 * LANES),
         per_seq(length, LANES), per_seq(length, INNER), per_seq(INNER, STATE),
         per_rows(length, INNER), whole((8, INNER))],
        [(per_rows(length, INNER), ((count, INNER), bf16)),
         (per_rows(length, INNER), ((count, INNER), bf16)),
         (per_seq(length, INNER), ((seqs, length, INNER), bf16)),
         (per_seq(INNER, STATE), ((seqs, INNER, STATE), bf16)),
         (per_seq(length, STATE), ((seqs, length, STATE), f32)),
         (per_seq(length, LANES), ((seqs, length, LANES), f32)),
         (per_seq(8, INNER), ((seqs, 8, INNER), f32))],
        [pltpu.VMEM((length, INNER), f32), pltpu.VMEM((length, STATE), f32)],
        pz, act, tok, cols, y, entering, dgn, lanes, mib=44,
    )
    tn = (((0,), (0,)), ((), ()))

    def output_weights():
        return lax.dot_general(gn, g2, tn, preferred_element_type=f32).astype(bf16)

    def scan_back():
        return call(
            scan_back_kernel, seqs,
            [per_seq(length, CHANNELS), per_seq(length, 2 * LANES), per_seq(HEADS, length),
             per_seq(length, LANES), per_seq(8, length), per_seq(length, INNER)],
            [(per_seq(length, INNER), ((seqs, length, INNER), f32)),
             (per_seq(length, 2 * STATE), ((seqs, length, 2 * STATE), f32))],
            [pltpu.VMEM((length, length), f32)] * 3,
            act, tok, cst, cols, rows, dy, mib=28,
        )

    def gate_weights():
        return lax.dot_general(normed[:count], dz, tn, preferred_element_type=f32).astype(bf16)

    later, (dw_out, (dx, dbc), dw_z) = chain(
        dstate, kept, [(b, a) for a, b in reversed(onward)], (output_weights, scan_back, gate_weights)
    )
    dpx, dconv, dheads = call(
        after_kernel, seqs,
        [per_rows(length, px_width), tail_spec, whole((8, CHANNELS)), whole((8, CHANNELS)),
         per_seq(length, LANES), whole((8, LANES)), per_seq(length, CHANNELS),
         per_seq(length, 2 * LANES), whole((8, INNER)), per_seq(length, INNER),
         per_seq(length, INNER), per_seq(length, 2 * STATE), per_seq(length, STATE),
         per_seq(length, LANES), per_seq(INNER, STATE), per_seq(INNER, STATE)],
        [(whole((count + seqs * 8, px_width)), ((count + seqs * 8, px_width), bf16)),
         (per_seq(8, CHANNELS), ((seqs, 8, CHANNELS), f32)),
         (per_seq(8, LANES), ((seqs, 8, LANES), f32))],
        [pltpu.VMEM((length + 8, LANES), f32), pltpu.VMEM((CONV - 1, length + 16, LANES), f32),
         pltpu.VMEM((length, CHANNELS), f32), pltpu.VMEM((length, LANES), f32),
         pltpu.VMEM((length, LANES), f32), pltpu.VMEM((length, STATE), f32), pltpu.VMEM((LANES, LANES), f32),
         pltpu.VMEM((8, INNER), f32), pltpu.VMEM((seqs, 8, px_width), f32)],
        px, px, conv_w8, conv_b8, cols, heads, act, tok, lanes, dy, dx, dbc, dqueries, ddecay,
        later, entering, mib=48,
    )
    sums = jnp.sum(sums, axis=0)
    dconv = jnp.sum(dconv, axis=0)
    dheads = jnp.sum(dheads, axis=0)
    d_skip_sum = jnp.sum(sums[1].reshape(HEADS, HEADDIM), axis=1)
    split = [sums[0].reshape(n_all, -1),
             dconv[:CONV].reshape(CONV, n_all, -1).transpose(1, 0, 2).reshape(n_all, -1),
             dconv[CONV].reshape(n_all, -1)]
    shared = jnp.concatenate([dheads[0, :HEADS], dheads[1, :HEADS], d_skip_sum])
    split = jnp.concatenate(split, axis=1)
    share = split.shape[1]
    if torus:
        fill = 8 * LANES - share - shared.shape[0]
        split = [split, jnp.broadcast_to(shared, (n_all,) + shared.shape), jnp.zeros((n_all, fill), f32)]
        dw_z, dw_x, mine, d_norm, input_grad, output = finish(
            jnp.concatenate(split, axis=1).reshape(n_all, 8, LANES), dw_z, dpx, normed, dz,
            w_x, w_z, tokens.reshape(count, width), tail, jnp.pad(norm_full, ((0, 7), (0, 0))), g2,
            gn, w_out,
        )
        d_norm = d_norm[:, 0]
        dw_out = lax.psum_scatter(dw_out, BOTH, scatter_dimension=0, tiled=True).astype(f32)
        dw_in = jnp.concatenate([dw_z, dw_x[:, :used]], axis=1)
        mine = mine.reshape(-1)
        mine, shared = mine[:share], mine[share : share + shared.shape[0]]
    else:
        nt = (((1,), (1,)), ((), ()))
        dnormed_x = lax.dot_general(dpx, w_x, nt, preferred_element_type=f32)
        dnormed = dnormed_x[:count] + lax.dot_general(dz, w_z, nt, preferred_element_type=f32)
        back = dnormed_x[count:].reshape(seqs, 8, width)[:, 8 - (CONV - 1) :].astype(bf16)
        back = lax.ppermute(back, "ctx", [(b, a) for a, b in onward])
        dw_x = lax.dot_general(normed, dpx, tn, preferred_element_type=f32).astype(bf16)
        x, r = x_all[:count], r_all[:count]
        d_gain = jnp.sum(x * r * dnormed, axis=0) + jnp.sum(
            x_all[count:] * r_all[count:] * dnormed_x[count:], axis=0
        )
        back, d_gain, dw_x = lax.optimization_barrier((back, d_gain, dw_x))
        back = jnp.pad(back.astype(f32), ((0, 0), (length - (CONV - 1), 0), (0, 0)))
        scaled = norm_full * (dnormed + back.reshape(count, width))
        dx_in = r * (scaled - x * (r * r) * jnp.mean(x * scaled, axis=-1, keepdims=True))
        input_grad = (g2.astype(f32) + dx_in).astype(bf16)
        output = (x_all[:count] + MM(gn, w_out)).astype(bf16)
        dw_in = jnp.concatenate([dw_z, dw_x[:, :used]], axis=1)
        dw_out, dw_in = (
            lax.psum_scatter(v.astype(f32), BOTH, scatter_dimension=0, tiled=True)
            for v in (dw_out, dw_in)
        )
        every = lax.psum(jnp.concatenate([split.reshape(-1), shared, d_gain]), BOTH)
        me = lax.axis_index("seq") * n_ctx + lax.axis_index("ctx")
        d_norm = lax.dynamic_slice(every[-width:], (me * shares[0],), (shares[0],))
        mine = lax.dynamic_slice(every, (me * share,), (share,))
        shared = every[n_all * share : n_all * share + shared.shape[0]]
    d_gate, d_conv_w, d_conv_b = jnp.split(mine, [v - cuts[0] for v in cuts[1:]])
    d_bias, d_alog, d_skips = jnp.split(shared, 3)
    return (
        output.reshape(tokens.shape), input_grad.reshape(tokens.shape), d_norm, dw_in,
        d_conv_w.reshape(CONV, -1), d_conv_b, d_bias, d_alog, d_skips, d_gate, dw_out,
    )


def solution(mesh):
    split = P(BOTH)
    rows = P(BOTH, None)
    seq = P("seq", "ctx", None)
    in_specs = (seq, split, rows, P(None, BOTH), split, P(), P(), P(), split, rows,
                P("seq", "ctx"), seq)
    out_specs = (seq, seq, split, rows, P(None, BOTH), split, P(), P(), P(), split, rows)
    return jax.shard_map(local, mesh=mesh, in_specs=in_specs, out_specs=out_specs, check_vma=False)
```
